32 devices in a mesh: dp: 2 (over core), ctx: 16 (over z, y, x).
Axes of the slice: x: 2, y: 2, z: 4, core: 2. Of those that a mesh axis runs over, the one named last changes fastest.
Arguments:
- latent_in: bfloat16 [4096, 1024], P(('dp', 'ctx')), may hold values from -6 to 6
- gain_attn: float32 [1024], replicated, may hold values from 0.4 to 1.6
- w_query: bfloat16 [1024, 1024], replicated, may hold values from -0.1875 to 0.1875
- w_key: bfloat16 [1024, 1024], replicated, may hold values from -0.1875 to 0.1875
- w_value: bfloat16 [1024, 1024], replicated, may hold values from -0.1875 to 0.1875
- w_out: bfloat16 [1024, 1024], replicated, may hold values from -0.75 to 0.75
- gain_ffn: float32 [1024], replicated, may hold values from 0.4 to 1.6
- w_gate: bfloat16 [1024, 2816], replicated, may hold values from -0.1875 to 0.1875
- w_up: bfloat16 [1024, 2816], replicated, may hold values from -0.1875 to 0.1875
- w_down: bfloat16 [2816, 1024], replicated, may hold values from -0.109375 to 0.109375
- cotangent: bfloat16 [4096, 1024], P(('dp', 'ctx')), may hold values from -6 to 6
- seq_lengths: int32 [2, 4], P('dp'), may hold values from 1 to 1024, as said below
- span_order: int32 [2, 16], P('dp'), may hold values from 0 to 15, as said below
Outputs:
- latents: bfloat16 [4096, 1024], P(('dp', 'ctx'))
- latent_grad: bfloat16 [4096, 1024], P(('dp', 'ctx'))
- gain_attn_grad: float32 [1024], P(('dp', 'ctx'))
- query_grad: float32 [1024, 1024], P(('dp', 'ctx'))
- key_grad: float32 [1024, 1024], P(('dp', 'ctx'))
- value_grad: float32 [1024, 1024], P(('dp', 'ctx'))
- out_grad: float32 [1024, 1024], P(('dp', 'ctx'))
- gain_ffn_grad: float32 [1024], P(('dp', 'ctx'))
- gate_grad: float32 [1024, 2816], P(('dp', 'ctx'))
- up_grad: float32 [1024, 2816], P(('dp', 'ctx'))
- down_grad: float32 [2816, 1024], P(('dp', 'ctx'))
The draws below stay inside these ranges and needn't reach their ends.
Inputs may be any that keep to these rules, and one draw needn't show every extreme that they name: `seq_lengths`: in each row the 4 lengths sum to at most 2048; exactly one of them is 1024; positions at or after the sum are padding. `span_order`: each row is a permutation of the 16 blocks of 128 positions of a group.
All inputs are finite; a program needn't handle non-finite values.
Results may differ from the reference program's by a relative error of at most 0.023.
Values may be sent and summed in bfloat16 or wider, within the bound.
No kernel may reach another device: no remote copies, remote signals or barrier semaphores. Data moves between devices by JAX's collectives and lax.ppermute only.
A program may use at most 256 MiB of HBM per device.

```python
import jax
import jax.numpy as jnp
from jax import lax

D = 1024
FF = 2816
HEADS = 16
HEAD_DIM = 64
TOK_DEV = 128
NSEQ = 4
GROUP_TOK = 2048
TOKENS = 4096
N_DP = 2
N_CTX = 16


def group_lengths(key):
    sub_keys = jax.random.split(key, 4)
    longest = GROUP_TOK // 2
    padding = jax.random.randint(sub_keys[0], (), 1, TOK_DEV + 1)
    remain = GROUP_TOK - longest - padding
    first_len = jax.random.randint(sub_keys[1], (), remain // 6, remain // 2)
    second_len = jax.random.randint(sub_keys[2], (), remain // 6, (remain - first_len) * 2 // 3)
    third_len = remain - first_len - second_len
    others = jnp.stack([first_len, second_len, third_len]).astype(jnp.int32)
    long_slot = jax.random.randint(sub_keys[3], (), 0, NSEQ)
    places = jnp.arange(NSEQ, dtype=jnp.int32)
    picked = jnp.clip(places - (places > long_slot).astype(jnp.int32), 0, NSEQ - 2)
    return jnp.where(places == long_slot, longest, others[picked]).astype(jnp.int32)


def all_lengths(key):
    return jax.vmap(group_lengths)(jax.random.split(key, N_DP))


def place_spans(key, lengths):
    key_perm, key_targets = jax.random.split(key)
    span_of = jax.random.permutation(key_perm, N_CTX).astype(jnp.int32)
    longest = GROUP_TOK // 2
    seq_ends = jnp.cumsum(lengths).astype(jnp.int32)
    start = jnp.sum(jnp.where(lengths == longest, seq_ends - lengths, 0)).astype(jnp.int32)
    first_span = start // TOK_DEV + 1
    last_span = (start + longest) // TOK_DEV - 1
    targets = jnp.stack([first_span, (first_span + last_span) // 2, last_span]).astype(jnp.int32)
    targets = targets[jax.random.permutation(key_targets, 3)]
    places = jnp.arange(N_CTX, dtype=jnp.int32)
    devices = [0, N_CTX // 2, N_CTX - 1]
    for number in range(3):
        device = devices[number]
        target = targets[number]
        where_now = jnp.sum(jnp.where(span_of == target, places, 0))
        held = span_of[device]
        span_of = span_of.at[where_now].set(held).at[device].set(target)
    return span_of


def draw_seq_lengths(key, part):
    shared = all_lengths(key)
    return shared


def draw_span_order(key, part):
    shared = all_lengths(key)
    key = jax.random.fold_in(key, 2)
    return jax.vmap(place_spans)(jax.random.split(key, N_DP), shared).astype(jnp.int32)


def shard_levels(rng, shape, cuts, least, largest):
    def one(axis_at, parts):
        heights = jax.random.uniform(jax.random.fold_in(jax.random.fold_in(rng, 6), axis_at), (parts,), jnp.float32, least / len(cuts), largest / len(cuts))
        return jnp.repeat(jnp.exp(heights), shape[axis_at] // parts).reshape((-1,) + (1,) * (len(shape) - axis_at - 1))

    gain = one(*cuts[0])
    for cut in cuts[1:]:
        gain = gain * one(*cut)
    return gain


def normal_values(rng, dims, deviation, reach, shards=(), kind=jnp.bfloat16):
    drawn = deviation * jax.random.normal(rng, dims, jnp.float32)
    if shards:
        drawn = drawn * shard_levels(rng, dims, shards, -0.22, 0.18)
    return jnp.clip(drawn, -reach, reach).astype(kind)


def setup_inputs(seed: int = 0) -> dict:
    seeds = jax.random.split(jax.random.key(seed), 14)
    return {
        "latent_in": normal_values(seeds[0], (TOKENS, D), 1.0, 6.0, ((0, 32),)),
        "gain_attn": jnp.clip(1.0 + 0.12 * jax.random.normal(seeds[1], (D,), jnp.float32), 0.4, 1.6),
        "w_query": normal_values(seeds[2], (D, D), D ** -0.5, 0.1875),
        "w_key": normal_values(seeds[3], (D, D), D ** -0.5, 0.1875),
        "w_value": normal_values(seeds[4], (D, D), D ** -0.5, 0.1875),
        "w_out": normal_values(seeds[5], (D, D), (D // 16) ** -0.5, 0.75),
        "gain_ffn": jnp.clip(1.0 + 0.12 * jax.random.normal(seeds[6], (D,), jnp.float32), 0.4, 1.6),
        "w_gate": normal_values(seeds[7], (D, FF), D ** -0.5, 0.1875),
        "w_up": normal_values(seeds[8], (D, FF), D ** -0.5, 0.1875),
        "w_down": normal_values(seeds[9], (FF, D), FF ** -0.5, 0.109375),
        "cotangent": normal_values(seeds[10], (TOKENS, D), 1.0, 6.0, ((0, 32),)),
        "seq_lengths": draw_seq_lengths(jax.random.fold_in(seeds[13], 71), 0),
        "span_order": draw_span_order(jax.random.fold_in(seeds[13], 71), 0),
    }


EPS = 1e-06
NEG_FILL = -1e+30

@jax.custom_vjp
def low(v):
    return lax.optimization_barrier(v.astype(jnp.bfloat16)).astype(jnp.float32)

@jax.custom_vjp
def low_back(v):
    return v

def low_keep(v):
    return (low(v), None)

def low_pass(kept, grad):
    return (grad,)

def back_keep(v):
    return (v, None)

def back_low(kept, grad):
    return (low(grad),)
low.defvjp(low_keep, low_pass)
low_back.defvjp(back_keep, back_low)

def matmul_hi(left, right):
    return jnp.dot(left, right, precision=lax.Precision.HIGHEST, preferred_element_type=jnp.float32)

def rms_scale(values_in, gain_vec):
    return values_in * lax.rsqrt(lax.optimization_barrier(jnp.mean(values_in * values_in, axis=-1, keepdims=True)) + EPS) * gain_vec

def layout(lengths, span_of):
    row_ids = jnp.arange(GROUP_TOK, dtype=jnp.int32)
    position = (span_of[row_ids // TOK_DEV] * TOK_DEV + row_ids % TOK_DEV).astype(jnp.int32)
    seq_ends = jnp.cumsum(lengths).astype(jnp.int32)
    seq_id = lax.optimization_barrier(jnp.sum((position[:, None] >= seq_ends[None, :]).astype(jnp.int32), axis=1)).astype(jnp.int32)
    return (position, seq_id)

def attend_group(pieces):
    query_g, key_g, value_g, lengths, span_of = pieces
    position, seq_id = layout(lengths, span_of)
    rows_blk = 2 * TOK_DEV
    count_blk = GROUP_TOK // rows_blk
    score_scale = HEAD_DIM ** (-0.5)

    def one_block(block_in):
        query_b, query_pos, query_seq = block_in
        scores = jnp.einsum('qhd,khd->hqk', query_b, key_g, precision=lax.Precision.HIGHEST) * score_scale
        scores = low_back(scores)
        key_mask = (query_seq[:, None] == seq_id[None, :]) & (position[None, :] <= query_pos[:, None])
        scores = jnp.where(key_mask[None], scores, NEG_FILL)
        row_top = lax.optimization_barrier(jnp.max(scores, axis=-1, keepdims=True))
        weight = jnp.where(key_mask[None], jnp.exp(scores - row_top), 0.0)
        prob = low(weight / lax.optimization_barrier(jnp.sum(weight, axis=-1, keepdims=True)))
        return jnp.einsum('hqk,khd->qhd', prob, value_g, precision=lax.Precision.HIGHEST)
    blocks = (query_g.reshape(count_blk, rows_blk, HEADS, HEAD_DIM), position.reshape(count_blk, rows_blk), seq_id.reshape(count_blk, rows_blk))
    return lax.map(jax.checkpoint(one_block), blocks).reshape(GROUP_TOK, HEADS, HEAD_DIM)

def reference(latent_in, gain_attn, w_query, w_key, w_value, w_out, gain_ffn, w_gate, w_up, w_down, cotangent, seq_lengths, span_order):
    inputs = (latent_in.astype(jnp.float32), gain_attn.astype(jnp.float32), w_query.astype(jnp.float32), w_key.astype(jnp.float32), w_value.astype(jnp.float32), w_out.astype(jnp.float32), gain_ffn.astype(jnp.float32), w_gate.astype(jnp.float32), w_up.astype(jnp.float32), w_down.astype(jnp.float32))

    def forward(latent_f, gain_one, wq_f, wk_f, wv_f, wo_f, gain_two, wg_f, wu_f, wd_f):
        normed = low(rms_scale(latent_f, gain_one))
        query_p = low(low_back(matmul_hi(normed, wq_f)))
        key_p = low(low_back(matmul_hi(normed, wk_f)))
        value_p = low(low_back(matmul_hi(normed, wv_f)))
        shaped = (N_DP, GROUP_TOK, HEADS, HEAD_DIM)
        attn = lax.map(attend_group, (query_p.reshape(shaped), key_p.reshape(shaped), value_p.reshape(shaped), seq_lengths, span_order))
        attn_low = low(low_back(attn.reshape(TOKENS, D)))
        resid = latent_f + low_back(matmul_hi(attn_low, wo_f))
        normed_two = low(rms_scale(resid, gain_two))
        gate_pre = low_back(matmul_hi(normed_two, wg_f))
        up_pre = low_back(matmul_hi(normed_two, wu_f))
        hidden = low(jax.nn.silu(gate_pre) * up_pre)
        return resid + low_back(matmul_hi(hidden, wd_f))
    result, pullback = jax.vjp(forward, *inputs)
    grads = pullback(cotangent.astype(jnp.float32))
    return (result.astype(jnp.bfloat16), grads[0].astype(jnp.bfloat16), grads[1], grads[2], grads[3], grads[4], grads[5], grads[6], grads[7], grads[8], grads[9])
```

```python
import functools

import jax
import jax.numpy as jnp
from jax import lax
from jax.experimental import pallas as pl
from jax.experimental.pallas import tpu as pltpu
from jax.sharding import PartitionSpec as P

HEADS = 16
HEAD_DIM = 64
EPS = 1e-06
NEG_FILL = -1e30
LOG2E = 1.4426950408889634
SCALE = HEAD_DIM**-0.5

BF16 = jnp.bfloat16
F32 = jnp.float32


def dot(a, b, dims):
    return lax.dot_general(a, b, (dims, ((), ())), preferred_element_type=F32)


def query_starts(ends_ref, pos):
    start = jnp.zeros_like(pos)
    for n in range(ends_ref.shape[0]):
        start = jnp.where(pos >= ends_ref[n], ends_ref[n], start)
    return start


def block_mask(ends_ref, i, j, blk):
    pos = lax.broadcasted_iota(jnp.int32, (1, blk), 1) + i * blk
    start = query_starts(ends_ref, pos) - j * blk
    key = lax.broadcasted_iota(jnp.int32, (blk, blk), 0)
    return (key <= pos - j * blk) & (key >= start)


def attn_fwd_kernel(rep, slot_ref, low_ref, ends_ref, part_ref, qkv_ref, out_ref, full_ref, top_ref, inv_ref, key_ref):
    slots, _, rows = qkv_ref.shape
    blk = 2 * rows
    count = slots // 2
    hd = HEAD_DIM

    def flip(s, c):
        key_ref[s] = qkv_ref[s, hd : 2 * hd, :].T
        return c

    lax.fori_loop(0, slots, flip, 0)
    if rep > 1:
        out_ref[...] = jnp.zeros_like(out_ref)
        full_ref[...] = jnp.zeros_like(full_ref)

    def query_block(i, c):
        s0, s1 = slot_ref[2 * i], slot_ref[2 * i + 1]
        q = jnp.concatenate([qkv_ref[s0, :hd, :], qkv_ref[s1, :hd, :]], axis=1)

        def key_block(j, state):
            top, mass, acc = state
            k0, k1 = slot_ref[2 * j], slot_ref[2 * j + 1]
            k = jnp.concatenate([key_ref[k0], key_ref[k1]], axis=0)
            v = jnp.concatenate([qkv_ref[k0, 2 * hd :, :], qkv_ref[k1, 2 * hd :, :]], axis=1)
            s = dot(k, q, ((1,), (0,))) * (SCALE * LOG2E)
            s = jnp.where(block_mask(ends_ref, i, j, blk), s, NEG_FILL)
            new_top = jnp.maximum(top, jnp.max(s, axis=0, keepdims=True))
            shrink = jnp.exp2(top - new_top)
            w = jnp.exp2(s - new_top)
            mass = mass * shrink + jnp.sum(w, axis=0, keepdims=True)
            acc = acc * shrink + dot(v, w.astype(BF16), ((1,), (0,)))
            return new_top, mass, acc

        init = (
            jnp.full((1, blk), NEG_FILL, F32),
            jnp.zeros((1, blk), F32),
            jnp.zeros((hd, blk), F32),
        )
        top, mass, acc = lax.fori_loop(low_ref[i], i + 1, key_block, init)
        inv = 1.0 / mass
        acc = acc * inv
        full_ref[s0] = acc[:, :rows]
        full_ref[s1] = acc[:, rows:]
        low = acc.astype(BF16)
        out_ref[s0] = low[:, :rows]
        out_ref[s1] = low[:, rows:]
        top_ref[i] = top
        inv_ref[i] = inv
        return c

    lax.fori_loop(0, count // rep, lambda n, c: query_block(n * rep + part_ref[0], c), 0)


def attn_bwd_kernel(
    rep, slot_ref, low_ref, ends_ref, part_ref, qkv_ref, da_ref, full_ref, top_ref, inv_ref,
    out_ref, key_ref, value_ref, dk_ref, dv_ref,
):
    slots, _, rows = qkv_ref.shape
    blk = 2 * rows
    count = slots // 2
    hd = HEAD_DIM

    def flip(s, c):
        key_ref[s] = qkv_ref[s, hd : 2 * hd, :].T
        value_ref[s] = qkv_ref[s, 2 * hd :, :].T
        return c

    lax.fori_loop(0, slots, flip, 0)
    dk_ref[...] = jnp.zeros_like(dk_ref)
    dv_ref[...] = jnp.zeros_like(dv_ref)
    if rep > 1:
        out_ref[...] = jnp.zeros_like(out_ref)

    def pair(ref, a, b, lo, hi):
        return jnp.concatenate([ref[a, lo:hi, :], ref[b, lo:hi, :]], axis=1)

    def query_block(i, c):
        s0, s1 = slot_ref[2 * i], slot_ref[2 * i + 1]
        q = pair(qkv_ref, s0, s1, 0, hd)
        da = pair(da_ref, s0, s1, 0, hd)
        full = pair(full_ref, s0, s1, 0, hd)
        delta = jnp.sum(da.astype(F32) * full, axis=0, keepdims=True)
        top, inv = top_ref[i], inv_ref[i]

        def key_block(j, dq):
            k0, k1 = slot_ref[2 * j], slot_ref[2 * j + 1]
            k = jnp.concatenate([key_ref[k0], key_ref[k1]], axis=0)
            v = jnp.concatenate([value_ref[k0], value_ref[k1]], axis=0)
            s = dot(k, q, ((1,), (0,))) * (SCALE * LOG2E)
            s = jnp.where(block_mask(ends_ref, i, j, blk), s, NEG_FILL)
            p = jnp.exp2(s - top) * inv
            dp = dot(v, da, ((1,), (0,)))
            ds = (p * (dp - delta)).astype(BF16)
            dk_ref[j] += dot(q, ds, ((1,), (1,)))
            dv_ref[j] += dot(da, p.astype(BF16), ((1,), (1,)))
            return dq + dot(pair(qkv_ref, k0, k1, hd, 2 * hd), ds, ((1,), (0,)))

        dq = lax.fori_loop(low_ref[i], i + 1, key_block, jnp.zeros((hd, blk), F32))
        dq = (dq * SCALE).astype(BF16)
        out_ref[s0, :hd, :] = dq[:, :rows]
        out_ref[s1, :hd, :] = dq[:, rows:]
        return c

    lax.fori_loop(0, count // rep, lambda n, c: query_block(n * rep + part_ref[0], c), 0)

    def finish(j, c):
        k0, k1 = slot_ref[2 * j], slot_ref[2 * j + 1]
        dk = (dk_ref[j] * SCALE).astype(BF16)
        dv = dv_ref[j].astype(BF16)
        out_ref[k0, hd : 2 * hd, :] = dk[:, :rows]
        out_ref[k1, hd : 2 * hd, :] = dk[:, rows:]
        out_ref[k0, 2 * hd :, :] = dv[:, :rows]
        out_ref[k1, 2 * hd :, :] = dv[:, rows:]
        return c

    lax.fori_loop(0, count, finish, 0)


SMEM = pl.BlockSpec(memory_space=pltpu.SMEM)
VMEM = pl.BlockSpec(memory_space=pltpu.VMEM)


def attn_fwd(rep, scalars, qkv):
    slots, _, rows = qkv.shape
    stat = jax.ShapeDtypeStruct((slots // 2, 1, 2 * rows), F32)
    return pl.pallas_call(
        functools.partial(attn_fwd_kernel, rep),
        in_specs=[SMEM] * 4 + [VMEM],
        out_specs=[VMEM] * 4,
        out_shape=[
            jax.ShapeDtypeStruct((slots, HEAD_DIM, rows), BF16),
            jax.ShapeDtypeStruct((slots, HEAD_DIM, rows), F32),
            stat,
            stat,
        ],
        scratch_shapes=[pltpu.VMEM((slots, rows, HEAD_DIM), BF16)],
        cost_estimate=pl.CostEstimate(flops=10**9, bytes_accessed=3 * 10**6, transcendentals=2 * 10**6),
        compiler_params=pltpu.CompilerParams(vmem_limit_bytes=32 * 2**20),
        name="attn_fwd",
    )(*scalars, qkv)


def attn_bwd(rep, scalars, qkv, da, full, top, inv):
    slots, _, rows = qkv.shape
    return pl.pallas_call(
        functools.partial(attn_bwd_kernel, rep),
        in_specs=[SMEM] * 4 + [VMEM] * 5,
        out_specs=VMEM,
        out_shape=jax.ShapeDtypeStruct((slots, 3 * HEAD_DIM, rows), BF16),
        scratch_shapes=[
            pltpu.VMEM((slots, rows, HEAD_DIM), BF16),
            pltpu.VMEM((slots, rows, HEAD_DIM), BF16),
            pltpu.VMEM((slots // 2, HEAD_DIM, 2 * rows), F32),
            pltpu.VMEM((slots // 2, HEAD_DIM, 2 * rows), F32),
        ],
        cost_estimate=pl.CostEstimate(flops=2 * 10**9, bytes_accessed=4 * 10**6, transcendentals=2 * 10**6),
        compiler_params=pltpu.CompilerParams(vmem_limit_bytes=32 * 2**20),
        name="attn_bwd",
    )(*scalars, qkv, da, full, top, inv)


def norm_back(grad_normed, unit_rows, inv_rows, gain_vec):
    scaled = grad_normed * gain_vec
    return inv_rows * (scaled - unit_rows * jnp.mean(scaled * unit_rows, axis=-1, keepdims=True))


class Moves:
    def __init__(self, n_dp, n_ctx):
        self.n_dp, self.n_ctx = n_dp, n_ctx
        self.grid = n_dp == 2 and n_ctx == 16

    def swap(self, v):
        return lax.ppermute(v, "dp", [(0, 1), (1, 0)])

    def rows_gather(self, v):
        if self.grid:
            return jnp.concatenate([v, self.swap(v)], axis=0)
        return lax.all_gather(v, "dp", axis=0, tiled=True)

    def rows_sum(self, v):
        if self.grid:
            rows = v.shape[0] // 2
            return v[:rows] + self.swap(v[rows:].astype(BF16)).astype(F32)
        return lax.psum_scatter(v, "dp", scatter_dimension=0, tiled=True)

    def columns_gather(self, v):
        if self.grid:
            rows = v.shape[0] // 2
            other = self.swap(v)
            other = jnp.concatenate([other[rows:], other[:rows]], axis=0)
            first = lax.axis_index("dp") == 0
            return jnp.concatenate([jnp.where(first, v, other), jnp.where(first, other, v)], axis=1)
        return lax.all_gather(v, "dp", axis=1, tiled=True)

    def to_ctx(self, v):
        return lax.all_to_all(v, "ctx", 0, 0, tiled=True)

    def sum_product(self, left, right, first):
        if not self.grid:
            part = dot(left, right, ((1,), (0,))).astype(BF16)
            return lax.psum_scatter(part, "ctx", scatter_dimension=0, tiled=True).astype(F32)
        chunk, depth, wide = left.shape[0] // 16, left.shape[1], right.shape[1]
        c = lax.axis_index("ctx")
        z, y, x = c // 4, (c // 2) % 2, c % 2
        left = left.reshape(4, 2, 2, chunk, depth)
        axis = {"x": 2, "y": 1}[first]
        here = {"x": x, "y": y}
        step = {"x": 1, "y": 2}
        second = {"x": "y", "y": "x"}[first]

        def product(at):
            rows = lax.dynamic_index_in_dim(left, at, axis, keepdims=False)
            out = dot(rows.reshape(8 * chunk, depth), right, ((1,), (0,)))
            return out.astype(BF16).reshape(4, 2, chunk, wide)

        def across(v, name):
            return lax.ppermute(v, "ctx", [(i, i ^ step[name]) for i in range(16)])

        got = across(product(1 - here[first]), first)
        kept = product(here[first])

        def half(at):
            a = lax.dynamic_index_in_dim(got, at, 1, keepdims=False)
            b = lax.dynamic_index_in_dim(kept, at, 1, keepdims=False)
            return a.astype(F32) + b.astype(F32)

        got_two = across(half(1 - here[second]).astype(BF16), second)
        own = half(here[second]) + got_two.astype(F32)
        up = jnp.zeros((chunk, wide), F32)
        down = jnp.zeros((chunk, wide), F32)

        def level(at):
            return lax.dynamic_index_in_dim(own, jnp.clip(at, 0, 3), 0, keepdims=False)

        for n in range(1, 4):
            send_up = (level(z + 4 - n) + up).astype(BF16)
            send_down = (level(z - 4 + n) + down).astype(BF16)
            up = lax.ppermute(send_up, "ctx", [(i, i + 4) for i in range(12)]).astype(F32)
            down = lax.ppermute(send_down, "ctx", [(i + 4, i) for i in range(12)]).astype(F32)
        return level(z) + up + down


def per_device(
    moves,
    latent_in,
    gain_attn,
    w_query,
    w_key,
    w_value,
    w_out,
    gain_ffn,
    w_gate,
    w_up,
    w_down,
    cotangent,
    seq_lengths,
    span_order,
):
    n_dp, n_ctx = moves.n_dp, moves.n_ctx
    rows, width = latent_in.shape
    ff = w_gate.shape[1]
    dp, ctx = lax.axis_index("dp"), lax.axis_index("ctx")
    rep = n_ctx // HEADS

    ends = jnp.cumsum(seq_lengths[0]).astype(jnp.int32)
    slot_of = jnp.zeros((n_ctx,), jnp.int32).at[span_order[0]].set(jnp.arange(n_ctx, dtype=jnp.int32))
    starts = jnp.arange(n_ctx // 2, dtype=jnp.int32) * (2 * rows)
    low = jnp.max(jnp.where(starts[:, None] >= ends[None, :], ends[None, :], 0), axis=1) // (2 * rows)
    scalars = (slot_of, low, ends, (ctx % rep).reshape(1).astype(jnp.int32))

    share = ff // n_dp
    gate_w = lax.dynamic_slice_in_dim(w_gate, dp * share, share, 1)
    up_w = lax.dynamic_slice_in_dim(w_up, dp * share, share, 1)
    down_w = lax.dynamic_slice_in_dim(w_down, dp * share, share, 0)

    latent_f = latent_in.astype(F32)
    inv_one = lax.rsqrt(jnp.mean(latent_f * latent_f, axis=-1, keepdims=True) + EPS)
    unit_one = latent_f * inv_one
    normed_one = (unit_one * gain_attn).astype(BF16)

    def project(w):
        return dot(w, normed_one, ((0,), (1,))).astype(BF16).reshape(HEADS, HEAD_DIM, rows)

    qkv = jnp.concatenate([project(w_query), project(w_key), project(w_value)], axis=1)
    qkv = moves.to_ctx(jnp.repeat(qkv, rep, axis=0) if rep > 1 else qkv)
    normed_all = lax.all_gather(normed_one, "ctx", axis=0, tiled=True)

    out, full, top, inv = attn_fwd(rep, scalars, qkv)

    def from_heads(v):
        v = moves.to_ctx(v)
        if rep > 1:
            v = jnp.sum(v.astype(F32).reshape((HEADS, rep) + v.shape[1:]), axis=1).astype(BF16)
        return v

    attn_t = from_heads(out).reshape(width, rows)
    resid = latent_f + dot(attn_t, w_out, ((0,), (0,)))
    inv_two = lax.rsqrt(jnp.mean(resid * resid, axis=-1, keepdims=True) + EPS)
    unit_two = resid * inv_two
    normed_two = (unit_two * gain_ffn).astype(BF16)

    top_all = moves.rows_gather(cotangent)
    grad_hidden = dot(top_all, down_w, ((1,), (1,)))
    normed_two_all = moves.rows_gather(normed_two)
    gate_pre = dot(normed_two_all, gate_w, ((1,), (0,)))
    up_pre = dot(normed_two_all, up_w, ((1,), (0,)))
    gate_sig = jax.nn.sigmoid(gate_pre)
    swish = gate_pre * gate_sig
    hidden = (swish * up_pre).astype(BF16)
    latents = (resid + moves.rows_sum(dot(hidden, down_w, ((1,), (0,))))).astype(BF16)
    grad_gate = (grad_hidden * up_pre * gate_sig * (1.0 + gate_pre * (1.0 - gate_sig))).astype(BF16)
    grad_up = (grad_hidden * swish).astype(BF16)
    grad_norm_two = moves.rows_sum(
        dot(grad_gate, gate_w, ((1,), (1,))) + dot(grad_up, up_w, ((1,), (1,)))
    )
    grad_resid = cotangent.astype(F32) + norm_back(grad_norm_two, unit_two, inv_two, gain_ffn)
    grad_mixed = grad_resid.astype(BF16)

    grad_attn = dot(w_out, grad_mixed, ((1,), (1,))).astype(BF16).reshape(HEADS, HEAD_DIM, rows)
    grad_attn = moves.to_ctx(jnp.repeat(grad_attn, rep, axis=0) if rep > 1 else grad_attn)
    grad_qkv = attn_bwd(rep, scalars, qkv, grad_attn, full, top, inv)

    strip = width // n_dp
    down_sum = moves.sum_product(hidden.T, top_all, "x")
    normed_rows = lax.dynamic_slice_in_dim(normed_two_all, dp * strip, strip, 1).T
    gate_sum = moves.sum_product(normed_rows, moves.columns_gather(grad_gate), "y")
    up_sum = moves.sum_product(normed_rows, moves.columns_gather(grad_up), "x")
    attn_rows = moves.rows_gather(attn_t.T)
    attn_rows = lax.dynamic_slice_in_dim(attn_rows, dp * strip, strip, 1).T
    out_sum = moves.sum_product(attn_rows, moves.rows_gather(grad_mixed), "y")

    lanes = jnp.transpose(grad_qkv, (0, 2, 1)).reshape(n_ctx * rows, 3 * HEAD_DIM)
    head_grad = dot(normed_all, lanes, ((0,), (0,)))
    head_grad = head_grad.reshape(n_dp, strip, 3 * HEAD_DIM)
    if moves.grid:
        mine = lax.dynamic_index_in_dim(head_grad, dp, 0, keepdims=False)
        theirs = lax.dynamic_index_in_dim(head_grad, 1 - dp, 0, keepdims=False)
        head_grad = mine + moves.swap(theirs.astype(BF16)).astype(F32)
    else:
        head_grad = lax.psum_scatter(head_grad, "dp", scatter_dimension=0, tiled=False)
    own = strip // n_ctx
    head_grad = moves.to_ctx(head_grad.astype(BF16).reshape(n_ctx, own, 3 * HEAD_DIM)).astype(F32)
    head_grad = jnp.sum(head_grad.reshape(HEADS, rep, own, 3, HEAD_DIM), axis=1)
    head_grad = jnp.transpose(head_grad, (2, 1, 0, 3)).reshape(3, own, width)
    query_sum, key_sum, value_sum = head_grad[0], head_grad[1], head_grad[2]

    first_row = (dp * n_ctx + ctx) * own

    def own_rows(w):
        return lax.dynamic_slice_in_dim(w, first_row, own, 0).astype(F32)

    def own_gain(v):
        return lax.dynamic_slice_in_dim(v, first_row, own, 0)

    gain_ffn_sum = jnp.sum(own_rows(w_gate) * gate_sum + own_rows(w_up) * up_sum, axis=1) / own_gain(gain_ffn)
    gain_attn_sum = jnp.sum(
        own_rows(w_query) * query_sum + own_rows(w_key) * key_sum + own_rows(w_value) * value_sum, axis=1
    ) / own_gain(gain_attn)

    back = from_heads(grad_qkv).reshape(HEADS, 3, HEAD_DIM, rows)
    grad_norm_one = sum(
        dot(back[:, n].reshape(width, rows), w, ((0,), (1,)))
        for n, w in enumerate((w_query, w_key, w_value))
    )
    latent_grad = (grad_resid + norm_back(grad_norm_one, unit_one, inv_one, gain_attn)).astype(BF16)
    return (
        latents,
        latent_grad,
        gain_attn_sum,
        query_sum,
        key_sum,
        value_sum,
        out_sum,
        gain_ffn_sum,
        gate_sum,
        up_sum,
        down_sum,
    )


def solution(mesh):
    moves = Moves(mesh.shape["dp"], mesh.shape["ctx"])
    rows, whole, share = P(("dp", "ctx"), None), P(), P("dp", None)
    flat = P(("dp", "ctx"))
    return jax.shard_map(
        functools.partial(per_device, moves),
        mesh=mesh,
        in_specs=(rows,) + (whole,) * 9 + (rows, share, share),
        out_specs=(rows, rows, flat, rows, rows, rows, rows, flat, rows, rows, rows),
        check_vma=False,
    )
```

```python
import functools

import jax
import jax.numpy as jnp
from jax import lax
from jax.experimental import pallas as pl
from jax.experimental.pallas import tpu as pltpu
from jax.sharding import PartitionSpec as P

HEADS = 16
HEAD_DIM = 64
EPS = 1e-06
NEG_FILL = -1e30
LOG2E = 1.4426950408889634
SCALE = HEAD_DIM**-0.5

BF16 = jnp.bfloat16
F32 = jnp.float32


def dot(a, b, dims):
    return lax.dot_general(a, b, (dims, ((), ())), preferred_element_type=F32)


def query_starts(ends_ref, pos):
    start = jnp.zeros_like(pos)
    for n in range(ends_ref.shape[0]):
        start = jnp.where(pos >= ends_ref[n], ends_ref[n], start)
    return start


def block_mask(ends_ref, i, j, blk):
    pos = lax.broadcasted_iota(jnp.int32, (1, blk), 1) + i * blk
    start = query_starts(ends_ref, pos) - j * blk
    key = lax.broadcasted_iota(jnp.int32, (blk, blk), 0)
    return (key <= pos - j * blk) & (key >= start)


def attn_fwd_kernel(rep, slot_ref, low_ref, ends_ref, part_ref, qkv_ref, out_ref, full_ref, top_ref, inv_ref, key_ref):
    slots, _, rows = qkv_ref.shape
    blk = 2 * rows
    count = slots // 2
    hd = HEAD_DIM

    def flip(s, c):
        key_ref[s] = qkv_ref[s, hd : 2 * hd, :].T
        return c

    lax.fori_loop(0, slots, flip, 0)
    if rep > 1:
        out_ref[...] = jnp.zeros_like(out_ref)
        full_ref[...] = jnp.zeros_like(full_ref)

    def query_block(i, c):
        s0, s1 = slot_ref[2 * i], slot_ref[2 * i + 1]
        q = jnp.concatenate([qkv_ref[s0, :hd, :], qkv_ref[s1, :hd, :]], axis=1)

        def key_block(j, state):
            top, mass, acc = state
            k0, k1 = slot_ref[2 * j], slot_ref[2 * j + 1]
            k = jnp.concatenate([key_ref[k0], key_ref[k1]], axis=0)
            v = jnp.concatenate([qkv_ref[k0, 2 * hd :, :], qkv_ref[k1, 2 * hd :, :]], axis=1)
            s = dot(k, q, ((1,), (0,))) * (SCALE * LOG2E)
            s = jnp.where(block_mask(ends_ref, i, j, blk), s, NEG_FILL)
            new_top = jnp.maximum(top, jnp.max(s, axis=0, keepdims=True))
            shrink = jnp.exp2(top - new_top)
            w = jnp.exp2(s - new_top)
            mass = mass * shrink + jnp.sum(w, axis=0, keepdims=True)
            acc = acc * shrink + dot(v, w.astype(BF16), ((1,), (0,)))
            return new_top, mass, acc

        init = (
            jnp.full((1, blk), NEG_FILL, F32),
            jnp.zeros((1, blk), F32),
            jnp.zeros((hd, blk), F32),
        )
        top, mass, acc = lax.fori_loop(low_ref[i], i + 1, key_block, init)
        inv = 1.0 / mass
        acc = acc * inv
        full_ref[s0] = acc[:, :rows]
        full_ref[s1] = acc[:, rows:]
        low = acc.astype(BF16)
        out_ref[s0] = low[:, :rows]
        out_ref[s1] = low[:, rows:]
        top_ref[i] = top
        inv_ref[i] = inv
        return c

    lax.fori_loop(0, count // rep, lambda n, c: query_block(n * rep + part_ref[0], c), 0)


def attn_bwd_kernel(
    rep, place, slot_ref, low_ref, ends_ref, part_ref, qkv_ref, da_ref, full_ref, top_ref, inv_ref,
    out_ref, key_ref, value_ref, dk_ref, dv_ref,
):
    slots, _, rows = qkv_ref.shape
    blk = 2 * rows
    count = slots // 2
    hd = HEAD_DIM

    def flip(s, c):
        key_ref[s] = qkv_ref[s, hd : 2 * hd, :].T
        value_ref[s] = qkv_ref[s, 2 * hd :, :].T
        return c

    lax.fori_loop(0, slots, flip, 0)
    dk_ref[...] = jnp.zeros_like(dk_ref)
    dv_ref[...] = jnp.zeros_like(dv_ref)
    if rep > 1:
        out_ref[...] = jnp.zeros_like(out_ref)

    def pair(ref, a, b, lo, hi):
        return jnp.concatenate([ref[a, lo:hi, :], ref[b, lo:hi, :]], axis=1)

    def query_block(i, c):
        s0, s1 = slot_ref[2 * i], slot_ref[2 * i + 1]
        q = pair(qkv_ref, s0, s1, 0, hd)
        da = pair(da_ref, s0, s1, 0, hd)
        full = pair(full_ref, s0, s1, 0, hd)
        delta = jnp.sum(da.astype(F32) * full, axis=0, keepdims=True)
        top, inv = top_ref[i], inv_ref[i]

        def key_block(j, dq):
            k0, k1 = slot_ref[2 * j], slot_ref[2 * j + 1]
            k = jnp.concatenate([key_ref[k0], key_ref[k1]], axis=0)
            v = jnp.concatenate([value_ref[k0], value_ref[k1]], axis=0)
            s = dot(k, q, ((1,), (0,))) * (SCALE * LOG2E)
            s = jnp.where(block_mask(ends_ref, i, j, blk), s, NEG_FILL)
            p = jnp.exp2(s - top) * inv
            dp = dot(v, da, ((1,), (0,)))
            ds = (p * (dp - delta)).astype(BF16)
            dk_ref[j] += dot(q, ds, ((1,), (1,)))
            dv_ref[j] += dot(da, p.astype(BF16), ((1,), (1,)))
            return dq + dot(pair(qkv_ref, k0, k1, hd, 2 * hd), ds, ((1,), (0,)))

        dq = lax.fori_loop(low_ref[i], i + 1, key_block, jnp.zeros((hd, blk), F32))
        dq = (dq * SCALE).astype(BF16)
        out_ref[place(s0), :hd, :] = dq[:, :rows]
        out_ref[place(s1), :hd, :] = dq[:, rows:]
        return c

    lax.fori_loop(0, count // rep, lambda n, c: query_block(n * rep + part_ref[0], c), 0)

    def finish(j, c):
        k0, k1 = place(slot_ref[2 * j]), place(slot_ref[2 * j + 1])
        dk = (dk_ref[j] * SCALE).astype(BF16)
        dv = dv_ref[j].astype(BF16)
        out_ref[k0, hd : 2 * hd, :] = dk[:, :rows]
        out_ref[k1, hd : 2 * hd, :] = dk[:, rows:]
        out_ref[k0, 2 * hd :, :] = dv[:, :rows]
        out_ref[k1, 2 * hd :, :] = dv[:, rows:]
        return c

    lax.fori_loop(0, count, finish, 0)


def in_hbm(v):
    return pltpu.with_memory_space_constraint(v, pltpu.HBM)


def call(kernel, name, args, after=(), smem=0, outs=(), scratch=(), vmem=24, far=0):
    held = len(args)

    def body(*refs):
        return kernel(*refs[:held], *refs[held + len(after) :])

    if far:
        args = (*args[: held - far], *(in_hbm(v) for v in args[held - far :]))
    return pl.pallas_call(
        body,
        in_specs=[SMEM] * smem + [VMEM] * (held - smem - far) + [HBM] * far + [ANY] * len(after),
        out_specs=[VMEM] * len(outs),
        out_shape=[jax.ShapeDtypeStruct(*o) for o in outs],
        scratch_shapes=list(scratch),
        cost_estimate=COST,
        compiler_params=pltpu.CompilerParams(vmem_limit_bytes=vmem * 2**20),
        name=name,
    )(*args, *after)


COST = pl.CostEstimate(flops=10**6, bytes_accessed=10**5, transcendentals=0)
SMEM = pl.BlockSpec(memory_space=pltpu.SMEM)
ANY = pl.BlockSpec(memory_space=pl.ANY)
HBM = pl.BlockSpec(memory_space=pltpu.HBM)
VMEM = pl.BlockSpec(memory_space=pltpu.VMEM)


def attn_fwd(rep, scalars, qkv, after=()):
    slots, _, rows = qkv.shape
    stat = ((slots // 2, 1, 2 * rows), F32)
    return call(
        functools.partial(attn_fwd_kernel, rep),
        "attn_fwd",
        (*scalars, qkv),
        after,
        smem=4,
        outs=[((slots, HEAD_DIM, rows), BF16), ((slots, HEAD_DIM, rows), F32), stat, stat],
        scratch=[pltpu.VMEM((slots, rows, HEAD_DIM), BF16)],
        vmem=24,
    )


def attn_bwd(rep, place, scalars, qkv, da, full, top, inv, after=()):
    slots, _, rows = qkv.shape
    return call(
        functools.partial(attn_bwd_kernel, rep, place),
        "attn_bwd",
        (*scalars, qkv, da, full, top, inv),
        after,
        smem=4,
        outs=[((slots, 3 * HEAD_DIM, rows), BF16)],
        scratch=[
            pltpu.VMEM((slots, rows, HEAD_DIM), BF16),
            pltpu.VMEM((slots, rows, HEAD_DIM), BF16),
            pltpu.VMEM((slots // 2, HEAD_DIM, 2 * rows), F32),
            pltpu.VMEM((slots // 2, HEAD_DIM, 2 * rows), F32),
        ],
        vmem=24,
    )[0]


def positions(seq_lengths, span_order, rows, part):
    ends = jnp.cumsum(seq_lengths[0]).astype(jnp.int32)
    count = span_order.shape[1]
    blocks = jnp.arange(count, dtype=jnp.int32)
    slot_of = jnp.sum(jnp.where(span_order[0][None, :] == blocks[:, None], blocks[None, :], 0), axis=1)
    starts = jnp.arange(count // 2, dtype=jnp.int32) * (2 * rows)
    low = jnp.max(jnp.where(starts[:, None] >= ends[None, :], ends[None, :], 0), axis=1) // (2 * rows)
    return slot_of.astype(jnp.int32), low.astype(jnp.int32), ends, part.reshape(1).astype(jnp.int32)


def norm_back(grad_normed, unit_rows, inv_rows, gain_vec):
    scaled = grad_normed * gain_vec
    return inv_rows * (scaled - unit_rows * jnp.mean(scaled * unit_rows, axis=-1, keepdims=True))


class Moves:
    def __init__(self, n_dp, n_ctx):
        self.n_dp, self.n_ctx = n_dp, n_ctx

    def rows_gather(self, v):
        return lax.all_gather(v, "dp", axis=0, tiled=True)

    def rows_sum(self, v):
        return lax.psum_scatter(v, "dp", scatter_dimension=0, tiled=True)

    def columns_gather(self, v):
        return lax.all_gather(v, "dp", axis=1, tiled=True)

    def to_ctx(self, v):
        return lax.all_to_all(v, "ctx", 0, 0, tiled=True)

    def sum_product(self, left, right):
        part = dot(left, right, ((1,), (0,))).astype(BF16)
        return lax.psum_scatter(part, "ctx", scatter_dimension=0, tiled=True).astype(F32)


def per_device_any(
    moves,
    latent_in,
    gain_attn,
    w_query,
    w_key,
    w_value,
    w_out,
    gain_ffn,
    w_gate,
    w_up,
    w_down,
    cotangent,
    seq_lengths,
    span_order,
):
    n_dp, n_ctx = moves.n_dp, moves.n_ctx
    rows, width = latent_in.shape
    ff = w_gate.shape[1]
    dp, ctx = lax.axis_index("dp"), lax.axis_index("ctx")
    rep = n_ctx // HEADS

    scalars = positions(seq_lengths, span_order, rows, ctx % rep)

    share = ff // n_dp
    gate_w = lax.dynamic_slice_in_dim(w_gate, dp * share, share, 1)
    up_w = lax.dynamic_slice_in_dim(w_up, dp * share, share, 1)
    down_w = lax.dynamic_slice_in_dim(w_down, dp * share, share, 0)

    latent_f = latent_in.astype(F32)
    inv_one = lax.rsqrt(jnp.mean(latent_f * latent_f, axis=-1, keepdims=True) + EPS)
    unit_one = latent_f * inv_one
    normed_one = (unit_one * gain_attn).astype(BF16)

    def project(w):
        return dot(w, normed_one, ((0,), (1,))).astype(BF16).reshape(HEADS, HEAD_DIM, rows)

    qkv = jnp.concatenate([project(w_query), project(w_key), project(w_value)], axis=1)
    qkv = moves.to_ctx(jnp.repeat(qkv, rep, axis=0) if rep > 1 else qkv)
    normed_all = lax.all_gather(normed_one, "ctx", axis=0, tiled=True)

    out, full, top, inv = attn_fwd(rep, scalars, qkv)

    def from_heads(v):
        v = moves.to_ctx(v)
        if rep > 1:
            v = jnp.sum(v.astype(F32).reshape((HEADS, rep) + v.shape[1:]), axis=1).astype(BF16)
        return v

    attn_t = from_heads(out).reshape(width, rows)
    resid = latent_f + dot(attn_t, w_out, ((0,), (0,)))
    inv_two = lax.rsqrt(jnp.mean(resid * resid, axis=-1, keepdims=True) + EPS)
    unit_two = resid * inv_two
    normed_two = (unit_two * gain_ffn).astype(BF16)

    top_all = moves.rows_gather(cotangent)
    grad_hidden = dot(top_all, down_w, ((1,), (1,)))
    normed_two_all = moves.rows_gather(normed_two)
    gate_pre = dot(normed_two_all, gate_w, ((1,), (0,)))
    up_pre = dot(normed_two_all, up_w, ((1,), (0,)))
    gate_sig = jax.nn.sigmoid(gate_pre)
    swish = gate_pre * gate_sig
    hidden = (swish * up_pre).astype(BF16)
    latents = (resid + moves.rows_sum(dot(hidden, down_w, ((1,), (0,))))).astype(BF16)
    grad_gate = (grad_hidden * up_pre * gate_sig * (1.0 + gate_pre * (1.0 - gate_sig))).astype(BF16)
    grad_up = (grad_hidden * swish).astype(BF16)
    grad_norm_two = moves.rows_sum(
        dot(grad_gate, gate_w, ((1,), (1,))) + dot(grad_up, up_w, ((1,), (1,)))
    )
    grad_resid = cotangent.astype(F32) + norm_back(grad_norm_two, unit_two, inv_two, gain_ffn)
    grad_mixed = grad_resid.astype(BF16)

    grad_attn = dot(w_out, grad_mixed, ((1,), (1,))).astype(BF16).reshape(HEADS, HEAD_DIM, rows)
    grad_attn = moves.to_ctx(jnp.repeat(grad_attn, rep, axis=0) if rep > 1 else grad_attn)
    grad_qkv = attn_bwd(rep, lambda slot: slot, scalars, qkv, grad_attn, full, top, inv)

    strip = width // n_dp
    down_sum = moves.sum_product(hidden.T, top_all)
    normed_rows = lax.dynamic_slice_in_dim(normed_two_all, dp * strip, strip, 1).T
    gate_sum = moves.sum_product(normed_rows, moves.columns_gather(grad_gate))
    up_sum = moves.sum_product(normed_rows, moves.columns_gather(grad_up))
    attn_rows = moves.rows_gather(attn_t.T)
    attn_rows = lax.dynamic_slice_in_dim(attn_rows, dp * strip, strip, 1).T
    out_sum = moves.sum_product(attn_rows, moves.rows_gather(grad_mixed))

    lanes = jnp.transpose(grad_qkv, (0, 2, 1)).reshape(n_ctx * rows, 3 * HEAD_DIM)
    head_grad = dot(normed_all, lanes, ((0,), (0,)))
    head_grad = head_grad.reshape(n_dp, strip, 3 * HEAD_DIM)
    head_grad = lax.psum_scatter(head_grad, "dp", scatter_dimension=0, tiled=False)
    own = strip // n_ctx
    head_grad = moves.to_ctx(head_grad.astype(BF16).reshape(n_ctx, own, 3 * HEAD_DIM)).astype(F32)
    head_grad = jnp.sum(head_grad.reshape(HEADS, rep, own, 3, HEAD_DIM), axis=1)
    head_grad = jnp.transpose(head_grad, (2, 1, 0, 3)).reshape(3, own, width)
    query_sum, key_sum, value_sum = head_grad[0], head_grad[1], head_grad[2]

    first_row = (dp * n_ctx + ctx) * own

    def own_rows(w):
        return lax.dynamic_slice_in_dim(w, first_row, own, 0).astype(F32)

    def own_gain(v):
        return lax.dynamic_slice_in_dim(v, first_row, own, 0)

    gain_ffn_sum = jnp.sum(own_rows(w_gate) * gate_sum + own_rows(w_up) * up_sum, axis=1) / own_gain(gain_ffn)
    gain_attn_sum = jnp.sum(
        own_rows(w_query) * query_sum + own_rows(w_key) * key_sum + own_rows(w_value) * value_sum, axis=1
    ) / own_gain(gain_attn)

    back = from_heads(grad_qkv).reshape(HEADS, 3, HEAD_DIM, rows)
    grad_norm_one = sum(
        dot(back[:, n].reshape(width, rows), w, ((0,), (1,)))
        for n, w in enumerate((w_query, w_key, w_value))
    )
    latent_grad = (grad_resid + norm_back(grad_norm_one, unit_one, inv_one, gain_attn)).astype(BF16)
    return (
        latents,
        latent_grad,
        gain_attn_sum,
        query_sum,
        key_sum,
        value_sum,
        out_sum,
        gain_ffn_sum,
        gate_sum,
        up_sum,
        down_sum,
    )


def low_t(v):
    return v.astype(F32).T.astype(BF16)


def sel(at, other):
    return 1 - at if other else at


def norm_qkv_kernel(x_ref, gain_ref, wq_ref, wk_ref, wv_ref, n_ref, qkv_ref, held_ref, sems):
    loads = [pltpu.make_async_copy(w, held_ref.at[t], sems.at[t]) for t, w in enumerate((wq_ref, wk_ref, wv_ref))]
    for load in loads:
        load.start()
    x = x_ref[...].astype(F32)
    inv = lax.rsqrt(jnp.mean(x * x, axis=-1, keepdims=True) + EPS)
    n = (x * inv * gain_ref[...]).astype(BF16)
    n_ref[...] = n
    cols = 256
    for t, load in enumerate(loads):
        load.wait()
        for c in range(0, held_ref.shape[2], cols):
            p = dot(n, held_ref[t, :, c : c + cols], ((1,), (0,))).T.astype(BF16)
            for h in range(cols // HEAD_DIM):
                qkv_ref[c // HEAD_DIM + h, t * HEAD_DIM : (t + 1) * HEAD_DIM, :] = p[h * HEAD_DIM : (h + 1) * HEAD_DIM]


def norm_qkv(x, gain, wq, wk, wv):
    rows, width = x.shape
    return call(
        norm_qkv_kernel,
        "norm_qkv",
        (x, gain.reshape(1, width), wq, wk, wv),
        outs=[
            ((rows, width), BF16),
            ((HEADS, 3 * HEAD_DIM, rows), BF16),
        ],
        scratch=[pltpu.VMEM((3, width, width), BF16), pltpu.SemaphoreType.DMA((3,))],
        far=3,
    )


def out_norm_kernel(at_ref, ab_ref, x_ref, gain_ref, w_ref, resid_ref, n_ref, send_ref, held_ref, sem):
    load = pltpu.make_async_copy(w_ref, held_ref, sem)
    load.start()
    left = low_t(ab_ref[...])
    half = send_ref.shape[0]
    send_ref[...] = ab_ref[pl.ds(pl.multiple_of((1 - at_ref[0]) * half, half), half), :]
    load.wait()
    cols = 256
    mixed = [dot(left, held_ref[:, c : c + cols], ((1,), (0,))) for c in range(0, held_ref.shape[1], cols)]
    resid = x_ref[...].astype(F32) + jnp.concatenate(mixed, axis=1)
    resid_ref[...] = resid
    inv = lax.rsqrt(jnp.mean(resid * resid, axis=-1, keepdims=True) + EPS)
    n_ref[...] = (resid * inv * gain_ref[...]).astype(BF16)


def out_norm(at, ab, x, gain, w, after):
    rows, width = x.shape
    return call(
        out_norm_kernel,
        "out_norm",
        (at, ab, x, gain.reshape(1, width), w),
        after,
        smem=1,
        outs=[((rows, width), F32), ((rows, width), BF16), ((width // 2, rows), BF16)],
        scratch=[pltpu.VMEM(w.shape, BF16), pltpu.SemaphoreType.DMA],
        far=1,
    )


def ffn_kernel(
    at_ref, n0_ref, n1_ref, dy0_ref, dy1_ref, wg_ref, wu_ref, wd_ref,
    hid_ref, d0_ref, d1_ref, sx_ref, sy_ref, px_ref, py_ref, kx_ref, ky_ref,
    n_ref, dy_ref, dg_ref, du_ref, hid_t_ref, n_t_ref, g_w, u_w, d_w, sems,
):
    rows, width = n0_ref.shape
    share = g_w.shape[1]
    first = pl.multiple_of(at_ref[0] * share, 128)
    parts = ((0, 768), (768, share))
    loads = []
    for n, (lo, hi) in enumerate(parts):
        cols = pl.ds(pl.multiple_of(first + lo, 128), hi - lo)
        loads.append(
            (
                pltpu.make_async_copy(wg_ref.at[:, cols], g_w.at[:, pl.ds(lo, hi - lo)], sems.at[n, 0]),
                pltpu.make_async_copy(wu_ref.at[:, cols], u_w.at[:, pl.ds(lo, hi - lo)], sems.at[n, 1]),
                pltpu.make_async_copy(wd_ref.at[cols, :], d_w.at[pl.ds(lo, hi - lo), :], sems.at[n, 2]),
            )
        )
        for load in loads[n]:
            load.start()
    n_ref[:rows] = n0_ref[...]
    n_ref[rows:] = n1_ref[...]
    dy_ref[:rows] = dy0_ref[...]
    dy_ref[rows:] = dy1_ref[...]
    n_t_ref[...] = low_t(n_ref[...])

    for lo, hi in parts:
        for load in loads[parts.index((lo, hi))]:
            load.wait()
        for at in range(lo, hi, 256):
            lanes = slice(at, min(at + 256, share))
            g = dot(n_ref[...], g_w[:, lanes], ((1,), (0,)))
            u = dot(n_ref[...], u_w[:, lanes], ((1,), (0,)))
            dh = dot(dy_ref[...], d_w[lanes, :], ((1,), (1,)))
            sig = jax.nn.sigmoid(g)
            swish = g * sig
            hid = (swish * u).astype(BF16)
            dg = (dh * u * sig * (1.0 + g * (1.0 - sig))).astype(BF16)
            du = (dh * swish).astype(BF16)
            hid_ref[:, lanes] = hid
            hid_t_ref[lanes, :] = hid.astype(F32).T
            dg_ref[:, lanes] = dg
            du_ref[:, lanes] = du
            for k in range(dg.shape[1] // rows):
                to = (at // rows + k) * 2 * rows
                sx_ref[to : to + 2 * rows, :] = dg[:, k * rows : (k + 1) * rows]
                sy_ref[to : to + 2 * rows, :] = du[:, k * rows : (k + 1) * rows]

    for at in range(0, width, 256):
        cols = slice(at, at + 256)
        d = dot(dg_ref[...], g_w[cols, :], ((1,), (1,))) + dot(du_ref[...], u_w[cols, :], ((1,), (1,)))
        d0_ref[:, cols] = d[:rows]
        d1_ref[:, cols] = d[rows:].astype(BF16)

    own = width // 32
    chunk = share // 16
    base = px_ref.shape[0] - width
    padded = base // 16
    x, y = at_ref[1], at_ref[2]
    fill = jnp.zeros((padded - chunk, rows), F32)

    def put(ref, inner, z, xs, ys):
        c = z * 4 + ys * 2 + xs
        for half in range(2):
            lanes = slice(half * rows, (half + 1) * rows)
            v = hid_t_ref[pl.ds(pl.multiple_of(c * chunk, 8), chunk), lanes]
            to = ((inner * 4 + z) * 2 + half) * padded
            ref[to : to + padded, :] = jnp.concatenate([v, fill], axis=0).astype(BF16)
            for d in range(2):
                to = base + half * (width // 2) + ((inner * 4 + z) * 2 + d) * own
                at = pl.multiple_of(d * (width // 2) + c * own, own)
                ref[to : to + own, :] = n_t_ref[pl.ds(at, own), lanes]

    for inner in range(2):
        for z in range(4):
            put(kx_ref, inner, z, x, sel(y, inner))
            put(px_ref, inner, z, 1 - x, sel(y, inner))
            put(ky_ref, inner, z, sel(x, inner), y)
            put(py_ref, inner, z, sel(x, inner), 1 - y)


def ffn(at, n0, n1, dy0, dy1, wg, wu, wd):
    rows, width = n0.shape
    share = wg.shape[1] // 2
    padded = -(-(share // 16) // 16) * 16
    sizes = [share // rows * 2 * rows] * 2 + [16 * padded + width] * 4
    return call(
        ffn_kernel,
        "ffn",
        (at, n0, n1, dy0, dy1, wg, wu, wd),
        smem=1,
        outs=[((2 * rows, share), BF16), ((rows, width), F32), ((rows, width), BF16)]
        + [((n, rows), BF16) for n in sizes],
        scratch=[
            pltpu.VMEM((2 * rows, width), BF16),
            pltpu.VMEM((2 * rows, width), BF16),
            pltpu.VMEM((2 * rows, share), BF16),
            pltpu.VMEM((2 * rows, share), BF16),
            pltpu.VMEM((share, 2 * rows), F32),
            pltpu.VMEM((width, 2 * rows), BF16),
            pltpu.VMEM((width, share), BF16),
            pltpu.VMEM((width, share), BF16),
            pltpu.VMEM((share, width), BF16),
            pltpu.SemaphoreType.DMA((2, 3)),
        ],
        vmem=40,
        far=3,
    )


def ffn_out_kernel(at_ref, hid_ref, w_ref, y0_ref, y1_ref, held_ref, sem):
    rows, width = y0_ref.shape
    share = held_ref.shape[0]
    first = pl.multiple_of(at_ref[0] * share, 128)
    load = pltpu.make_async_copy(w_ref.at[pl.ds(first, share), :], held_ref, sem)
    load.start()
    load.wait()
    for at in range(0, width, 256):
        cols = slice(at, at + 256)
        y = dot(hid_ref[...], held_ref[:, cols], ((1,), (0,)))
        y0_ref[:, cols] = y[:rows]
        y1_ref[:, cols] = y[rows:].astype(BF16)


def ffn_out(at, hid, w, after):
    shape = (hid.shape[0] // 2, w.shape[1])
    return call(
        ffn_out_kernel,
        "ffn_out",
        (at, hid, w),
        after,
        smem=1,
        outs=[(shape, F32), (shape, BF16)],
        scratch=[pltpu.VMEM((hid.shape[1], w.shape[1]), BF16), pltpu.SemaphoreType.DMA],
        far=1,
    )


def ffn_back_kernel(d_ref, got_ref, resid_ref, gain_ref, dy_ref, w_ref, dres_ref, low_ref, da_ref, held_ref, sem):
    load = pltpu.make_async_copy(w_ref, held_ref, sem)
    load.start()
    d = d_ref[...] + got_ref[...].astype(F32)
    resid = resid_ref[...]
    inv = lax.rsqrt(jnp.mean(resid * resid, axis=-1, keepdims=True) + EPS)
    dres = dy_ref[...].astype(F32) + norm_back(d, resid * inv, inv, gain_ref[...])
    dres_ref[...] = dres
    low = dres.astype(BF16)
    low_ref[...] = low
    load.wait()
    for at in range(0, held_ref.shape[0], 256):
        da_ref[at : at + 256, :] = dot(held_ref[at : at + 256, :], low, ((1,), (1,))).astype(BF16)


def ffn_back(d, got, resid, gain, dy, w, after):
    rows, width = d.shape
    return call(
        ffn_back_kernel,
        "ffn_back",
        (d, got, resid, gain.reshape(1, width), dy, w),
        after,
        outs=[((rows, width), F32), ((rows, width), BF16), ((width, rows), BF16)],
        scratch=[pltpu.VMEM(w.shape, BF16), pltpu.SemaphoreType.DMA],
        far=1,
    )


def out_product_kernel(at_ref, ab_ref, got_ref, low0_ref, low1_ref, kx_ref, px_ref, ky_ref, py_ref, acc_ref):
    half, rows = got_ref.shape
    own = half // 16
    x, y = at_ref[1], at_ref[2]
    mine = ab_ref[pl.ds(pl.multiple_of(at_ref[0] * half, half), half), :]
    left = jnp.concatenate([mine, got_ref[...]], axis=1)
    right = jnp.concatenate([low0_ref[...], low1_ref[...]], axis=0)
    for at in range(0, acc_ref.shape[1], 256):
        acc_ref[:, at : at + 256] = dot(left, right[:, at : at + 256], ((1,), (0,)))
    tiles = acc_ref.shape[1] // 2 // rows

    def put(ref, inner, z, xs, ys, side):
        at = pl.multiple_of((z * 4 + ys * 2 + xs) * own, own)
        for j in range(tiles):
            lanes = slice((side * tiles + j) * rows, (side * tiles + j + 1) * rows)
            to = ((inner * 4 + z) * tiles + j) * own
            ref[to : to + own, :] = acc_ref[pl.ds(at, own), lanes].astype(BF16)

    for inner in range(2):
        for z in range(4):
            put(kx_ref, inner, z, x, sel(y, inner), 0)
            put(px_ref, inner, z, 1 - x, sel(y, inner), 0)
            put(ky_ref, inner, z, sel(x, inner), y, 1)
            put(py_ref, inner, z, sel(x, inner), 1 - y, 1)


def out_product(at, ab, got, low, low_mate, after):
    half, rows = got.shape
    high = half // 2 * (low.shape[1] // 2) // rows
    return call(
        out_product_kernel,
        "out_product",
        (at, ab, got, low, low_mate),
        after,
        smem=1,
        outs=[((high, rows), BF16)] * 4,
        scratch=[pltpu.VMEM((half, low.shape[1]), F32)],
    )


def store(refs, v, lanes, high, to):
    for inner in range(2):
        for z in range(4):
            at = (inner * 4 + z) * high
            refs[inner][z, to : to + high, :] = v[at : at + high, lanes]


def down_product_kernel(side, p0, p1, dy0, dy1, dy2, same_ref, other_ref):
    rows, width = dy0.shape
    half = width // 2
    padded = (p0.shape[0] - width) // 16

    def lanes(ref, k):
        at = k * 2 * padded
        return jnp.concatenate([ref[at : at + padded, :], ref[at + padded : at + 2 * padded, :]], axis=1)

    hid = jnp.concatenate([jnp.concatenate([lanes(p0, k), lanes(p1, k)], axis=1) for k in range(8)], axis=0)
    cols = slice(side * half, (side + 1) * half)
    dy = jnp.concatenate([dy0[:, cols], dy1[:, cols], dy2[...]], axis=0)
    v = dot(hid, dy, ((1,), (0,))).astype(BF16)
    for j in range(half // rows):
        store((same_ref, other_ref), v, slice(j * rows, (j + 1) * rows), padded, j * padded)


def down_product(side, p, dy, after):
    rows, width = dy[0].shape
    high = width // 2 // rows * ((p[0].shape[0] - width) // 16)
    kernel = functools.partial(down_product_kernel, side)
    return call(kernel, "down_product", (*p, *dy), after, outs=[((4, high, rows), BF16)] * 2)


def pair_product_kernel(lo, hi, width, p0, p1, f0, f1, *rest):
    q, out = rest[:-2], rest[-2:]
    rows = p0.shape[1]
    base = p0.shape[0] - width
    half, own = width // 2, width // 32
    left = jnp.concatenate([p[base + k * half : base + (k + 1) * half, :] for p in (p0, p1) for k in range(2)], axis=1)
    for t in range(lo, hi, 2):
        n = min(2, hi - t)
        right = [
            jnp.concatenate([f[(t + k) * 2 * rows : (t + k + 1) * 2 * rows, :] for f in (f0, f1)], axis=0)
            for k in range(n)
        ]
        v = dot(left, jnp.concatenate(right, axis=1), ((1,), (0,))).astype(BF16)
        for k in range(n):
            store(out, v, slice(k * rows, (k + 1) * rows), 2 * own, (t + k - lo) * 2 * own)
    if q:
        high = q[0].shape[0] // 8
        to = (hi - lo) * 2 * own
        for k in range(8):
            v = q[0][k * high : (k + 1) * high, :].astype(F32) + q[1][k * high : (k + 1) * high, :].astype(F32)
            out[k // 4][k % 4, to : to + high, :] = v.astype(BF16)


def pair_product(lo, hi, width, p, f, q, after):
    rows = p[0].shape[1]
    high = (hi - lo) * 2 * (width // 32) + (q[0].shape[0] // 8 if q else 0)
    kernel = functools.partial(pair_product_kernel, lo, hi, width)
    return call(kernel, "pair_product", (*p, *f, *q), after, outs=[((4, high, rows), BF16)] * 2)


def combine_kernel(at_ref, a_ref, got_a_ref, b_ref, got_b_ref, *outs):
    high = a_ref.shape[1]
    for k, out_ref in enumerate(outs):
        z = jnp.bitwise_xor(at_ref[3], k)
        out_ref[:high, :] = (a_ref[z].astype(F32) + got_a_ref[z].astype(F32)).astype(BF16)
        out_ref[high:, :] = (b_ref[z].astype(F32) + got_b_ref[z].astype(F32)).astype(BF16)


def combine(at, a, got_a, b, got_b, after):
    _, high, rows = a.shape
    outs = [((2 * high, rows), BF16)] * 4
    return call(combine_kernel, "combine", (at, a, got_a, b, got_b), after, smem=1, outs=outs)


def add_lines(refs, sum_ref):
    total = refs[0][...].astype(F32)
    for ref in refs[1:]:
        total += ref[...].astype(F32)
    sum_ref[...] = total


def unpack_down_kernel(i0, i1, i2, i3, down_ref, sum_ref):
    add_lines((i0, i1, i2, i3), sum_ref)
    rows, (chunk, width) = i0.shape[1], down_ref.shape
    count = width // rows
    padded = i0.shape[0] // count
    for j in range(count):
        down_ref[:, j * rows : (j + 1) * rows] = sum_ref[j * padded : j * padded + chunk, :]


def unpack_down(v, chunk, width, after):
    scratch = [pltpu.VMEM(v[0].shape, F32)]
    return call(unpack_down_kernel, "unpack_down", v, after, outs=[((chunk, width), F32)], scratch=scratch)[0]


def unpack_kernel(at_ref, i0, i1, i2, i3, mine_ref, theirs_ref, *rest):
    out_ref, sum_ref = rest[:-1], rest[-1]
    add_lines((i0, i1, i2, i3), sum_ref)
    _, own, wide = mine_ref.shape
    high, rows = i0.shape[0] // 2, i0.shape[1]
    dp = at_ref[0]
    for part in range(2):
        for t in range(wide // rows):
            at = part * high + t * 2 * own
            lanes = slice(t * rows, (t + 1) * rows)
            mine_ref[part, :, lanes] = sum_ref[pl.ds(pl.multiple_of(at + dp * own, own), own), :]
            theirs = sum_ref[pl.ds(pl.multiple_of(at + (1 - dp) * own, own), own), :]
            theirs_ref[part, :, lanes] = theirs.astype(BF16)
        if out_ref:
            count = (high - wide // rows * 2 * own) // own
            for j in range(count):
                at = part * high + wide // rows * 2 * own + j * own
                out_ref[0][:, (part * count + j) * rows : (part * count + j + 1) * rows] = sum_ref[at : at + own, :]


def unpack(at, v, own, wide, width, after):
    outs = [((2, own, wide), F32), ((2, own, wide), BF16)] + ([((own, width), F32)] if width else [])
    scratch = [pltpu.VMEM(v[0].shape, F32)]
    return call(unpack_kernel, "unpack", (at, *v), after, smem=1, outs=outs, scratch=scratch)


def finish_kernel(at_ref, m0, m1, o0, o1, wg_ref, wu_ref, gate_ref, up_ref, dots_ref):
    dp = at_ref[0]
    share = gate_ref.shape[1] // 2
    early = m0.shape[2]
    for part, ref in enumerate((gate_ref, up_ref)):

        def put(at, a, b):
            ref[:, at : at + early] = a[part].astype(F32)
            ref[:, at + early : at + share] = b[part].astype(F32)

        @pl.when(dp == 0)
        def _():
            put(0, m0, m1)
            put(share, o0, o1)

        @pl.when(dp == 1)
        def _():
            put(0, o0, o1)
            put(share, m0, m1)

    total = gate_ref[...] * wg_ref[...].astype(F32) + up_ref[...] * wu_ref[...].astype(F32)
    dots_ref[...] = jnp.sum(total, axis=1, keepdims=True)


def finish(at, place, mine, theirs, wg, wu):
    own, ff = mine[0].shape[1], wg.shape[1]

    def whole(*shape):
        return pl.BlockSpec(shape, lambda g, at: (0,) * len(shape))

    weight = pl.BlockSpec((own, ff), lambda g, at: (at[1], 0))
    where = jnp.stack([at[0], place]).astype(jnp.int32)
    return pl.pallas_call(
        finish_kernel,
        grid_spec=pltpu.PrefetchScalarGridSpec(
            num_scalar_prefetch=1,
            grid=(1,),
            in_specs=[whole(*v.shape) for v in (*mine, *theirs)] + [weight, weight],
            out_specs=[whole(own, ff), whole(own, ff), whole(own, 1)],
        ),
        out_shape=[jax.ShapeDtypeStruct((own, ff), F32)] * 2 + [jax.ShapeDtypeStruct((own, 1), F32)],
        cost_estimate=COST,
        name="finish",
    )(where, *mine, *theirs, in_hbm(wg), in_hbm(wu))


def turn_kernel(in_ref, out_ref):
    for h in range(4):
        for z in range(4):
            out_ref[z, h] = in_ref[h, z]


def turn(v, after):
    return call(turn_kernel, "turn", (v,), after, outs=[(v.shape, BF16)])[0]


def head_product_kernel(at_ref, n0, n1, n2, n3, in_ref, mine_ref, theirs_ref, acc_ref):
    half = mine_ref.shape[0]
    left = jnp.concatenate(
        [
            jnp.concatenate([in_ref[h, jnp.bitwise_xor(at_ref[3], k)] for k in range(4)], axis=1)
            for h in range(4)
        ],
        axis=0,
    )
    right = jnp.concatenate([r[...] for r in (n0, n1, n2, n3)], axis=0)
    for at in range(0, acc_ref.shape[0], 256):
        acc_ref[at : at + 256, :] = dot(left, right[:, at : at + 256], ((1,), (0,))).T
    dp = at_ref[0]
    mine_ref[...] = acc_ref[pl.ds(pl.multiple_of(dp * half, half), half), :]
    theirs_ref[...] = acc_ref[pl.ds(pl.multiple_of((1 - dp) * half, half), half), :].astype(BF16)


def head_product(at, n, v, after):
    width, wide = n[0].shape[1], 4 * v.shape[2]
    return call(
        head_product_kernel,
        "head_product",
        (at, *n, v),
        after,
        smem=1,
        outs=[((width // 2, wide), F32), ((width // 2, wide), BF16)],
        scratch=[pltpu.VMEM((width, wide), F32)],
    )


def head_split_kernel(at_ref, mine_ref, got_ref, kx_ref, px_ref, ky_ref, py_ref, acc_ref):
    half, wide = mine_ref.shape
    own = half // 16
    x, y = at_ref[1], at_ref[2]
    acc_ref[...] = mine_ref[...] + got_ref[...].astype(F32)

    def put(ref, inner, z, xs, ys, lanes):
        to = (inner * 4 + z) * own
        at = pl.multiple_of((z * 4 + ys * 2 + xs) * own, own)
        ref[to : to + own, :] = acc_ref[pl.ds(at, own), lanes].astype(BF16)

    for inner in range(2):
        for z in range(4):
            low, high = slice(0, wide // 2), slice(wide // 2, wide)
            put(kx_ref, inner, z, x, sel(y, inner), low)
            put(px_ref, inner, z, 1 - x, sel(y, inner), low)
            put(ky_ref, inner, z, sel(x, inner), y, high)
            put(py_ref, inner, z, sel(x, inner), 1 - y, high)


def head_split(at, mine, got, after):
    half, wide = mine.shape
    outs = [((half // 2, wide // 2), BF16)] * 4
    scratch = [pltpu.VMEM((half, wide), F32)]
    return call(head_split_kernel, "head_split", (at, mine, got), after, smem=1, outs=outs, scratch=scratch)


def head_mid_kernel(kx, gx, ky, gy, same_a, other_a, same_b, other_b):
    half = kx.shape[0] // 2
    for k, g, same, other in ((kx, gx, same_a, other_a), (ky, gy, same_b, other_b)):
        v = (k[...].astype(F32) + g[...].astype(F32)).astype(BF16)
        same[...] = v[:half]
        other[...] = v[half:]


def head_mid(kx, gx, ky, gy, after):
    outs = [((kx.shape[0] // 2, kx.shape[1]), BF16)] * 4
    return call(head_mid_kernel, "head_mid", (kx, gx, ky, gy), after, outs=outs)


def head_end_kernel(a, ga, b, gb, out_ref):
    own = a.shape[0] // 4
    v = jnp.concatenate(
        [(r[...].astype(F32) + g[...].astype(F32)).astype(BF16) for r, g in ((a, ga), (b, gb))], axis=1
    )
    for z in range(4):
        out_ref[z] = v[z * own : (z + 1) * own]


def head_end(a, ga, b, gb, after):
    outs = [((4, a.shape[0] // 4, 2 * a.shape[1]), BF16)]
    return call(head_end_kernel, "head_end", (a, ga, b, gb), after, outs=outs)[0]


def latent_back_kernel(
    back_ref, dres_ref, x_ref, gain_ref, wq_ref, wk_ref, wv_ref, out_ref, left_ref, d_ref, held_ref, sems
):
    loads = [pltpu.make_async_copy(w, held_ref.at[t], sems.at[t]) for t, w in enumerate((wq_ref, wk_ref, wv_ref))]
    for load in loads:
        load.start()
    for h in range(HEADS):
        for t in range(3):
            left_ref[t, h * HEAD_DIM : (h + 1) * HEAD_DIM, :] = back_ref[h, t * HEAD_DIM : (t + 1) * HEAD_DIM, :]
    for load in loads:
        load.wait()
    for at in range(0, d_ref.shape[1], 256):
        v = dot(held_ref[0, at : at + 256, :], left_ref[0], ((1,), (0,)))
        v += dot(held_ref[1, at : at + 256, :], left_ref[1], ((1,), (0,)))
        v += dot(held_ref[2, at : at + 256, :], left_ref[2], ((1,), (0,)))
        d_ref[:, at : at + 256] = v.T
    x = x_ref[...].astype(F32)
    inv = lax.rsqrt(jnp.mean(x * x, axis=-1, keepdims=True) + EPS)
    out_ref[...] = (dres_ref[...] + norm_back(d_ref[...], x * inv, inv, gain_ref[...])).astype(BF16)


def latent_back(back, dres, x, gain, wq, wk, wv, after):
    rows, width = x.shape
    return call(
        latent_back_kernel,
        "latent_back",
        (back, dres, x, gain.reshape(1, width), wq, wk, wv),
        after,
        outs=[((rows, width), BF16)],
        scratch=[
            pltpu.VMEM((3, width, rows), BF16),
            pltpu.VMEM((rows, width), F32),
            pltpu.VMEM((3, width, width), BF16),
            pltpu.SemaphoreType.DMA((3,)),
        ],
        far=3,
    )[0]


def head_rows_kernel(at_ref, in_ref, wq_ref, wk_ref, wv_ref, q_ref, k_ref, v_ref, dots_ref):
    total = None
    for t, (w_ref, o_ref) in enumerate(((wq_ref, q_ref), (wk_ref, k_ref), (wv_ref, v_ref))):
        for h in range(0, HEADS, 2):
            lanes = [((h + n) % 4 * 3 + t) * HEAD_DIM for n in range(2)]
            pair = [in_ref[h // 4][:, at : at + HEAD_DIM] for at in lanes]
            o_ref[:, h * HEAD_DIM : (h + 2) * HEAD_DIM] = jnp.concatenate(pair, axis=1).astype(F32)
        v = jnp.sum(o_ref[...] * w_ref[...].astype(F32), axis=1, keepdims=True)
        total = v if total is None else total + v
    dots_ref[...] = total


def head_rows(place, v, wq, wk, wv):
    own, width = v.shape[1], wq.shape[1]
    weight = pl.BlockSpec((own, width), lambda g, at: (at[0], 0))
    out = pl.BlockSpec((own, width), lambda g, at: (0, 0))
    return pl.pallas_call(
        head_rows_kernel,
        grid_spec=pltpu.PrefetchScalarGridSpec(
            num_scalar_prefetch=1,
            grid=(1,),
            in_specs=[pl.BlockSpec(v.shape, lambda g, at: (0, 0, 0)), weight, weight, weight],
            out_specs=[out, out, out, pl.BlockSpec((own, 1), lambda g, at: (0, 0))],
        ),
        out_shape=[jax.ShapeDtypeStruct((own, width), F32)] * 3 + [jax.ShapeDtypeStruct((own, 1), F32)],
        cost_estimate=COST,
        name="head_rows",
    )(place, v, in_hbm(wq), in_hbm(wk), in_hbm(wv))


X_PAIRS = [(i, i ^ 1) for i in range(16)]
Y_PAIRS = [(i, i ^ 2) for i in range(16)]


def swap(v):
    return lax.ppermute(v, "dp", [(0, 1), (1, 0)])


def over_x(v):
    return lax.ppermute(v, "ctx", X_PAIRS)


def over_y(v):
    return lax.ppermute(v, "ctx", Y_PAIRS)


def over_z(v, k):
    return lax.ppermute(v, "ctx", [(i, i ^ (4 * k)) for i in range(16)])


Z_LINES = [[i + 4 * z for z in range(4)] for i in range(4)]
PLANES = [[i + 4 * z for i in range(4)] for z in range(4)]


def in_group(v, groups):
    return lax.all_to_all(v, "ctx", 0, 0, tiled=True, axis_index_groups=groups)


def sum_z(v):
    return (v[0], *(over_z(v[k], k) for k in range(1, 4)))


def to_ctx(v):
    return lax.all_to_all(v, "ctx", 0, 0, tiled=True)


def per_device_grid(
    latent_in,
    gain_attn,
    w_query,
    w_key,
    w_value,
    w_out,
    gain_ffn,
    w_gate,
    w_up,
    w_down,
    cotangent,
    seq_lengths,
    span_order,
):
    rows, width = latent_in.shape
    ff = w_gate.shape[1]
    half, own = width // 2, width // 32
    dp, ctx = lax.axis_index("dp"), lax.axis_index("ctx")
    at = jnp.stack([dp, ctx % 2, (ctx // 2) % 2, ctx // 4]).astype(jnp.int32)
    scalars = positions(seq_lengths, span_order, rows, ctx * 0)

    dy_mate = swap(cotangent)
    dy_x = over_x(jnp.concatenate([cotangent[:, :half], dy_mate[:, :half]], axis=0))
    dy_y = over_y(jnp.concatenate([cotangent[:, half:], dy_mate[:, half:]], axis=0))

    normed, qkv = norm_qkv(latent_in, gain_attn, w_query, w_key, w_value)
    qkv = to_ctx(qkv)

    out, full, top, inv = attn_fwd(1, scalars, qkv, (dy_x, dy_y))
    attn_t = to_ctx(out).reshape(width, rows)
    line = (normed, *(over_z(normed, k) for k in range(1, 4)))
    resid, normed_two, attn_send = out_norm(at, attn_t, latent_in, gain_ffn, w_out, ())
    normed_mate = swap(normed_two)
    attn_mate = swap(attn_send)

    hid, d_own, d_mate, send_x, send_y, left_sx, left_sy, left_x, left_y = ffn(
        at, normed_two, normed_mate, cotangent, dy_mate, w_gate, w_up, w_down
    )
    d_got = swap(d_mate)
    left_gx, left_gy = over_x(left_sx), over_y(left_sy)
    f_x, f_y = over_x(send_x), over_y(send_y)
    dres, dres_low, grad_attn = ffn_back(d_own, d_got, resid, gain_ffn, cotangent, w_out, line[1:])
    grad_attn = to_ctx(grad_attn.reshape(HEADS, HEAD_DIM, rows))
    y_own, y_mate = ffn_out(at, hid, w_down, (dres_low,))
    latents = (resid + y_own + swap(y_mate).astype(F32)).astype(BF16)
    out_x, out_sx, out_y, out_sy = out_product(at, attn_t, attn_mate, dres_low, swap(dres_low), (y_own,))
    out_gx, out_gy = over_x(out_sx), over_y(out_sy)

    same_a, other_a = down_product(0, (left_x, left_gx), (cotangent, dy_mate, dy_x), (out_x,))
    same_b, other_b = down_product(1, (left_y, left_gy), (cotangent, dy_mate, dy_y), (same_a,))
    sent_a, sent_b = over_y(other_a), over_x(other_b)

    grad_qkv = attn_bwd(
        1, lambda slot: (slot & 3) * 4 + (slot >> 2), scalars, qkv, grad_attn, full, top, inv, (same_b,)
    )
    four = in_group(grad_qkv, PLANES).reshape(4, 4, 3 * HEAD_DIM, rows)

    tiles = send_x.shape[0] // (2 * rows)
    split = (tiles + 1) // 2
    early_a, other_a = pair_product(0, split, width, (left_x, left_gx), (send_x, f_x), (), (grad_qkv,))
    early_b, other_b = pair_product(0, split, width, (left_y, left_gy), (send_y, f_y), (), (early_a,))
    early_sa, early_sb = over_y(other_a), over_x(other_b)
    down = combine(at, same_a, sent_a, same_b, sent_b, (early_b,))

    back = in_group(turn(four, (down[0],)), Z_LINES).reshape(16, 3 * HEAD_DIM, rows)
    late_a, other_a = pair_product(split, tiles, width, (left_x, left_gx), (send_x, f_x), (out_x, out_gx), (four,))
    late_b, other_b = pair_product(split, tiles, width, (left_y, left_gy), (send_y, f_y), (out_y, out_gy), (late_a,))
    late_sa, late_sb = over_y(other_a), over_x(other_b)
    head_mine, head_theirs = head_product(at, line, four, (late_b,))
    head_x, head_sx, head_y, head_sy = head_split(at, head_mine, swap(head_theirs), (late_b,))
    early = combine(at, early_a, early_sa, early_b, early_sb, (head_x,))
    head_a, other_a, head_b, other_b = head_mid(head_x, over_x(head_sx), head_y, over_y(head_sy), (early[0],))
    late = combine(at, late_a, late_sa, late_b, late_sb, (head_a,))
    heads = head_end(head_a, over_y(other_a), head_b, over_x(other_b), (late[0],))
    latent_grad = latent_back(back, dres, latent_in, gain_attn, w_query, w_key, w_value, (heads,))
    heads = in_group(heads, Z_LINES)
    place = dp * 16 + ctx
    down_sum = unpack_down(sum_z(down), ff // 32, width, (latent_grad,))
    wide = split * rows
    mine0, theirs0 = unpack(at, sum_z(early), own, wide, 0, (down_sum,))
    query_sum, key_sum, value_sum, dots = head_rows(place.reshape(1).astype(jnp.int32), heads, w_query, w_key, w_value)
    mine1, theirs1, out_sum = unpack(at, sum_z(late), own, ff // 2 - wide, width, (mine0, dots))
    gate_sum, up_sum, ffn_dots = finish(at, place, (mine0, mine1), (swap(theirs0), swap(theirs1)), w_gate, w_up)

    def own_gain(v):
        return lax.dynamic_slice_in_dim(v, place * own, own, 0)

    gain_attn_sum = dots[:, 0] / own_gain(gain_attn)
    gain_ffn_sum = ffn_dots[:, 0] / own_gain(gain_ffn)
    return (
        latents,
        latent_grad,
        gain_attn_sum,
        query_sum,
        key_sum,
        value_sum,
        out_sum,
        gain_ffn_sum,
        gate_sum,
        up_sum,
        down_sum,
    )


def solution(mesh):
    n_dp, n_ctx = mesh.shape["dp"], mesh.shape["ctx"]
    if n_dp == 2 and n_ctx == 16:
        body = per_device_grid
    else:
        body = functools.partial(per_device_any, Moves(n_dp, n_ctx))
    rows, whole, share = P(("dp", "ctx"), None), P(), P("dp", None)
    flat = P(("dp", "ctx"))
    return jax.shard_map(
        body,
        mesh=mesh,
        in_specs=(rows,) + (whole,) * 9 + (rows, share, share),
        out_specs=(rows, rows, flat, rows, rows, rows, rows, flat, rows, rows, rows),
        check_vma=False,
    )
```

```python
import functools

import jax
import jax.numpy as jnp
from jax import lax
from jax.experimental import pallas as pl
from jax.experimental.pallas import tpu as pltpu
from jax.sharding import PartitionSpec as P

HEADS = 16
HEAD_DIM = 64
EPS = 1e-06
NEG_FILL = -1e30
LOG2E = 1.4426950408889634
SCALE = HEAD_DIM**-0.5

BF16 = jnp.bfloat16
F32 = jnp.float32


def dot(a, b, dims):
    return lax.dot_general(a, b, (dims, ((), ())), preferred_element_type=F32)


def query_starts(ends_ref, pos):
    start = jnp.zeros_like(pos)
    for n in range(ends_ref.shape[0]):
        start = jnp.where(pos >= ends_ref[n], ends_ref[n], start)
    return start


def block_mask(ends_ref, i, j, blk):
    pos = lax.broadcasted_iota(jnp.int32, (1, blk), 1) + i * blk
    start = query_starts(ends_ref, pos) - j * blk
    key = lax.broadcasted_iota(jnp.int32, (blk, blk), 0)
    return (key <= pos - j * blk) & (key >= start)


def attn_fwd_kernel(rep, slot_ref, low_ref, ends_ref, part_ref, qkv_ref, out_ref, full_ref, top_ref, inv_ref, key_ref):
    slots, _, rows = qkv_ref.shape
    blk = 2 * rows
    count = slots // 2
    hd = HEAD_DIM

    def flip(s, c):
        key_ref[s] = qkv_ref[s, hd : 2 * hd, :].T
        return c

    lax.fori_loop(0, slots, flip, 0)
    if rep > 1:
        out_ref[...] = jnp.zeros_like(out_ref)
        full_ref[...] = jnp.zeros_like(full_ref)

    def query_block(i, c):
        s0, s1 = slot_ref[2 * i], slot_ref[2 * i + 1]
        q = jnp.concatenate([qkv_ref[s0, :hd, :], qkv_ref[s1, :hd, :]], axis=1)

        def key_block(j, state):
            top, mass, acc = state
            k0, k1 = slot_ref[2 * j], slot_ref[2 * j + 1]
            k = jnp.concatenate([key_ref[k0], key_ref[k1]], axis=0)
            v = jnp.concatenate([qkv_ref[k0, 2 * hd :, :], qkv_ref[k1, 2 * hd :, :]], axis=1)
            s = dot(k, q, ((1,), (0,))) * (SCALE * LOG2E)
            s = jnp.where(block_mask(ends_ref, i, j, blk), s, NEG_FILL)
            new_top = jnp.maximum(top, jnp.max(s, axis=0, keepdims=True))
            shrink = jnp.exp2(top - new_top)
            w = jnp.exp2(s - new_top)
            mass = mass * shrink + jnp.sum(w, axis=0, keepdims=True)
            acc = acc * shrink + dot(v, w.astype(BF16), ((1,), (0,)))
            return new_top, mass, acc

        init = (
            jnp.full((1, blk), NEG_FILL, F32),
            jnp.zeros((1, blk), F32),
            jnp.zeros((hd, blk), F32),
        )
        top, mass, acc = lax.fori_loop(low_ref[i], i + 1, key_block, init)
        inv = 1.0 / mass
        acc = acc * inv
        full_ref[s0] = acc[:, :rows]
        full_ref[s1] = acc[:, rows:]
        low = acc.astype(BF16)
        out_ref[s0] = low[:, :rows]
        out_ref[s1] = low[:, rows:]
        top_ref[i] = top
        inv_ref[i] = inv
        return c

    lax.fori_loop(0, count // rep, lambda n, c: query_block(n * rep + part_ref[0], c), 0)


def attn_bwd_kernel(
    rep, place, slot_ref, low_ref, ends_ref, part_ref, qkv_ref, da_ref, full_ref, top_ref, inv_ref,
    out_ref, key_ref, value_ref, dk_ref, dv_ref,
):
    slots, _, rows = qkv_ref.shape
    blk = 2 * rows
    count = slots // 2
    hd = HEAD_DIM

    def flip(s, c):
        key_ref[s] = qkv_ref[s, hd : 2 * hd, :].T
        value_ref[s] = qkv_ref[s, 2 * hd :, :].T
        return c

    lax.fori_loop(0, slots, flip, 0)
    dk_ref[...] = jnp.zeros_like(dk_ref)
    dv_ref[...] = jnp.zeros_like(dv_ref)
    if rep > 1:
        out_ref[...] = jnp.zeros_like(out_ref)

    def pair(ref, a, b, lo, hi):
        return jnp.concatenate([ref[a, lo:hi, :], ref[b, lo:hi, :]], axis=1)

    def query_block(i, c):
        s0, s1 = slot_ref[2 * i], slot_ref[2 * i + 1]
        q = pair(qkv_ref, s0, s1, 0, hd)
        da = pair(da_ref, s0, s1, 0, hd)
        full = pair(full_ref, s0, s1, 0, hd)
        delta = jnp.sum(da.astype(F32) * full, axis=0, keepdims=True)
        top, inv = top_ref[i], inv_ref[i]

        def key_block(j, dq):
            k0, k1 = slot_ref[2 * j], slot_ref[2 * j + 1]
            k = jnp.concatenate([key_ref[k0], key_ref[k1]], axis=0)
            v = jnp.concatenate([value_ref[k0], value_ref[k1]], axis=0)
            s = dot(k, q, ((1,), (0,))) * (SCALE * LOG2E)
            s = jnp.where(block_mask(ends_ref, i, j, blk), s, NEG_FILL)
            p = jnp.exp2(s - top) * inv
            dp = dot(v, da, ((1,), (0,)))
            ds = (p * (dp - delta)).astype(BF16)
            dk_ref[j] += dot(q, ds, ((1,), (1,)))
            dv_ref[j] += dot(da, p.astype(BF16), ((1,), (1,)))
            return dq + dot(pair(qkv_ref, k0, k1, hd, 2 * hd), ds, ((1,), (0,)))

        dq = lax.fori_loop(low_ref[i], i + 1, key_block, jnp.zeros((hd, blk), F32))
        dq = (dq * SCALE).astype(BF16)
        out_ref[place(s0), :hd, :] = dq[:, :rows]
        out_ref[place(s1), :hd, :] = dq[:, rows:]
        return c

    lax.fori_loop(0, count // rep, lambda n, c: query_block(n * rep + part_ref[0], c), 0)

    def finish(j, c):
        k0, k1 = place(slot_ref[2 * j]), place(slot_ref[2 * j + 1])
        dk = (dk_ref[j] * SCALE).astype(BF16)
        dv = dv_ref[j].astype(BF16)
        out_ref[k0, hd : 2 * hd, :] = dk[:, :rows]
        out_ref[k1, hd : 2 * hd, :] = dk[:, rows:]
        out_ref[k0, 2 * hd :, :] = dv[:, :rows]
        out_ref[k1, 2 * hd :, :] = dv[:, rows:]
        return c

    lax.fori_loop(0, count, finish, 0)


def in_hbm(v):
    return pltpu.with_memory_space_constraint(v, pltpu.HBM)


def call(kernel, name, args, after=(), smem=0, outs=(), scratch=(), vmem=24, far=0):
    held = len(args)

    def body(*refs):
        return kernel(*refs[:held], *refs[held + len(after) :])

    if far:
        args = (*args[: held - far], *(in_hbm(v) for v in args[held - far :]))
    return pl.pallas_call(
        body,
        in_specs=[SMEM] * smem + [VMEM] * (held - smem - far) + [HBM] * far + [ANY] * len(after),
        out_specs=[VMEM] * len(outs),
        out_shape=[jax.ShapeDtypeStruct(*o) for o in outs],
        scratch_shapes=list(scratch),
        cost_estimate=COST,
        compiler_params=pltpu.CompilerParams(vmem_limit_bytes=vmem * 2**20),
        name=name,
    )(*args, *after)


def order(v, after):
    return pl.pallas_call(
        lambda *refs: None,
        in_specs=[ANY] * (1 + len(after)),
        out_specs=ANY,
        out_shape=jax.ShapeDtypeStruct(v.shape, v.dtype),
        input_output_aliases={0: 0},
        cost_estimate=COST,
        name="order",
    )(v, *after)


COST = pl.CostEstimate(flops=10**6, bytes_accessed=10**5, transcendentals=0)
SMEM = pl.BlockSpec(memory_space=pltpu.SMEM)
ANY = pl.BlockSpec(memory_space=pl.ANY)
HBM = pl.BlockSpec(memory_space=pltpu.HBM)
VMEM = pl.BlockSpec(memory_space=pltpu.VMEM)


def attn_fwd(rep, scalars, qkv, after=()):
    slots, _, rows = qkv.shape
    stat = ((slots // 2, 1, 2 * rows), F32)
    return call(
        functools.partial(attn_fwd_kernel, rep),
        "attn_fwd",
        (*scalars, qkv),
        after,
        smem=4,
        outs=[((slots, HEAD_DIM, rows), BF16), ((slots, HEAD_DIM, rows), F32), stat, stat],
        scratch=[pltpu.VMEM((slots, rows, HEAD_DIM), BF16)],
        vmem=24,
    )


def attn_bwd(rep, place, scalars, qkv, da, full, top, inv, after=()):
    slots, _, rows = qkv.shape
    return call(
        functools.partial(attn_bwd_kernel, rep, place),
        "attn_bwd",
        (*scalars, qkv, da, full, top, inv),
        after,
        smem=4,
        outs=[((slots, 3 * HEAD_DIM, rows), BF16)],
        scratch=[
            pltpu.VMEM((slots, rows, HEAD_DIM), BF16),
            pltpu.VMEM((slots, rows, HEAD_DIM), BF16),
            pltpu.VMEM((slots // 2, HEAD_DIM, 2 * rows), F32),
            pltpu.VMEM((slots // 2, HEAD_DIM, 2 * rows), F32),
        ],
        vmem=24,
    )[0]


def positions(seq_lengths, span_order, rows, part):
    ends = jnp.cumsum(seq_lengths[0]).astype(jnp.int32)
    count = span_order.shape[1]
    blocks = jnp.arange(count, dtype=jnp.int32)
    slot_of = jnp.sum(jnp.where(span_order[0][None, :] == blocks[:, None], blocks[None, :], 0), axis=1)
    starts = jnp.arange(count // 2, dtype=jnp.int32) * (2 * rows)
    low = jnp.max(jnp.where(starts[:, None] >= ends[None, :], ends[None, :], 0), axis=1) // (2 * rows)
    return slot_of.astype(jnp.int32), low.astype(jnp.int32), ends, part.reshape(1).astype(jnp.int32)


def norm_back(grad_normed, unit_rows, inv_rows, gain_vec):
    scaled = grad_normed * gain_vec
    return inv_rows * (scaled - unit_rows * jnp.mean(scaled * unit_rows, axis=-1, keepdims=True))


class Moves:
    def __init__(self, n_dp, n_ctx):
        self.n_dp, self.n_ctx = n_dp, n_ctx

    def rows_gather(self, v):
        return lax.all_gather(v, "dp", axis=0, tiled=True)

    def rows_sum(self, v):
        return lax.psum_scatter(v, "dp", scatter_dimension=0, tiled=True)

    def columns_gather(self, v):
        return lax.all_gather(v, "dp", axis=1, tiled=True)

    def to_ctx(self, v):
        return lax.all_to_all(v, "ctx", 0, 0, tiled=True)

    def sum_product(self, left, right):
        part = dot(left, right, ((1,), (0,))).astype(BF16)
        return lax.psum_scatter(part, "ctx", scatter_dimension=0, tiled=True).astype(F32)


def per_device_any(
    moves,
    latent_in,
    gain_attn,
    w_query,
    w_key,
    w_value,
    w_out,
    gain_ffn,
    w_gate,
    w_up,
    w_down,
    cotangent,
    seq_lengths,
    span_order,
):
    n_dp, n_ctx = moves.n_dp, moves.n_ctx
    rows, width = latent_in.shape
    ff = w_gate.shape[1]
    dp, ctx = lax.axis_index("dp"), lax.axis_index("ctx")
    rep = n_ctx // HEADS

    scalars = positions(seq_lengths, span_order, rows, ctx % rep)

    share = ff // n_dp
    gate_w = lax.dynamic_slice_in_dim(w_gate, dp * share, share, 1)
    up_w = lax.dynamic_slice_in_dim(w_up, dp * share, share, 1)
    down_w = lax.dynamic_slice_in_dim(w_down, dp * share, share, 0)

    latent_f = latent_in.astype(F32)
    inv_one = lax.rsqrt(jnp.mean(latent_f * latent_f, axis=-1, keepdims=True) + EPS)
    unit_one = latent_f * inv_one
    normed_one = (unit_one * gain_attn).astype(BF16)

    def project(w):
        return dot(w, normed_one, ((0,), (1,))).astype(BF16).reshape(HEADS, HEAD_DIM, rows)

    qkv = jnp.concatenate([project(w_query), project(w_key), project(w_value)], axis=1)
    qkv = moves.to_ctx(jnp.repeat(qkv, rep, axis=0) if rep > 1 else qkv)
    normed_all = lax.all_gather(normed_one, "ctx", axis=0, tiled=True)

    out, full, top, inv = attn_fwd(rep, scalars, qkv)

    def from_heads(v):
        v = moves.to_ctx(v)
        if rep > 1:
            v = jnp.sum(v.astype(F32).reshape((HEADS, rep) + v.shape[1:]), axis=1).astype(BF16)
        return v

    attn_t = from_heads(out).reshape(width, rows)
    resid = latent_f + dot(attn_t, w_out, ((0,), (0,)))
    inv_two = lax.rsqrt(jnp.mean(resid * resid, axis=-1, keepdims=True) + EPS)
    unit_two = resid * inv_two
    normed_two = (unit_two * gain_ffn).astype(BF16)

    top_all = moves.rows_gather(cotangent)
    grad_hidden = dot(top_all, down_w, ((1,), (1,)))
    normed_two_all = moves.rows_gather(normed_two)
    gate_pre = dot(normed_two_all, gate_w, ((1,), (0,)))
    up_pre = dot(normed_two_all, up_w, ((1,), (0,)))
    gate_sig = jax.nn.sigmoid(gate_pre)
    swish = gate_pre * gate_sig
    hidden = (swish * up_pre).astype(BF16)
    latents = (resid + moves.rows_sum(dot(hidden, down_w, ((1,), (0,))))).astype(BF16)
    grad_gate = (grad_hidden * up_pre * gate_sig * (1.0 + gate_pre * (1.0 - gate_sig))).astype(BF16)
    grad_up = (grad_hidden * swish).astype(BF16)
    grad_norm_two = moves.rows_sum(
        dot(grad_gate, gate_w, ((1,), (1,))) + dot(grad_up, up_w, ((1,), (1,)))
    )
    grad_resid = cotangent.astype(F32) + norm_back(grad_norm_two, unit_two, inv_two, gain_ffn)
    grad_mixed = grad_resid.astype(BF16)

    grad_attn = dot(w_out, grad_mixed, ((1,), (1,))).astype(BF16).reshape(HEADS, HEAD_DIM, rows)
    grad_attn = moves.to_ctx(jnp.repeat(grad_attn, rep, axis=0) if rep > 1 else grad_attn)
    grad_qkv = attn_bwd(rep, lambda slot: slot, scalars, qkv, grad_attn, full, top, inv)

    strip = width // n_dp
    down_sum = moves.sum_product(hidden.T, top_all)
    normed_rows = lax.dynamic_slice_in_dim(normed_two_all, dp * strip, strip, 1).T
    gate_sum = moves.sum_product(normed_rows, moves.columns_gather(grad_gate))
    up_sum = moves.sum_product(normed_rows, moves.columns_gather(grad_up))
    attn_rows = moves.rows_gather(attn_t.T)
    attn_rows = lax.dynamic_slice_in_dim(attn_rows, dp * strip, strip, 1).T
    out_sum = moves.sum_product(attn_rows, moves.rows_gather(grad_mixed))

    lanes = jnp.transpose(grad_qkv, (0, 2, 1)).reshape(n_ctx * rows, 3 * HEAD_DIM)
    head_grad = dot(normed_all, lanes, ((0,), (0,)))
    head_grad = head_grad.reshape(n_dp, strip, 3 * HEAD_DIM)
    head_grad = lax.psum_scatter(head_grad, "dp", scatter_dimension=0, tiled=False)
    own = strip // n_ctx
    head_grad = moves.to_ctx(head_grad.astype(BF16).reshape(n_ctx, own, 3 * HEAD_DIM)).astype(F32)
    head_grad = jnp.sum(head_grad.reshape(HEADS, rep, own, 3, HEAD_DIM), axis=1)
    head_grad = jnp.transpose(head_grad, (2, 1, 0, 3)).reshape(3, own, width)
    query_sum, key_sum, value_sum = head_grad[0], head_grad[1], head_grad[2]

    first_row = (dp * n_ctx + ctx) * own

    def own_rows(w):
        return lax.dynamic_slice_in_dim(w, first_row, own, 0).astype(F32)

    def own_gain(v):
        return lax.dynamic_slice_in_dim(v, first_row, own, 0)

    gain_ffn_sum = jnp.sum(own_rows(w_gate) * gate_sum + own_rows(w_up) * up_sum, axis=1) / own_gain(gain_ffn)
    gain_attn_sum = jnp.sum(
        own_rows(w_query) * query_sum + own_rows(w_key) * key_sum + own_rows(w_value) * value_sum, axis=1
    ) / own_gain(gain_attn)

    back = from_heads(grad_qkv).reshape(HEADS, 3, HEAD_DIM, rows)
    grad_norm_one = sum(
        dot(back[:, n].reshape(width, rows), w, ((0,), (1,)))
        for n, w in enumerate((w_query, w_key, w_value))
    )
    latent_grad = (grad_resid + norm_back(grad_norm_one, unit_one, inv_one, gain_attn)).astype(BF16)
    return (
        latents,
        latent_grad,
        gain_attn_sum,
        query_sum,
        key_sum,
        value_sum,
        out_sum,
        gain_ffn_sum,
        gate_sum,
        up_sum,
        down_sum,
    )


def low_t(v):
    return v.astype(F32).T.astype(BF16)


def sel(at, other):
    return 1 - at if other else at


def norm_qkv_kernel(x_ref, gain_ref, wq_ref, wk_ref, wv_ref, n_ref, qkv_ref, held_ref, sems):
    loads = [pltpu.make_async_copy(w, held_ref.at[t], sems.at[t]) for t, w in enumerate((wq_ref, wk_ref, wv_ref))]
    for load in loads:
        load.start()
    x = x_ref[...].astype(F32)
    inv = lax.rsqrt(jnp.mean(x * x, axis=-1, keepdims=True) + EPS)
    n = (x * inv * gain_ref[...]).astype(BF16)
    n_ref[...] = n
    cols = 256
    for t, load in enumerate(loads):
        load.wait()
        for c in range(0, held_ref.shape[2], cols):
            p = dot(n, held_ref[t, :, c : c + cols], ((1,), (0,))).T.astype(BF16)
            for h in range(cols // HEAD_DIM):
                qkv_ref[c // HEAD_DIM + h, t * HEAD_DIM : (t + 1) * HEAD_DIM, :] = p[h * HEAD_DIM : (h + 1) * HEAD_DIM]


def norm_qkv(x, gain, wq, wk, wv):
    rows, width = x.shape
    return call(
        norm_qkv_kernel,
        "norm_qkv",
        (x, gain.reshape(1, width), wq, wk, wv),
        outs=[
            ((rows, width), BF16),
            ((HEADS, 3 * HEAD_DIM, rows), BF16),
        ],
        scratch=[pltpu.VMEM((3, width, width), BF16), pltpu.SemaphoreType.DMA((3,))],
        far=3,
    )


def out_norm_kernel(at_ref, ab_ref, x_ref, gain_ref, w_ref, resid_ref, n_ref, send_ref, held_ref, sem):
    load = pltpu.make_async_copy(w_ref, held_ref, sem)
    load.start()
    left = low_t(ab_ref[...])
    half = send_ref.shape[0]
    send_ref[...] = ab_ref[pl.ds(pl.multiple_of((1 - at_ref[0]) * half, half), half), :]
    load.wait()
    cols = 256
    mixed = [dot(left, held_ref[:, c : c + cols], ((1,), (0,))) for c in range(0, held_ref.shape[1], cols)]
    resid = x_ref[...].astype(F32) + jnp.concatenate(mixed, axis=1)
    resid_ref[...] = resid
    inv = lax.rsqrt(jnp.mean(resid * resid, axis=-1, keepdims=True) + EPS)
    n_ref[...] = (resid * inv * gain_ref[...]).astype(BF16)


def out_norm(at, ab, x, gain, w):
    rows, width = x.shape
    return call(
        out_norm_kernel,
        "out_norm",
        (at, ab, x, gain.reshape(1, width), w),
        smem=1,
        outs=[((rows, width), F32), ((rows, width), BF16), ((width // 2, rows), BF16)],
        scratch=[pltpu.VMEM(w.shape, BF16), pltpu.SemaphoreType.DMA],
        far=1,
    )


def ffn_kernel(
    at_ref, n0_ref, n1_ref, dy0_ref, dy1_ref, wg_ref, wu_ref, wd_ref,
    hid_ref, d0_ref, d1_ref, px_ref, py_ref, tx_ref, ty_ref, kx_ref, ky_ref,
    n_ref, dy_ref, dg_ref, du_ref, hid_t_ref, n_t_ref, g_w, u_w, d_w, sems,
):
    rows, width = n0_ref.shape
    share = g_w.shape[1]
    high = kx_ref.shape[0]
    first = pl.multiple_of(at_ref[0] * share, 128)
    parts = ((0, 768), (768, share))
    loads = []
    for n, (lo, hi) in enumerate(parts):
        cols = pl.ds(pl.multiple_of(first + lo, 128), hi - lo)
        loads.append(
            (
                pltpu.make_async_copy(wg_ref.at[:, cols], g_w.at[:, pl.ds(lo, hi - lo)], sems.at[n, 0]),
                pltpu.make_async_copy(wu_ref.at[:, cols], u_w.at[:, pl.ds(lo, hi - lo)], sems.at[n, 1]),
                pltpu.make_async_copy(wd_ref.at[cols, :], d_w.at[pl.ds(lo, hi - lo), :], sems.at[n, 2]),
            )
        )
        for load in loads[n]:
            load.start()
    n_ref[:rows] = n0_ref[...]
    n_ref[rows:] = n1_ref[...]
    dy_ref[:rows] = dy0_ref[...]
    dy_ref[rows:] = dy1_ref[...]
    n_t_ref[...] = low_t(n_ref[...])

    for lo, hi in parts:
        for load in loads[parts.index((lo, hi))]:
            load.wait()
        for at in range(lo, hi, 256):
            lanes = slice(at, min(at + 256, share))
            g = dot(n_ref[...], g_w[:, lanes], ((1,), (0,)))
            u = dot(n_ref[...], u_w[:, lanes], ((1,), (0,)))
            dh = dot(dy_ref[...], d_w[lanes, :], ((1,), (1,)))
            sig = jax.nn.sigmoid(g)
            swish = g * sig
            hid = (swish * u).astype(BF16)
            dg = (dh * u * sig * (1.0 + g * (1.0 - sig))).astype(BF16)
            du = (dh * swish).astype(BF16)
            hid_ref[:, lanes] = hid
            hid_t_ref[lanes, :] = hid.astype(F32).T
            dg_ref[:, lanes] = dg
            du_ref[:, lanes] = du
            for k in range(dg.shape[1] // rows):
                to = high + (at // rows + k) * 2 * rows
                x_ref, y_ref = px_ref, py_ref
                if to >= px_ref.shape[0]:
                    to, x_ref, y_ref = to - px_ref.shape[0], tx_ref, ty_ref
                x_ref[to : to + 2 * rows, :] = dg[:, k * rows : (k + 1) * rows]
                y_ref[to : to + 2 * rows, :] = du[:, k * rows : (k + 1) * rows]

    for at in range(0, width, 256):
        cols = slice(at, at + 256)
        d = dot(dg_ref[...], g_w[cols, :], ((1,), (1,))) + dot(du_ref[...], u_w[cols, :], ((1,), (1,)))
        d0_ref[:, cols] = d[:rows]
        d1_ref[:, cols] = d[rows:].astype(BF16)

    own = width // 32
    chunk = share // 16
    base = high - width
    padded = base // 16
    x, y = at_ref[1], at_ref[2]
    fill = jnp.zeros((padded - chunk, rows), F32)

    def put(ref, inner, z, xs, ys):
        c = z * 4 + ys * 2 + xs
        for half in range(2):
            lanes = slice(half * rows, (half + 1) * rows)
            v = hid_t_ref[pl.ds(pl.multiple_of(c * chunk, 8), chunk), lanes]
            to = ((inner * 4 + z) * 2 + half) * padded
            ref[to : to + padded, :] = jnp.concatenate([v, fill], axis=0).astype(BF16)
            for d in range(2):
                to = base + half * (width // 2) + ((inner * 4 + z) * 2 + d) * own
                at = pl.multiple_of(d * (width // 2) + c * own, own)
                ref[to : to + own, :] = n_t_ref[pl.ds(at, own), lanes]

    for inner in range(2):
        for z in range(4):
            put(kx_ref, inner, z, x, sel(y, inner))
            put(px_ref, inner, z, 1 - x, sel(y, inner))
            put(ky_ref, inner, z, sel(x, inner), y)
            put(py_ref, inner, z, sel(x, inner), 1 - y)


def ffn(at, n0, n1, dy0, dy1, wg, wu, wd, after):
    rows, width = n0.shape
    share = wg.shape[1] // 2
    padded = -(-(share // 16) // 16) * 16
    high = 16 * padded + width
    early = EARLY * 2 * rows
    sizes = [high + early] * 2 + [2 * share - early] * 2 + [high] * 2
    return call(
        ffn_kernel,
        "ffn",
        (at, n0, n1, dy0, dy1, wg, wu, wd),
        after,
        smem=1,
        outs=[((2 * rows, share), BF16), ((rows, width), F32), ((rows, width), BF16)]
        + [((n, rows), BF16) for n in sizes],
        scratch=[
            pltpu.VMEM((2 * rows, width), BF16),
            pltpu.VMEM((2 * rows, width), BF16),
            pltpu.VMEM((2 * rows, share), BF16),
            pltpu.VMEM((2 * rows, share), BF16),
            pltpu.VMEM((share, 2 * rows), F32),
            pltpu.VMEM((width, 2 * rows), BF16),
            pltpu.VMEM((width, share), BF16),
            pltpu.VMEM((width, share), BF16),
            pltpu.VMEM((share, width), BF16),
            pltpu.SemaphoreType.DMA((2, 3)),
        ],
        vmem=40,
        far=3,
    )


def ffn_out_kernel(at_ref, hid_ref, w_ref, y0_ref, y1_ref, held_ref, sem):
    rows, width = y0_ref.shape
    share = held_ref.shape[0]
    first = pl.multiple_of(at_ref[0] * share, 128)
    load = pltpu.make_async_copy(w_ref.at[pl.ds(first, share), :], held_ref, sem)
    load.start()
    load.wait()
    for at in range(0, width, 256):
        cols = slice(at, at + 256)
        y = dot(hid_ref[...], held_ref[:, cols], ((1,), (0,)))
        y0_ref[:, cols] = y[:rows]
        y1_ref[:, cols] = y[rows:].astype(BF16)


def ffn_out(at, hid, w, after):
    shape = (hid.shape[0] // 2, w.shape[1])
    return call(
        ffn_out_kernel,
        "ffn_out",
        (at, hid, w),
        after,
        smem=1,
        outs=[(shape, F32), (shape, BF16)],
        scratch=[pltpu.VMEM((hid.shape[1], w.shape[1]), BF16), pltpu.SemaphoreType.DMA],
        far=1,
    )


def ffn_back_kernel(d_ref, got_ref, resid_ref, gain_ref, dy_ref, w_ref, dres_ref, low_ref, da_ref, held_ref, sem):
    load = pltpu.make_async_copy(w_ref, held_ref, sem)
    load.start()
    d = d_ref[...] + got_ref[...].astype(F32)
    resid = resid_ref[...]
    inv = lax.rsqrt(jnp.mean(resid * resid, axis=-1, keepdims=True) + EPS)
    dres = dy_ref[...].astype(F32) + norm_back(d, resid * inv, inv, gain_ref[...])
    dres_ref[...] = dres
    low = dres.astype(BF16)
    low_ref[...] = low
    load.wait()
    for at in range(0, held_ref.shape[0], 256):
        da_ref[at : at + 256, :] = dot(held_ref[at : at + 256, :], low, ((1,), (1,))).astype(BF16)


def ffn_back(d, got, resid, gain, dy, w, after):
    rows, width = d.shape
    return call(
        ffn_back_kernel,
        "ffn_back",
        (d, got, resid, gain.reshape(1, width), dy, w),
        after,
        outs=[((rows, width), F32), ((rows, width), BF16), ((width, rows), BF16)],
        scratch=[pltpu.VMEM(w.shape, BF16), pltpu.SemaphoreType.DMA],
        far=1,
    )


EARLY = 4


def out_product_kernel(at_ref, ab_ref, got_ref, low0_ref, low1_ref, kx_ref, px_ref, ky_ref, py_ref, acc_ref):
    half, rows = got_ref.shape
    own = half // 16
    x, y = at_ref[1], at_ref[2]
    mine = ab_ref[pl.ds(pl.multiple_of(at_ref[0] * half, half), half), :]
    left = jnp.concatenate([mine, got_ref[...]], axis=1)
    right = jnp.concatenate([low0_ref[...], low1_ref[...]], axis=0)
    for at in range(0, acc_ref.shape[1], 256):
        acc_ref[:, at : at + 256] = dot(left, right[:, at : at + 256], ((1,), (0,)))
    tiles = acc_ref.shape[1] // 2 // rows

    def put(ref, inner, z, xs, ys, side):
        at = pl.multiple_of((z * 4 + ys * 2 + xs) * own, own)
        for j in range(tiles):
            lanes = slice((side * tiles + j) * rows, (side * tiles + j + 1) * rows)
            to = ((inner * 4 + z) * tiles + j) * own
            ref[to : to + own, :] = acc_ref[pl.ds(at, own), lanes].astype(BF16)

    for inner in range(2):
        for z in range(4):
            put(kx_ref, inner, z, x, sel(y, inner), 0)
            put(px_ref, inner, z, 1 - x, sel(y, inner), 0)
            put(ky_ref, inner, z, sel(x, inner), y, 1)
            put(py_ref, inner, z, sel(x, inner), 1 - y, 1)


def out_product(at, ab, got, low, low_mate, after):
    half, rows = got.shape
    high = half // 2 * (low.shape[1] // 2) // rows
    return call(
        out_product_kernel,
        "out_product",
        (at, ab, got, low, low_mate),
        after,
        smem=1,
        outs=[((high, rows), BF16)] * 4,
        scratch=[pltpu.VMEM((half, low.shape[1]), F32)],
    )


def store(refs, v, lanes, high, to):
    for inner in range(2):
        for z in range(4):
            at = (inner * 4 + z) * high
            refs[inner][z, to : to + high, :] = v[at : at + high, lanes]


def pair_tiles(out, left, f0, f1, start, count, base, own):
    rows = f0.shape[1]
    for t in range(0, count, 2):
        n = min(2, count - t)
        at = [start + (t + k) * 2 * rows for k in range(n)]
        right = [jnp.concatenate([f[a : a + 2 * rows, :] for f in (f0, f1)], axis=0) for a in at]
        v = dot(left, jnp.concatenate(right, axis=1), ((1,), (0,))).astype(BF16)
        for k in range(n):
            store(out, v, slice(k * rows, (k + 1) * rows), 2 * own, base + (t + k) * 2 * own)


def left_rows(k0, p1, width):
    high, half = k0.shape[0], width // 2
    at = high - width
    return jnp.concatenate([r[at + k * half : at + (k + 1) * half, :] for r in (k0, p1) for k in range(2)], axis=1)


def first_product_kernel(side, k0, p0, p1, dy0, dy1, dy2, same_ref, other_ref):
    out = (same_ref, other_ref)
    high, rows = k0.shape
    width = dy0.shape[1]
    half, own = width // 2, width // 32
    padded = (high - width) // 16

    def lanes(ref, k):
        at = k * 2 * padded
        return jnp.concatenate([ref[at : at + padded, :], ref[at + padded : at + 2 * padded, :]], axis=1)

    hid = jnp.concatenate([jnp.concatenate([lanes(k0, k), lanes(p1, k)], axis=1) for k in range(8)], axis=0)
    cols = slice(side * half, (side + 1) * half)
    dy = jnp.concatenate([dy0[:, cols], dy1[:, cols], dy2[...]], axis=0)
    v = dot(hid, dy, ((1,), (0,))).astype(BF16)
    for j in range(half // rows):
        store(out, v, slice(j * rows, (j + 1) * rows), padded, j * padded)
    count = (p0.shape[0] - high) // (2 * rows)
    pair_tiles(out, left_rows(k0, p1, width), p0, p1, high, count, half // rows * padded, own)


def first_product(side, kept, sent, got, dy, after):
    (high, rows), width = kept.shape, dy[0].shape[1]
    tall = width // 2 // rows * (high - width) // 16 + (sent.shape[0] - high) // (2 * rows) * (width // 16)
    kernel = functools.partial(first_product_kernel, side)
    outs = [((4, tall, rows), BF16)] * 2
    return call(kernel, "first_product", (kept, sent, got, *dy), after, outs=outs)


def second_product_kernel(width, k0, p1, f0, f1, q0, q1, same_ref, other_ref):
    out = (same_ref, other_ref)
    count, own = f0.shape[0] // (2 * f0.shape[1]), width // 32
    pair_tiles(out, left_rows(k0, p1, width), f0, f1, 0, count, 0, own)
    base, tall = count * 2 * own, q0.shape[0] // 8
    for k in range(8):
        v = q0[k * tall : (k + 1) * tall, :].astype(F32) + q1[k * tall : (k + 1) * tall, :].astype(F32)
        out[k // 4][k % 4, base : base + tall, :] = v.astype(BF16)


def second_product(width, kept, got, tiles, q, after):
    rows = kept.shape[1]
    tall = tiles[0].shape[0] // (2 * rows) * (width // 16) + q[0].shape[0] // 8
    kernel = functools.partial(second_product_kernel, width)
    outs = [((4, tall, rows), BF16)] * 2
    return call(kernel, "second_product", (kept, got, *tiles, *q), after, outs=outs)


def combine_kernel(at_ref, *refs):
    parts, (own_ref, far_ref, send_ref) = refs[:-3], refs[-3:]
    high = own_ref.shape[0]
    for k, out_ref, start in ((0, own_ref, 0), (3, far_ref, 0), (1, send_ref, 0), (2, send_ref, high)):
        z = jnp.bitwise_xor(at_ref[3], k)
        to = start
        for n in range(0, len(parts), 2):
            rows = parts[n].shape[1]
            out_ref[to : to + rows, :] = (parts[n][z].astype(F32) + parts[n + 1][z].astype(F32)).astype(BF16)
            to += rows


def combine(at, parts, after):
    high, rows = sum(v.shape[1] for v in parts[::2]), parts[0].shape[2]
    outs = [((high, rows), BF16), ((high, rows), BF16), ((2 * high, rows), BF16)]
    return call(combine_kernel, "combine", (at, *parts), after, smem=1, outs=outs)


def cross_kernel(own_ref, far_ref, got_ref, sum_ref, send_ref):
    high = own_ref.shape[0]
    sum_ref[...] = (own_ref[...].astype(F32) + got_ref[:high, :].astype(F32)).astype(BF16)
    send_ref[...] = (far_ref[...].astype(F32) + got_ref[high:, :].astype(F32)).astype(BF16)


def cross(own, far, got, after):
    return call(cross_kernel, "cross", (own, far, got), after, outs=[(own.shape, BF16)] * 2)


def add_lines(refs, sum_ref):
    total = refs[0][...].astype(F32)
    for ref in refs[1:]:
        total += ref[...].astype(F32)
    sum_ref[...] = total


def unpack_kernel(at_ref, a0, a1, b0, b1, down_ref, mine_ref, theirs_ref, out_ref, a_ref, b_ref):
    add_lines((a0, a1), a_ref)
    add_lines((b0, b1), b_ref)
    rows = a0.shape[1]
    _, own, wide = mine_ref.shape
    chunk, width = down_ref.shape
    padded = -(-chunk // 16) * 16
    count = width // 2 // rows
    dp = at_ref[0]
    for part in range(2):
        base = part * (a0.shape[0] // 2)
        for j in range(count):
            lanes = slice((part * count + j) * rows, (part * count + j + 1) * rows)
            down_ref[:, lanes] = a_ref[base + j * padded : base + j * padded + chunk, :]
        for t in range(wide // rows):
            ref, at = a_ref, base + count * padded + t * 2 * own
            if t >= EARLY:
                ref, at = b_ref, part * (b0.shape[0] // 2) + (t - EARLY) * 2 * own
            lanes = slice(t * rows, (t + 1) * rows)
            mine_ref[part, :, lanes] = ref[pl.ds(pl.multiple_of(at + dp * own, own), own), :]
            theirs_ref[part, :, lanes] = ref[pl.ds(pl.multiple_of(at + (1 - dp) * own, own), own), :].astype(BF16)
        base = part * (b0.shape[0] // 2) + (wide // rows - EARLY) * 2 * own
        for j in range(count):
            lanes = slice((part * count + j) * rows, (part * count + j + 1) * rows)
            out_ref[:, lanes] = b_ref[base + j * own : base + (j + 1) * own, :]


def unpack(at, v, own, wide, chunk, width, after):
    outs = [((chunk, width), F32), ((2, own, wide), F32), ((2, own, wide), BF16), ((own, width), F32)]
    scratch = [pltpu.VMEM(v[0].shape, F32), pltpu.VMEM(v[2].shape, F32)]
    return call(unpack_kernel, "unpack", (at, *v), after, smem=1, outs=outs, scratch=scratch)


def finish_kernel(at_ref, mine, theirs, gain_ref, wg_ref, wu_ref, gate_ref, up_ref, dots_ref):
    dp = at_ref[1]
    share = gate_ref.shape[1] // 2
    for part, ref in enumerate((gate_ref, up_ref)):

        @pl.when(dp == 0)
        def _():
            ref[:, :share] = mine[part]
            ref[:, share:] = theirs[part].astype(F32)

        @pl.when(dp == 1)
        def _():
            ref[:, :share] = theirs[part].astype(F32)
            ref[:, share:] = mine[part]

    total = gate_ref[...] * wg_ref[...].astype(F32) + up_ref[...] * wu_ref[...].astype(F32)
    dots_ref[...] = by_gain(jnp.sum(total, axis=1, keepdims=True), gain_ref, at_ref[0])


def finish(where, mine, theirs, gain, wg, wu):
    own, ff = mine.shape[1], wg.shape[1]
    count = wg.shape[0] // own

    def whole(*shape):
        return pl.BlockSpec(shape, lambda g, at: (0,) * len(shape))

    weight = pl.BlockSpec((own, ff), lambda g, at: (at[0], 0))
    gate, up, dots = pl.pallas_call(
        finish_kernel,
        grid_spec=pltpu.PrefetchScalarGridSpec(
            num_scalar_prefetch=1,
            grid=(1,),
            in_specs=[whole(*mine.shape), whole(*theirs.shape), whole(count, own), weight, weight],
            out_specs=[whole(own, ff), whole(own, ff), whole(1, own)],
        ),
        out_shape=[jax.ShapeDtypeStruct((own, ff), F32)] * 2 + [jax.ShapeDtypeStruct((1, own), F32)],
        cost_estimate=COST,
        name="finish",
    )(where, mine, theirs, gain.reshape(count, own), in_hbm(wg), in_hbm(wu))
    return gate, up, dots.reshape(own)


def turn_kernel(in_ref, out_ref):
    for h in range(4):
        for z in range(4):
            out_ref[z, h] = in_ref[h, z]


def turn(v, after):
    return call(turn_kernel, "turn", (v,), after, outs=[(v.shape, BF16)])[0]


def head_product_kernel(at_ref, n0, n1, in_ref, mine_ref, theirs_ref, acc_ref):
    half = mine_ref.shape[0]
    x, y = at_ref[1], at_ref[2]
    left = jnp.concatenate(
        [
            jnp.concatenate([in_ref[h, sel(y, oy) * 2 + sel(x, ox)] for oy in range(2) for ox in range(2)], axis=1)
            for h in range(4)
        ],
        axis=0,
    )
    right = jnp.concatenate([n0[...], n1[...]], axis=0)
    for at in range(0, acc_ref.shape[0], 256):
        acc_ref[at : at + 256, :] = dot(left, right[:, at : at + 256], ((1,), (0,))).T
    dp = at_ref[0]
    mine_ref[...] = acc_ref[pl.ds(pl.multiple_of(dp * half, half), half), :]
    theirs_ref[...] = acc_ref[pl.ds(pl.multiple_of((1 - dp) * half, half), half), :].astype(BF16)


def head_product(at, n, v, after):
    width, wide = n[0].shape[1], 4 * v.shape[2]
    return call(
        head_product_kernel,
        "head_product",
        (at, *n, v),
        after,
        smem=1,
        outs=[((width // 2, wide), F32), ((width // 2, wide), BF16)],
        scratch=[pltpu.VMEM((width, wide), F32)],
    )


def head_split_kernel(at_ref, mine_ref, got_ref, own_ref, far_ref, send_ref):
    high = own_ref.shape[0]
    for k, ref, to in ((0, own_ref, 0), (3, far_ref, 0), (1, send_ref, 0), (2, send_ref, high)):
        rows = pl.ds(pl.multiple_of(jnp.bitwise_xor(at_ref[3], k) * high, high), high)
        ref[to : to + high, :] = (mine_ref[rows, :] + got_ref[rows, :].astype(F32)).astype(BF16)


def head_split(at, mine, got, after):
    half, wide = mine.shape
    outs = [((half // 4, wide), BF16), ((half // 4, wide), BF16), ((half // 2, wide), BF16)]
    return call(head_split_kernel, "head_split", (at, mine, got), after, smem=1, outs=outs)


def head_end_kernel(a, ga, out_ref):
    own = a.shape[0] // 4
    v = (a[...].astype(F32) + ga[...].astype(F32)).astype(BF16)
    for p in range(4):
        out_ref[p] = v[p * own : (p + 1) * own]


def head_end(a, ga, after):
    outs = [((4, a.shape[0] // 4, a.shape[1]), BF16)]
    return call(head_end_kernel, "head_end", (a, ga), after, outs=outs)[0]


def latent_back_kernel(
    back_ref, dres_ref, x_ref, gain_ref, wq_ref, wk_ref, wv_ref, out_ref, left_ref, d_ref, held_ref, sems
):
    loads = [pltpu.make_async_copy(w, held_ref.at[t], sems.at[t]) for t, w in enumerate((wq_ref, wk_ref, wv_ref))]
    for load in loads:
        load.start()
    for h in range(HEADS):
        for t in range(3):
            left_ref[t, h * HEAD_DIM : (h + 1) * HEAD_DIM, :] = back_ref[h % 4 * 4 + h // 4, t * HEAD_DIM : (t + 1) * HEAD_DIM, :]
    for load in loads:
        load.wait()
    for at in range(0, d_ref.shape[1], 256):
        v = dot(held_ref[0, at : at + 256, :], left_ref[0], ((1,), (0,)))
        v += dot(held_ref[1, at : at + 256, :], left_ref[1], ((1,), (0,)))
        v += dot(held_ref[2, at : at + 256, :], left_ref[2], ((1,), (0,)))
        d_ref[:, at : at + 256] = v.T
    x = x_ref[...].astype(F32)
    inv = lax.rsqrt(jnp.mean(x * x, axis=-1, keepdims=True) + EPS)
    out_ref[...] = (dres_ref[...] + norm_back(d_ref[...], x * inv, inv, gain_ref[...])).astype(BF16)


def latent_back(back, dres, x, gain, wq, wk, wv, after):
    rows, width = x.shape
    return call(
        latent_back_kernel,
        "latent_back",
        (back, dres, x, gain.reshape(1, width), wq, wk, wv),
        after,
        outs=[((rows, width), BF16)],
        scratch=[
            pltpu.VMEM((3, width, rows), BF16),
            pltpu.VMEM((rows, width), F32),
            pltpu.VMEM((3, width, width), BF16),
            pltpu.SemaphoreType.DMA((3,)),
        ],
        far=3,
    )[0]


def by_gain(sums, gain_ref, place):
    return jnp.broadcast_to(sums, (sums.shape[0], 128)).T[:1] / gain_ref[pl.ds(place, 1), :]


def head_rows_kernel(at_ref, in_ref, gain_ref, wq_ref, wk_ref, wv_ref, q_ref, k_ref, v_ref, dots_ref):
    total = None
    for t, (w_ref, o_ref) in enumerate(((wq_ref, q_ref), (wk_ref, k_ref), (wv_ref, v_ref))):
        for h in range(0, HEADS, 2):
            at = (h // 4 * 3 + t) * HEAD_DIM
            pair = [in_ref[h % 4 + n][:, at : at + HEAD_DIM] for n in range(2)]
            o_ref[:, h * HEAD_DIM : (h + 2) * HEAD_DIM] = jnp.concatenate(pair, axis=1).astype(F32)
        v = jnp.sum(o_ref[...] * w_ref[...].astype(F32), axis=1, keepdims=True)
        total = v if total is None else total + v
    dots_ref[...] = by_gain(total, gain_ref, at_ref[0])


def head_rows(where, v, gain, wq, wk, wv):
    own, width = v.shape[1], wq.shape[1]
    weight = pl.BlockSpec((own, width), lambda g, at: (at[0], 0))

    def whole(*shape):
        return pl.BlockSpec(shape, lambda g, at: (0,) * len(shape))

    out = pl.pallas_call(
        head_rows_kernel,
        grid_spec=pltpu.PrefetchScalarGridSpec(
            num_scalar_prefetch=1,
            grid=(1,),
            in_specs=[whole(*v.shape), whole(width // own, own), weight, weight, weight],
            out_specs=[whole(own, width)] * 3 + [whole(1, own)],
        ),
        out_shape=[jax.ShapeDtypeStruct((own, width), F32)] * 3 + [jax.ShapeDtypeStruct((1, own), F32)],
        cost_estimate=COST,
        name="head_rows",
    )(where, v, gain.reshape(width // own, own), in_hbm(wq), in_hbm(wk), in_hbm(wv))
    return *out[:3], out[3].reshape(own)


X_PAIRS = [(i, i ^ 1) for i in range(16)]
Y_PAIRS = [(i, i ^ 2) for i in range(16)]


def swap(v):
    return lax.ppermute(v, "dp", [(0, 1), (1, 0)])


def over_x(v):
    return lax.ppermute(v, "ctx", X_PAIRS)


def over_y(v):
    return lax.ppermute(v, "ctx", Y_PAIRS)


def over_z(v, k):
    return lax.ppermute(v, "ctx", [(i, i ^ (4 * k)) for i in range(16)])


Z_LINES = [[i + 4 * z for z in range(4)] for i in range(4)]
PLANES = [[i + 4 * z for i in range(4)] for z in range(4)]


def in_group(v, groups):
    return lax.all_to_all(v, "ctx", 0, 0, tiled=True, axis_index_groups=groups)


def to_ctx(v):
    return lax.all_to_all(v, "ctx", 0, 0, tiled=True)


def per_device_grid(
    latent_in,
    gain_attn,
    w_query,
    w_key,
    w_value,
    w_out,
    gain_ffn,
    w_gate,
    w_up,
    w_down,
    cotangent,
    seq_lengths,
    span_order,
):
    rows, width = latent_in.shape
    ff = w_gate.shape[1]
    half, own = width // 2, width // 32
    dp, ctx = lax.axis_index("dp"), lax.axis_index("ctx")
    at = jnp.stack([dp, ctx % 2, (ctx // 2) % 2, ctx // 4]).astype(jnp.int32)
    scalars = positions(seq_lengths, span_order, rows, ctx * 0)

    dy_mate = swap(cotangent)
    dy_x = over_x(jnp.concatenate([cotangent[:, :half], dy_mate[:, :half]], axis=0))
    dy_y = over_y(jnp.concatenate([cotangent[:, half:], dy_mate[:, half:]], axis=0))

    normed, qkv = norm_qkv(latent_in, gain_attn, w_query, w_key, w_value)
    qkv = to_ctx(qkv)

    line = jnp.concatenate([normed, over_x(normed)], axis=0)
    line = (line, over_y(line))
    out, full, top, inv = attn_fwd(1, scalars, qkv, (dy_x, dy_y))
    attn_t = to_ctx(out).reshape(width, rows)
    resid, normed_two, attn_send = out_norm(at, attn_t, latent_in, gain_ffn, w_out)
    normed_mate = swap(normed_two)
    attn_mate = swap(attn_send)

    hid, d_own, d_mate, send_x, send_y, tiles_x, tiles_y, kept_x, kept_y = ffn(
        at, normed_two, normed_mate, cotangent, dy_mate, w_gate, w_up, w_down, (line[1],)
    )
    d_got = swap(d_mate)
    got_x, got_y = over_x(send_x), over_y(send_y)
    tiles_x, tiles_y = (tiles_x, over_x(tiles_x)), (tiles_y, over_y(tiles_y))
    dres, dres_low, grad_attn = ffn_back(d_own, d_got, resid, gain_ffn, cotangent, w_out, ())
    grad_attn = to_ctx(grad_attn.reshape(HEADS, HEAD_DIM, rows))
    out_x, out_sx, out_y, out_sy = out_product(at, attn_t, attn_mate, dres_low, swap(dres_low), ())
    out_x, out_y = (out_x, over_x(out_sx)), (out_y, over_y(out_sy))

    dy_a, dy_b = (cotangent, dy_mate, dy_x), (cotangent, dy_mate, dy_y)
    one_a, other_a = first_product(0, kept_x, send_x, got_x, dy_a, (out_x[0],))
    one_b, other_b = first_product(1, kept_y, send_y, got_y, dy_b, (one_a,))
    one = (one_a, over_y(other_a), one_b, over_x(other_b))
    grad_qkv = attn_bwd(1, lambda slot: slot, scalars, qkv, grad_attn, full, top, inv, (one_b,))
    four = in_group(grad_qkv, Z_LINES).reshape(4, 4, 3 * HEAD_DIM, rows)
    two_a, other_a = second_product(width, kept_x, got_x, tiles_x, out_x, (grad_qkv,))
    two_b, other_b = second_product(width, kept_y, got_y, tiles_y, out_y, (two_a,))
    two = (two_a, over_y(other_a), two_b, over_x(other_b))
    one_own, one_far, one_send = combine(at, one, (two_b,))
    one_got = over_z(one_send, 1)
    y_own, y_mate = ffn_out(at, hid, w_down, (one_own,))
    latents = (resid + y_own + swap(y_mate).astype(F32)).astype(BF16)
    two_own, two_far, two_send = combine(at, two, (y_own,))
    two_got = over_z(two_send, 1)

    turned = turn(four, (two_own,))
    back = in_group(turned, PLANES).reshape(16, 3 * HEAD_DIM, rows)
    one_own, one_send = cross(one_own, one_far, one_got, (turned,))
    head_mine, head_theirs = head_product(at, line, four, (one_own,))
    head_own, head_far, head_send = head_split(at, head_mine, swap(head_theirs), ())
    head_got = over_z(head_send, 1)
    latent_grad = latent_back(back, dres, latent_in, gain_attn, w_query, w_key, w_value, (head_own,))
    two_own, two_send = cross(two_own, two_far, two_got, (latent_grad,))
    head_own, head_send = cross(head_own, head_far, head_got, (two_own,))
    heads = head_end(head_own, over_z(head_send, 3), ())
    heads = in_group(heads, PLANES)
    place = dp * 16 + ctx
    where = jnp.stack([place, dp]).astype(jnp.int32)
    query_sum, key_sum, value_sum, gain_attn_sum = head_rows(where, heads, gain_attn, w_query, w_key, w_value)
    down_sum, mine, theirs, out_sum = unpack(at, (one_own, over_z(one_send, 3), two_own, over_z(two_send, 3)), own, ff // 2, ff // 32, width, (gain_attn_sum,))
    gate_sum, up_sum, gain_ffn_sum = finish(where, mine, swap(theirs), gain_ffn, w_gate, w_up)
    return (
        latents,
        latent_grad,
        gain_attn_sum,
        query_sum,
        key_sum,
        value_sum,
        out_sum,
        gain_ffn_sum,
        gate_sum,
        up_sum,
        down_sum,
    )


def solution(mesh):
    n_dp, n_ctx = mesh.shape["dp"], mesh.shape["ctx"]
    if n_dp == 2 and n_ctx == 16:
        body = per_device_grid
    else:
        body = functools.partial(per_device_any, Moves(n_dp, n_ctx))
    rows, whole, share = P(("dp", "ctx"), None), P(), P("dp", None)
    flat = P(("dp", "ctx"))
    return jax.shard_map(
        body,
        mesh=mesh,
        in_specs=(rows,) + (whole,) * 9 + (rows, share, share),
        out_specs=(rows, rows, flat, rows, rows, rows, rows, flat, rows, rows, rows),
        check_vma=False,
    )
```

```python
import functools

import jax
import jax.numpy as jnp
from jax import lax
from jax.experimental import pallas as pl
from jax.experimental.pallas import tpu as pltpu
from jax.sharding import PartitionSpec as P

HEADS = 16
HEAD_DIM = 64
EPS = 1e-06
NEG_FILL = -1e30
LOG2E = 1.4426950408889634
SCALE = HEAD_DIM**-0.5

BF16 = jnp.bfloat16
F32 = jnp.float32


def dot(a, b, dims):
    return lax.dot_general(a, b, (dims, ((), ())), preferred_element_type=F32)


def query_starts(ends_ref, pos):
    start = jnp.zeros_like(pos)
    for n in range(ends_ref.shape[0]):
        start = jnp.where(pos >= ends_ref[n], ends_ref[n], start)
    return start


def block_mask(ends_ref, i, j, blk):
    pos = lax.broadcasted_iota(jnp.int32, (1, blk), 1) + i * blk
    start = query_starts(ends_ref, pos) - j * blk
    key = lax.broadcasted_iota(jnp.int32, (blk, blk), 0)
    return (key <= pos - j * blk) & (key >= start)


def attn_fwd_kernel(rep, slot_ref, low_ref, ends_ref, part_ref, qkv_ref, out_ref, full_ref, top_ref, inv_ref, key_ref):
    slots, _, rows = qkv_ref.shape
    blk = 2 * rows
    count = slots // 2
    hd = HEAD_DIM

    def flip(s, c):
        key_ref[s] = qkv_ref[s, hd : 2 * hd, :].T
        return c

    lax.fori_loop(0, slots, flip, 0)
    if rep > 1:
        out_ref[...] = jnp.zeros_like(out_ref)
        full_ref[...] = jnp.zeros_like(full_ref)

    def query_block(i, c):
        s0, s1 = slot_ref[2 * i], slot_ref[2 * i + 1]
        q = jnp.concatenate([qkv_ref[s0, :hd, :], qkv_ref[s1, :hd, :]], axis=1)

        def key_block(j, state):
            top, mass, acc = state
            k0, k1 = slot_ref[2 * j], slot_ref[2 * j + 1]
            k = jnp.concatenate([key_ref[k0], key_ref[k1]], axis=0)
            v = jnp.concatenate([qkv_ref[k0, 2 * hd :, :], qkv_ref[k1, 2 * hd :, :]], axis=1)
            s = dot(k, q, ((1,), (0,))) * (SCALE * LOG2E)
            s = jnp.where(block_mask(ends_ref, i, j, blk), s, NEG_FILL)
            new_top = jnp.maximum(top, jnp.max(s, axis=0, keepdims=True))
            shrink = jnp.exp2(top - new_top)
            w = jnp.exp2(s - new_top)
            mass = mass * shrink + jnp.sum(w, axis=0, keepdims=True)
            acc = acc * shrink + dot(v, w.astype(BF16), ((1,), (0,)))
            return new_top, mass, acc

        init = (
            jnp.full((1, blk), NEG_FILL, F32),
            jnp.zeros((1, blk), F32),
            jnp.zeros((hd, blk), F32),
        )
        top, mass, acc = lax.fori_loop(low_ref[i], i + 1, key_block, init)
        inv = 1.0 / mass
        acc = acc * inv
        full_ref[s0] = acc[:, :rows]
        full_ref[s1] = acc[:, rows:]
        low = acc.astype(BF16)
        out_ref[s0] = low[:, :rows]
        out_ref[s1] = low[:, rows:]
        top_ref[i] = top
        inv_ref[i] = inv
        return c

    lax.fori_loop(0, count // rep, lambda n, c: query_block(n * rep + part_ref[0], c), 0)


def attn_bwd_kernel(
    rep, place, slot_ref, low_ref, ends_ref, part_ref, qkv_ref, da_ref, full_ref, top_ref, inv_ref,
    out_ref, key_ref, value_ref, dk_ref, dv_ref,
):
    slots, _, rows = qkv_ref.shape
    blk = 2 * rows
    count = slots // 2
    hd = HEAD_DIM

    def flip(s, c):
        key_ref[s] = qkv_ref[s, hd : 2 * hd, :].T
        value_ref[s] = qkv_ref[s, 2 * hd :, :].T
        return c

    lax.fori_loop(0, slots, flip, 0)
    dk_ref[...] = jnp.zeros_like(dk_ref)
    dv_ref[...] = jnp.zeros_like(dv_ref)
    if rep > 1:
        out_ref[...] = jnp.zeros_like(out_ref)

    def pair(ref, a, b, lo, hi):
        return jnp.concatenate([ref[a, lo:hi, :], ref[b, lo:hi, :]], axis=1)

    def query_block(i, c):
        s0, s1 = slot_ref[2 * i], slot_ref[2 * i + 1]
        q = pair(qkv_ref, s0, s1, 0, hd)
        da = pair(da_ref, s0, s1, 0, hd)
        full = pair(full_ref, s0, s1, 0, hd)
        delta = jnp.sum(da.astype(F32) * full, axis=0, keepdims=True)
        top, inv = top_ref[i], inv_ref[i]

        def key_block(j, dq):
            k0, k1 = slot_ref[2 * j], slot_ref[2 * j + 1]
            k = jnp.concatenate([key_ref[k0], key_ref[k1]], axis=0)
            v = jnp.concatenate([value_ref[k0], value_ref[k1]], axis=0)
            s = dot(k, q, ((1,), (0,))) * (SCALE * LOG2E)
            s = jnp.where(block_mask(ends_ref, i, j, blk), s, NEG_FILL)
            p = jnp.exp2(s - top) * inv
            dp = dot(v, da, ((1,), (0,)))
            ds = (p * (dp - delta)).astype(BF16)
            dk_ref[j] += dot(q, ds, ((1,), (1,)))
            dv_ref[j] += dot(da, p.astype(BF16), ((1,), (1,)))
            return dq + dot(pair(qkv_ref, k0, k1, hd, 2 * hd), ds, ((1,), (0,)))

        dq = lax.fori_loop(low_ref[i], i + 1, key_block, jnp.zeros((hd, blk), F32))
        dq = (dq * SCALE).astype(BF16)
        out_ref[place(s0), :hd, :] = dq[:, :rows]
        out_ref[place(s1), :hd, :] = dq[:, rows:]
        return c

    lax.fori_loop(0, count // rep, lambda n, c: query_block(n * rep + part_ref[0], c), 0)

    def finish(j, c):
        k0, k1 = place(slot_ref[2 * j]), place(slot_ref[2 * j + 1])
        dk = (dk_ref[j] * SCALE).astype(BF16)
        dv = dv_ref[j].astype(BF16)
        out_ref[k0, hd : 2 * hd, :] = dk[:, :rows]
        out_ref[k1, hd : 2 * hd, :] = dk[:, rows:]
        out_ref[k0, 2 * hd :, :] = dv[:, :rows]
        out_ref[k1, 2 * hd :, :] = dv[:, rows:]
        return c

    lax.fori_loop(0, count, finish, 0)


def in_hbm(v):
    return pltpu.with_memory_space_constraint(v, pltpu.HBM)


def call(kernel, name, args, after=(), smem=0, outs=(), scratch=(), vmem=24, far=0):
    held = len(args)

    def body(*refs):
        return kernel(*refs[:held], *refs[held + len(after) :])

    if far:
        args = (*args[: held - far], *(in_hbm(v) for v in args[held - far :]))
    return pl.pallas_call(
        body,
        in_specs=[SMEM] * smem + [VMEM] * (held - smem - far) + [HBM] * far + [ANY] * len(after),
        out_specs=[VMEM] * len(outs),
        out_shape=[pltpu.HBM(*o[:2]) if len(o) > 2 else jax.ShapeDtypeStruct(*o) for o in outs],
        scratch_shapes=list(scratch),
        cost_estimate=COST,
        compiler_params=pltpu.CompilerParams(vmem_limit_bytes=vmem * 2**20),
        name=name,
    )(*args, *after)


def order(v, after):
    return pl.pallas_call(
        lambda *refs: None,
        in_specs=[ANY] * (1 + len(after)),
        out_specs=ANY,
        out_shape=jax.ShapeDtypeStruct(v.shape, v.dtype),
        input_output_aliases={0: 0},
        cost_estimate=COST,
        name="order",
    )(v, *after)


COST = pl.CostEstimate(flops=10**6, bytes_accessed=10**5, transcendentals=0)
SMEM = pl.BlockSpec(memory_space=pltpu.SMEM)
ANY = pl.BlockSpec(memory_space=pl.ANY)
HBM = pl.BlockSpec(memory_space=pltpu.HBM)
VMEM = pl.BlockSpec(memory_space=pltpu.VMEM)


def attn_fwd(rep, scalars, qkv, after=()):
    slots, _, rows = qkv.shape
    stat = ((slots // 2, 1, 2 * rows), F32)
    return call(
        functools.partial(attn_fwd_kernel, rep),
        "attn_fwd",
        (*scalars, qkv),
        after,
        smem=4,
        outs=[((slots, HEAD_DIM, rows), BF16), ((slots, HEAD_DIM, rows), F32), stat, stat],
        scratch=[pltpu.VMEM((slots, rows, HEAD_DIM), BF16)],
        vmem=24,
    )


def attn_bwd(rep, place, scalars, qkv, da, full, top, inv, after=()):
    slots, _, rows = qkv.shape
    return call(
        functools.partial(attn_bwd_kernel, rep, place),
        "attn_bwd",
        (*scalars, qkv, da, full, top, inv),
        after,
        smem=4,
        outs=[((slots, 3 * HEAD_DIM, rows), BF16)],
        scratch=[
            pltpu.VMEM((slots, rows, HEAD_DIM), BF16),
            pltpu.VMEM((slots, rows, HEAD_DIM), BF16),
            pltpu.VMEM((slots // 2, HEAD_DIM, 2 * rows), F32),
            pltpu.VMEM((slots // 2, HEAD_DIM, 2 * rows), F32),
        ],
        vmem=24,
    )[0]


def positions(seq_lengths, span_order, rows, part):
    ends = jnp.cumsum(seq_lengths[0]).astype(jnp.int32)
    count = span_order.shape[1]
    blocks = jnp.arange(count, dtype=jnp.int32)
    slot_of = jnp.sum(jnp.where(span_order[0][None, :] == blocks[:, None], blocks[None, :], 0), axis=1)
    starts = jnp.arange(count // 2, dtype=jnp.int32) * (2 * rows)
    low = jnp.max(jnp.where(starts[:, None] >= ends[None, :], ends[None, :], 0), axis=1) // (2 * rows)
    return slot_of.astype(jnp.int32), low.astype(jnp.int32), ends, part.reshape(1).astype(jnp.int32)


def norm_back(grad_normed, unit_rows, inv_rows, gain_vec):
    scaled = grad_normed * gain_vec
    return inv_rows * (scaled - unit_rows * jnp.mean(scaled * unit_rows, axis=-1, keepdims=True))


class Moves:
    def __init__(self, n_dp, n_ctx):
        self.n_dp, self.n_ctx = n_dp, n_ctx

    def rows_gather(self, v):
        return lax.all_gather(v, "dp", axis=0, tiled=True)

    def rows_sum(self, v):
        return lax.psum_scatter(v, "dp", scatter_dimension=0, tiled=True)

    def columns_gather(self, v):
        return lax.all_gather(v, "dp", axis=1, tiled=True)

    def to_ctx(self, v):
        return lax.all_to_all(v, "ctx", 0, 0, tiled=True)

    def sum_product(self, left, right):
        part = dot(left, right, ((1,), (0,))).astype(BF16)
        return lax.psum_scatter(part, "ctx", scatter_dimension=0, tiled=True).astype(F32)


def per_device_any(
    moves,
    latent_in,
    gain_attn,
    w_query,
    w_key,
    w_value,
    w_out,
    gain_ffn,
    w_gate,
    w_up,
    w_down,
    cotangent,
    seq_lengths,
    span_order,
):
    n_dp, n_ctx = moves.n_dp, moves.n_ctx
    rows, width = latent_in.shape
    ff = w_gate.shape[1]
    dp, ctx = lax.axis_index("dp"), lax.axis_index("ctx")
    rep = n_ctx // HEADS

    scalars = positions(seq_lengths, span_order, rows, ctx % rep)

    share = ff // n_dp
    gate_w = lax.dynamic_slice_in_dim(w_gate, dp * share, share, 1)
    up_w = lax.dynamic_slice_in_dim(w_up, dp * share, share, 1)
    down_w = lax.dynamic_slice_in_dim(w_down, dp * share, share, 0)

    latent_f = latent_in.astype(F32)
    inv_one = lax.rsqrt(jnp.mean(latent_f * latent_f, axis=-1, keepdims=True) + EPS)
    unit_one = latent_f * inv_one
    normed_one = (unit_one * gain_attn).astype(BF16)

    def project(w):
        return dot(w, normed_one, ((0,), (1,))).astype(BF16).reshape(HEADS, HEAD_DIM, rows)

    qkv = jnp.concatenate([project(w_query), project(w_key), project(w_value)], axis=1)
    qkv = moves.to_ctx(jnp.repeat(qkv, rep, axis=0) if rep > 1 else qkv)
    normed_all = lax.all_gather(normed_one, "ctx", axis=0, tiled=True)

    out, full, top, inv = attn_fwd(rep, scalars, qkv)

    def from_heads(v):
        v = moves.to_ctx(v)
        if rep > 1:
            v = jnp.sum(v.astype(F32).reshape((HEADS, rep) + v.shape[1:]), axis=1).astype(BF16)
        return v

    attn_t = from_heads(out).reshape(width, rows)
    resid = latent_f + dot(attn_t, w_out, ((0,), (0,)))
    inv_two = lax.rsqrt(jnp.mean(resid * resid, axis=-1, keepdims=True) + EPS)
    unit_two = resid * inv_two
    normed_two = (unit_two * gain_ffn).astype(BF16)

    top_all = moves.rows_gather(cotangent)
    grad_hidden = dot(top_all, down_w, ((1,), (1,)))
    normed_two_all = moves.rows_gather(normed_two)
    gate_pre = dot(normed_two_all, gate_w, ((1,), (0,)))
    up_pre = dot(normed_two_all, up_w, ((1,), (0,)))
    gate_sig = jax.nn.sigmoid(gate_pre)
    swish = gate_pre * gate_sig
    hidden = (swish * up_pre).astype(BF16)
    latents = (resid + moves.rows_sum(dot(hidden, down_w, ((1,), (0,))))).astype(BF16)
    grad_gate = (grad_hidden * up_pre * gate_sig * (1.0 + gate_pre * (1.0 - gate_sig))).astype(BF16)
    grad_up = (grad_hidden * swish).astype(BF16)
    grad_norm_two = moves.rows_sum(
        dot(grad_gate, gate_w, ((1,), (1,))) + dot(grad_up, up_w, ((1,), (1,)))
    )
    grad_resid = cotangent.astype(F32) + norm_back(grad_norm_two, unit_two, inv_two, gain_ffn)
    grad_mixed = grad_resid.astype(BF16)

    grad_attn = dot(w_out, grad_mixed, ((1,), (1,))).astype(BF16).reshape(HEADS, HEAD_DIM, rows)
    grad_attn = moves.to_ctx(jnp.repeat(grad_attn, rep, axis=0) if rep > 1 else grad_attn)
    grad_qkv = attn_bwd(rep, lambda slot: slot, scalars, qkv, grad_attn, full, top, inv)

    strip = width // n_dp
    down_sum = moves.sum_product(hidden.T, top_all)
    normed_rows = lax.dynamic_slice_in_dim(normed_two_all, dp * strip, strip, 1).T
    gate_sum = moves.sum_product(normed_rows, moves.columns_gather(grad_gate))
    up_sum = moves.sum_product(normed_rows, moves.columns_gather(grad_up))
    attn_rows = moves.rows_gather(attn_t.T)
    attn_rows = lax.dynamic_slice_in_dim(attn_rows, dp * strip, strip, 1).T
    out_sum = moves.sum_product(attn_rows, moves.rows_gather(grad_mixed))

    lanes = jnp.transpose(grad_qkv, (0, 2, 1)).reshape(n_ctx * rows, 3 * HEAD_DIM)
    head_grad = dot(normed_all, lanes, ((0,), (0,)))
    head_grad = head_grad.reshape(n_dp, strip, 3 * HEAD_DIM)
    head_grad = lax.psum_scatter(head_grad, "dp", scatter_dimension=0, tiled=False)
    own = strip // n_ctx
    head_grad = moves.to_ctx(head_grad.astype(BF16).reshape(n_ctx, own, 3 * HEAD_DIM)).astype(F32)
    head_grad = jnp.sum(head_grad.reshape(HEADS, rep, own, 3, HEAD_DIM), axis=1)
    head_grad = jnp.transpose(head_grad, (2, 1, 0, 3)).reshape(3, own, width)
    query_sum, key_sum, value_sum = head_grad[0], head_grad[1], head_grad[2]

    first_row = (dp * n_ctx + ctx) * own

    def own_rows(w):
        return lax.dynamic_slice_in_dim(w, first_row, own, 0).astype(F32)

    def own_gain(v):
        return lax.dynamic_slice_in_dim(v, first_row, own, 0)

    gain_ffn_sum = jnp.sum(own_rows(w_gate) * gate_sum + own_rows(w_up) * up_sum, axis=1) / own_gain(gain_ffn)
    gain_attn_sum = jnp.sum(
        own_rows(w_query) * query_sum + own_rows(w_key) * key_sum + own_rows(w_value) * value_sum, axis=1
    ) / own_gain(gain_attn)

    back = from_heads(grad_qkv).reshape(HEADS, 3, HEAD_DIM, rows)
    grad_norm_one = sum(
        dot(back[:, n].reshape(width, rows), w, ((0,), (1,)))
        for n, w in enumerate((w_query, w_key, w_value))
    )
    latent_grad = (grad_resid + norm_back(grad_norm_one, unit_one, inv_one, gain_attn)).astype(BF16)
    return (
        latents,
        latent_grad,
        gain_attn_sum,
        query_sum,
        key_sum,
        value_sum,
        out_sum,
        gain_ffn_sum,
        gate_sum,
        up_sum,
        down_sum,
    )


def low_t(v):
    return v.astype(F32).T.astype(BF16)


def sel(at, other):
    return 1 - at if other else at


def norm_qkv_kernel(x_ref, gain_ref, wq_ref, wk_ref, wv_ref, n_ref, qkv_ref, held_ref, sems):
    loads = [pltpu.make_async_copy(w, held_ref.at[t], sems.at[t]) for t, w in enumerate((wq_ref, wk_ref, wv_ref))]
    for load in loads:
        load.start()
    x = x_ref[...].astype(F32)
    inv = lax.rsqrt(jnp.mean(x * x, axis=-1, keepdims=True) + EPS)
    n = (x * inv * gain_ref[...]).astype(BF16)
    n_ref[...] = n
    cols = 256
    for t, load in enumerate(loads):
        load.wait()
        for c in range(0, held_ref.shape[2], cols):
            p = dot(n, held_ref[t, :, c : c + cols], ((1,), (0,))).T.astype(BF16)
            for h in range(cols // HEAD_DIM):
                qkv_ref[c // HEAD_DIM + h, t * HEAD_DIM : (t + 1) * HEAD_DIM, :] = p[h * HEAD_DIM : (h + 1) * HEAD_DIM]


def norm_qkv(x, gain, wq, wk, wv):
    rows, width = x.shape
    return call(
        norm_qkv_kernel,
        "norm_qkv",
        (x, gain.reshape(1, width), wq, wk, wv),
        outs=[
            ((rows, width), BF16),
            ((HEADS, 3 * HEAD_DIM, rows), BF16),
        ],
        scratch=[pltpu.VMEM((3, width, width), BF16), pltpu.SemaphoreType.DMA((3,))],
        far=3,
    )


def out_norm_kernel(at_ref, ab_ref, x_ref, gain_ref, w_ref, resid_ref, n_ref, send_ref, held_ref, sem):
    load = pltpu.make_async_copy(w_ref, held_ref, sem)
    load.start()
    left = low_t(ab_ref[...])
    half = send_ref.shape[0]
    send_ref[...] = ab_ref[pl.ds(pl.multiple_of((1 - at_ref[0]) * half, half), half), :]
    load.wait()
    cols = 256
    mixed = [dot(left, held_ref[:, c : c + cols], ((1,), (0,))) for c in range(0, held_ref.shape[1], cols)]
    resid = x_ref[...].astype(F32) + jnp.concatenate(mixed, axis=1)
    resid_ref[...] = resid
    inv = lax.rsqrt(jnp.mean(resid * resid, axis=-1, keepdims=True) + EPS)
    n_ref[...] = (resid * inv * gain_ref[...]).astype(BF16)


def out_norm(at, ab, x, gain, w, after):
    rows, width = x.shape
    return call(
        out_norm_kernel,
        "out_norm",
        (at, ab, x, gain.reshape(1, width), w),
        after,
        smem=1,
        outs=[((rows, width), F32), ((rows, width), BF16), ((width // 2, rows), BF16)],
        scratch=[pltpu.VMEM(w.shape, BF16), pltpu.SemaphoreType.DMA],
        far=1,
    )


def ffn_kernel(
    at_ref, n0_ref, n1_ref, dy0_ref, dy1_ref, wg_ref, wu_ref, wd_ref,
    hid_ref, d0_ref, d1_ref, px_ref, py_ref, tx_ref, ty_ref, kx_ref, ky_ref,
    n_ref, dy_ref, dg_ref, du_ref, hid_t_ref, n_t_ref, g_w, u_w, d_w, sems,
):
    rows, width = n0_ref.shape
    share = g_w.shape[1]
    high = kx_ref.shape[0]
    first = pl.multiple_of(at_ref[0] * share, 128)
    parts = ((0, 768), (768, share))
    loads = []
    for n, (lo, hi) in enumerate(parts):
        cols = pl.ds(pl.multiple_of(first + lo, 128), hi - lo)
        loads.append(
            (
                pltpu.make_async_copy(wg_ref.at[:, cols], g_w.at[:, pl.ds(lo, hi - lo)], sems.at[n, 0]),
                pltpu.make_async_copy(wu_ref.at[:, cols], u_w.at[:, pl.ds(lo, hi - lo)], sems.at[n, 1]),
                pltpu.make_async_copy(wd_ref.at[cols, :], d_w.at[pl.ds(lo, hi - lo), :], sems.at[n, 2]),
            )
        )
        for load in loads[n]:
            load.start()
    n_ref[:rows] = n0_ref[...]
    n_ref[rows:] = n1_ref[...]
    dy_ref[:rows] = dy0_ref[...]
    dy_ref[rows:] = dy1_ref[...]
    n_t_ref[...] = low_t(n_ref[...])

    for lo, hi in parts:
        for load in loads[parts.index((lo, hi))]:
            load.wait()
        for at in range(lo, hi, 256):
            lanes = slice(at, min(at + 256, share))
            g = dot(n_ref[...], g_w[:, lanes], ((1,), (0,)))
            u = dot(n_ref[...], u_w[:, lanes], ((1,), (0,)))
            dh = dot(dy_ref[...], d_w[lanes, :], ((1,), (1,)))
            sig = jax.nn.sigmoid(g)
            swish = g * sig
            hid = (swish * u).astype(BF16)
            dg = (dh * u * sig * (1.0 + g * (1.0 - sig))).astype(BF16)
            du = (dh * swish).astype(BF16)
            hid_ref[:, lanes] = hid
            hid_t_ref[lanes, :] = hid.astype(F32).T
            dg_ref[:, lanes] = dg
            du_ref[:, lanes] = du
            for k in range(dg.shape[1] // rows):
                to = high + (at // rows + k) * 2 * rows
                x_ref, y_ref = px_ref, py_ref
                if to >= px_ref.shape[0]:
                    to, x_ref, y_ref = to - px_ref.shape[0], tx_ref, ty_ref
                x_ref[to : to + 2 * rows, :] = dg[:, k * rows : (k + 1) * rows]
                y_ref[to : to + 2 * rows, :] = du[:, k * rows : (k + 1) * rows]

    for at in range(0, width, 256):
        cols = slice(at, at + 256)
        d = dot(dg_ref[...], g_w[cols, :], ((1,), (1,))) + dot(du_ref[...], u_w[cols, :], ((1,), (1,)))
        d0_ref[:, cols] = d[:rows]
        d1_ref[:, cols] = d[rows:].astype(BF16)

    own = width // 32
    chunk = share // 16
    base = high - width
    padded = base // 16
    x, y = at_ref[1], at_ref[2]
    fill = jnp.zeros((padded - chunk, rows), F32)

    def put(ref, inner, z, xs, ys):
        c = z * 4 + ys * 2 + xs
        for half in range(2):
            lanes = slice(half * rows, (half + 1) * rows)
            v = hid_t_ref[pl.ds(pl.multiple_of(c * chunk, 8), chunk), lanes]
            to = ((inner * 4 + z) * 2 + half) * padded
            ref[to : to + padded, :] = jnp.concatenate([v, fill], axis=0).astype(BF16)
            for d in range(2):
                to = base + half * (width // 2) + ((inner * 4 + z) * 2 + d) * own
                at = pl.multiple_of(d * (width // 2) + c * own, own)
                ref[to : to + own, :] = n_t_ref[pl.ds(at, own), lanes]

    for inner in range(2):
        for z in range(4):
            put(kx_ref, inner, z, x, sel(y, inner))
            put(px_ref, inner, z, 1 - x, sel(y, inner))
            put(ky_ref, inner, z, sel(x, inner), y)
            put(py_ref, inner, z, sel(x, inner), 1 - y)


def ffn(at, n0, n1, dy0, dy1, wg, wu, wd, after):
    rows, width = n0.shape
    share = wg.shape[1] // 2
    padded = -(-(share // 16) // 16) * 16
    high = 16 * padded + width
    early = EARLY * 2 * rows
    sizes = [high + early] * 2 + [2 * share - early] * 2 + [high] * 2
    return call(
        ffn_kernel,
        "ffn",
        (at, n0, n1, dy0, dy1, wg, wu, wd),
        after,
        smem=1,
        outs=[((2 * rows, share), BF16), ((rows, width), F32), ((rows, width), BF16)]
        + [((n, rows), BF16) for n in sizes[:4]]
        + [((n, rows), BF16, HBM) for n in sizes[4:]],
        scratch=[
            pltpu.VMEM((2 * rows, width), BF16),
            pltpu.VMEM((2 * rows, width), BF16),
            pltpu.VMEM((2 * rows, share), BF16),
            pltpu.VMEM((2 * rows, share), BF16),
            pltpu.VMEM((share, 2 * rows), F32),
            pltpu.VMEM((width, 2 * rows), BF16),
            pltpu.VMEM((width, share), BF16),
            pltpu.VMEM((width, share), BF16),
            pltpu.VMEM((share, width), BF16),
            pltpu.SemaphoreType.DMA((2, 3)),
        ],
        vmem=40,
        far=3,
    )


def ffn_out_kernel(at_ref, hid_ref, w_ref, y0_ref, y1_ref, held_ref, sem):
    rows, width = y0_ref.shape
    share = held_ref.shape[0]
    first = pl.multiple_of(at_ref[0] * share, 128)
    load = pltpu.make_async_copy(w_ref.at[pl.ds(first, share), :], held_ref, sem)
    load.start()
    load.wait()
    for at in range(0, width, 256):
        cols = slice(at, at + 256)
        y = dot(hid_ref[...], held_ref[:, cols], ((1,), (0,)))
        y0_ref[:, cols] = y[:rows]
        y1_ref[:, cols] = y[rows:].astype(BF16)


def ffn_out(at, hid, w, after):
    shape = (hid.shape[0] // 2, w.shape[1])
    return call(
        ffn_out_kernel,
        "ffn_out",
        (at, hid, w),
        after,
        smem=1,
        outs=[(shape, F32), (shape, BF16)],
        scratch=[pltpu.VMEM((hid.shape[1], w.shape[1]), BF16), pltpu.SemaphoreType.DMA],
        far=1,
    )


def ffn_back_kernel(d_ref, got_ref, resid_ref, gain_ref, dy_ref, w_ref, dres_ref, low_ref, da_ref, held_ref, sem):
    load = pltpu.make_async_copy(w_ref, held_ref, sem)
    load.start()
    d = d_ref[...] + got_ref[...].astype(F32)
    resid = resid_ref[...]
    inv = lax.rsqrt(jnp.mean(resid * resid, axis=-1, keepdims=True) + EPS)
    dres = dy_ref[...].astype(F32) + norm_back(d, resid * inv, inv, gain_ref[...])
    dres_ref[...] = dres
    low = dres.astype(BF16)
    low_ref[...] = low
    load.wait()
    for at in range(0, held_ref.shape[0], 256):
        da_ref[at : at + 256, :] = dot(held_ref[at : at + 256, :], low, ((1,), (1,))).astype(BF16)


def ffn_back(d, got, resid, gain, dy, w, after):
    rows, width = d.shape
    return call(
        ffn_back_kernel,
        "ffn_back",
        (d, got, resid, gain.reshape(1, width), dy, w),
        after,
        outs=[((rows, width), F32), ((rows, width), BF16), ((width, rows), BF16)],
        scratch=[pltpu.VMEM(w.shape, BF16), pltpu.SemaphoreType.DMA],
        far=1,
    )


EARLY = 4


def out_product_kernel(at_ref, ab_ref, got_ref, low0_ref, low1_ref, kx_ref, px_ref, ky_ref, py_ref, acc_ref):
    half, rows = got_ref.shape
    own = half // 16
    x, y = at_ref[1], at_ref[2]
    mine = ab_ref[pl.ds(pl.multiple_of(at_ref[0] * half, half), half), :]
    left = jnp.concatenate([mine, got_ref[...]], axis=1)
    right = jnp.concatenate([low0_ref[...], low1_ref[...]], axis=0)
    for at in range(0, acc_ref.shape[1], 256):
        acc_ref[:, at : at + 256] = dot(left, right[:, at : at + 256], ((1,), (0,)))
    tiles = acc_ref.shape[1] // 2 // rows

    def put(ref, inner, z, xs, ys, side):
        at = pl.multiple_of((z * 4 + ys * 2 + xs) * own, own)
        for j in range(tiles):
            lanes = slice((side * tiles + j) * rows, (side * tiles + j + 1) * rows)
            to = ((inner * 4 + z) * tiles + j) * own
            ref[to : to + own, :] = acc_ref[pl.ds(at, own), lanes].astype(BF16)

    for inner in range(2):
        for z in range(4):
            put(kx_ref, inner, z, x, sel(y, inner), 0)
            put(px_ref, inner, z, 1 - x, sel(y, inner), 0)
            put(ky_ref, inner, z, sel(x, inner), y, 1)
            put(py_ref, inner, z, sel(x, inner), 1 - y, 1)


def out_product(at, ab, got, low, low_mate, after):
    half, rows = got.shape
    high = half // 2 * (low.shape[1] // 2) // rows
    return call(
        out_product_kernel,
        "out_product",
        (at, ab, got, low, low_mate),
        after,
        smem=1,
        outs=[((high, rows), BF16)] * 4,
        scratch=[pltpu.VMEM((half, low.shape[1]), F32)],
    )


def store(refs, v, lanes, high, to):
    for inner in range(2):
        for z in range(4):
            at = (inner * 4 + z) * high
            refs[inner][z, to : to + high, :] = v[at : at + high, lanes]


def pair_tiles(out, left, f0, f1, start, count, base, own):
    rows = f0.shape[1]
    for t in range(0, count, 2):
        n = min(2, count - t)
        at = [start + (t + k) * 2 * rows for k in range(n)]
        right = [jnp.concatenate([f[a : a + 2 * rows, :] for f in (f0, f1)], axis=0) for a in at]
        v = dot(left, jnp.concatenate(right, axis=1), ((1,), (0,))).astype(BF16)
        for k in range(n):
            store(out, v, slice(k * rows, (k + 1) * rows), 2 * own, base + (t + k) * 2 * own)


def left_rows(k0, p1, width):
    high, half = k0.shape[0], width // 2
    at = high - width
    return jnp.concatenate([r[at + k * half : at + (k + 1) * half, :] for r in (k0, p1) for k in range(2)], axis=1)


def first_product_kernel(side, k0, p0, p1, dy0, dy1, dy2, same_ref, other_ref):
    out = (same_ref, other_ref)
    high, rows = k0.shape
    width = dy0.shape[1]
    half, own = width // 2, width // 32
    padded = (high - width) // 16

    def lanes(ref, k):
        at = k * 2 * padded
        return jnp.concatenate([ref[at : at + padded, :], ref[at + padded : at + 2 * padded, :]], axis=1)

    hid = jnp.concatenate([jnp.concatenate([lanes(k0, k), lanes(p1, k)], axis=1) for k in range(8)], axis=0)
    cols = slice(side * half, (side + 1) * half)
    dy = jnp.concatenate([dy0[:, cols], dy1[:, cols], dy2[...]], axis=0)
    v = dot(hid, dy, ((1,), (0,))).astype(BF16)
    for j in range(half // rows):
        store(out, v, slice(j * rows, (j + 1) * rows), padded, j * padded)
    count = (p0.shape[0] - high) // (2 * rows)
    pair_tiles(out, left_rows(k0, p1, width), p0, p1, high, count, half // rows * padded, own)


def first_product(side, kept, sent, got, dy, after):
    (high, rows), width = kept.shape, dy[0].shape[1]
    tall = width // 2 // rows * (high - width) // 16 + (sent.shape[0] - high) // (2 * rows) * (width // 16)
    kernel = functools.partial(first_product_kernel, side)
    outs = [((4, tall, rows), BF16)] * 2
    return call(kernel, "first_product", (kept, sent, got, *dy), after, outs=outs)


def second_product_kernel(width, k0, p1, f0, f1, q0, q1, same_ref, other_ref):
    out = (same_ref, other_ref)
    count, own = f0.shape[0] // (2 * f0.shape[1]), width // 32
    pair_tiles(out, left_rows(k0, p1, width), f0, f1, 0, count, 0, own)
    base, tall = count * 2 * own, q0.shape[0] // 8
    for k in range(8):
        v = q0[k * tall : (k + 1) * tall, :].astype(F32) + q1[k * tall : (k + 1) * tall, :].astype(F32)
        out[k // 4][k % 4, base : base + tall, :] = v.astype(BF16)


def second_product(width, kept, got, tiles, q, after):
    rows = kept.shape[1]
    tall = tiles[0].shape[0] // (2 * rows) * (width // 16) + q[0].shape[0] // 8
    kernel = functools.partial(second_product_kernel, width)
    outs = [((4, tall, rows), BF16)] * 2
    return call(kernel, "second_product", (kept, got, *tiles, *q), after, outs=outs)


def combine_kernel(at_ref, *refs):
    parts, (own_ref, far_ref, send_ref) = refs[:-3], refs[-3:]
    high = own_ref.shape[0]
    for k, out_ref, start in ((0, own_ref, 0), (3, far_ref, 0), (1, send_ref, 0), (2, send_ref, high)):
        z = jnp.bitwise_xor(at_ref[3], k)
        to = start
        for n in range(0, len(parts), 2):
            rows = parts[n].shape[1]
            out_ref[to : to + rows, :] = (parts[n][z].astype(F32) + parts[n + 1][z].astype(F32)).astype(BF16)
            to += rows


def combine(at, parts, after):
    high, rows = sum(v.shape[1] for v in parts[::2]), parts[0].shape[2]
    outs = [((high, rows), BF16), ((high, rows), BF16), ((2 * high, rows), BF16)]
    return call(combine_kernel, "combine", (at, *parts), after, smem=1, outs=outs)


def cross_kernel(own_ref, far_ref, got_ref, sum_ref, send_ref):
    high = own_ref.shape[0]
    sum_ref[...] = (own_ref[...].astype(F32) + got_ref[:high, :].astype(F32)).astype(BF16)
    send_ref[...] = (far_ref[...].astype(F32) + got_ref[high:, :].astype(F32)).astype(BF16)


def cross(own, far, got, after):
    return call(cross_kernel, "cross", (own, far, got), after, outs=[(own.shape, BF16)] * 2)


def add_lines(refs, sum_ref):
    total = refs[0][...].astype(F32)
    for ref in refs[1:]:
        total += ref[...].astype(F32)
    sum_ref[...] = total


def shares(ref, at, own, dp, mine_ref, theirs_ref, part, t):
    rows = ref.shape[1]
    lanes = slice(t * rows, (t + 1) * rows)
    mine_ref[part, :, lanes] = ref[pl.ds(pl.multiple_of(at + dp * own, own), own), :]
    theirs_ref[part, :, lanes] = ref[pl.ds(pl.multiple_of(at + (1 - dp) * own, own), own), :].astype(BF16)


def unpack_one_kernel(at_ref, i0, i1, down_ref, mine_ref, theirs_ref, sum_ref):
    add_lines((i0, i1), sum_ref)
    rows = i0.shape[1]
    own = mine_ref.shape[1]
    chunk, width = down_ref.shape
    padded = -(-chunk // 16) * 16
    count = width // 2 // rows
    for part in range(2):
        base = part * (i0.shape[0] // 2)
        for j in range(count):
            lanes = slice((part * count + j) * rows, (part * count + j + 1) * rows)
            down_ref[:, lanes] = sum_ref[base + j * padded : base + j * padded + chunk, :]
        for t in range(EARLY):
            shares(sum_ref, base + count * padded + t * 2 * own, own, at_ref[0], mine_ref, theirs_ref, part, t)


def unpack_one(at, v, own, chunk, width, after):
    wide = EARLY * v[0].shape[1]
    outs = [((chunk, width), F32), ((2, own, wide), F32), ((2, own, wide), BF16)]
    scratch = [pltpu.VMEM(v[0].shape, F32)]
    return call(unpack_one_kernel, "unpack_one", (at, *v), after, smem=1, outs=outs, scratch=scratch)


def unpack_two_kernel(at_ref, i0, i1, mine_ref, theirs_ref, out_ref, sum_ref):
    add_lines((i0, i1), sum_ref)
    rows = i0.shape[1]
    own, width = out_ref.shape
    tiles = mine_ref.shape[2] // rows
    count = width // 2 // rows
    for part in range(2):
        base = part * (i0.shape[0] // 2)
        for t in range(tiles):
            shares(sum_ref, base + t * 2 * own, own, at_ref[0], mine_ref, theirs_ref, part, t)
        base += tiles * 2 * own
        for j in range(count):
            lanes = slice((part * count + j) * rows, (part * count + j + 1) * rows)
            out_ref[:, lanes] = sum_ref[base + j * own : base + (j + 1) * own, :]


def unpack_two(at, v, own, wide, width, after):
    wide -= EARLY * v[0].shape[1]
    outs = [((2, own, wide), F32), ((2, own, wide), BF16), ((own, width), F32)]
    scratch = [pltpu.VMEM(v[0].shape, F32)]
    return call(unpack_two_kernel, "unpack_two", (at, *v), after, smem=1, outs=outs, scratch=scratch)


def finish_kernel(at_ref, m0, m1, o0, o1, gain_ref, wg_ref, wu_ref, gate_ref, up_ref, dots_ref):
    dp = at_ref[1]
    share = gate_ref.shape[1] // 2
    early = m0.shape[2]
    for part, ref in enumerate((gate_ref, up_ref)):

        def put(at, a, b):
            ref[:, at : at + early] = a[part].astype(F32)
            ref[:, at + early : at + share] = b[part].astype(F32)

        @pl.when(dp == 0)
        def _():
            put(0, m0, m1)
            put(share, o0, o1)

        @pl.when(dp == 1)
        def _():
            put(0, o0, o1)
            put(share, m0, m1)

    total = gate_ref[...] * wg_ref[...].astype(F32) + up_ref[...] * wu_ref[...].astype(F32)
    dots_ref[...] = by_gain(jnp.sum(total, axis=1, keepdims=True), gain_ref, at_ref[0])


def finish(where, mine, theirs, gain, wg, wu):
    own, ff = mine[0].shape[1], wg.shape[1]
    count = wg.shape[0] // own

    def whole(*shape):
        return pl.BlockSpec(shape, lambda g, at: (0,) * len(shape))

    weight = pl.BlockSpec((own, ff), lambda g, at: (at[0], 0))
    gate, up, dots = pl.pallas_call(
        finish_kernel,
        grid_spec=pltpu.PrefetchScalarGridSpec(
            num_scalar_prefetch=1,
            grid=(1,),
            in_specs=[whole(*v.shape) for v in (*mine, *theirs)] + [whole(count, own), weight, weight],
            out_specs=[whole(own, ff), whole(own, ff), whole(1, own)],
        ),
        out_shape=[jax.ShapeDtypeStruct((own, ff), F32)] * 2 + [jax.ShapeDtypeStruct((1, own), F32)],
        cost_estimate=COST,
        name="finish",
    )(where, *mine, *theirs, gain.reshape(count, own), in_hbm(wg), in_hbm(wu))
    return gate, up, dots.reshape(own)


def turn_kernel(in_ref, out_ref):
    for h in range(4):
        for z in range(4):
            out_ref[z, h] = in_ref[h, z]


def turn(v, after):
    return call(turn_kernel, "turn", (v,), after, outs=[(v.shape, BF16)])[0]


def head_product_kernel(at_ref, n0, n1, in_ref, mine_ref, theirs_ref, acc_ref):
    half = mine_ref.shape[0]
    x, y = at_ref[1], at_ref[2]
    left = jnp.concatenate(
        [
            jnp.concatenate([in_ref[h, sel(y, oy) * 2 + sel(x, ox)] for oy in range(2) for ox in range(2)], axis=1)
            for h in range(4)
        ],
        axis=0,
    )
    right = jnp.concatenate([n0[...], n1[...]], axis=0)
    for at in range(0, acc_ref.shape[0], 256):
        acc_ref[at : at + 256, :] = dot(left, right[:, at : at + 256], ((1,), (0,))).T
    dp = at_ref[0]
    mine_ref[...] = acc_ref[pl.ds(pl.multiple_of(dp * half, half), half), :]
    theirs_ref[...] = acc_ref[pl.ds(pl.multiple_of((1 - dp) * half, half), half), :].astype(BF16)


def head_product(at, n, v, after):
    width, wide = n[0].shape[1], 4 * v.shape[2]
    return call(
        head_product_kernel,
        "head_product",
        (at, *n, v),
        after,
        smem=1,
        outs=[((width // 2, wide), F32), ((width // 2, wide), BF16)],
        scratch=[pltpu.VMEM((width, wide), F32)],
    )


def head_split_kernel(at_ref, mine_ref, got_ref, own_ref, far_ref, send_ref):
    high = own_ref.shape[0]
    for k, ref, to in ((0, own_ref, 0), (3, far_ref, 0), (1, send_ref, 0), (2, send_ref, high)):
        rows = pl.ds(pl.multiple_of(jnp.bitwise_xor(at_ref[3], k) * high, high), high)
        ref[to : to + high, :] = (mine_ref[rows, :] + got_ref[rows, :].astype(F32)).astype(BF16)


def head_split(at, mine, got, after):
    half, wide = mine.shape
    outs = [((half // 4, wide), BF16), ((half // 4, wide), BF16), ((half // 2, wide), BF16)]
    return call(head_split_kernel, "head_split", (at, mine, got), after, smem=1, outs=outs)


def head_end_kernel(a, ga, out_ref):
    own = a.shape[0] // 4
    v = (a[...].astype(F32) + ga[...].astype(F32)).astype(BF16)
    for p in range(4):
        out_ref[p] = v[p * own : (p + 1) * own]


def head_end(a, ga, after):
    outs = [((4, a.shape[0] // 4, a.shape[1]), BF16)]
    return call(head_end_kernel, "head_end", (a, ga), after, outs=outs)[0]


def latent_back_kernel(
    back_ref, dres_ref, x_ref, gain_ref, wq_ref, wk_ref, wv_ref, out_ref, left_ref, d_ref, held_ref, sems
):
    loads = [pltpu.make_async_copy(w, held_ref.at[t], sems.at[t]) for t, w in enumerate((wq_ref, wk_ref, wv_ref))]
    for load in loads:
        load.start()
    for h in range(HEADS):
        for t in range(3):
            left_ref[t, h * HEAD_DIM : (h + 1) * HEAD_DIM, :] = back_ref[h % 4 * 4 + h // 4, t * HEAD_DIM : (t + 1) * HEAD_DIM, :]
    for load in loads:
        load.wait()
    for at in range(0, d_ref.shape[1], 256):
        v = dot(held_ref[0, at : at + 256, :], left_ref[0], ((1,), (0,)))
        v += dot(held_ref[1, at : at + 256, :], left_ref[1], ((1,), (0,)))
        v += dot(held_ref[2, at : at + 256, :], left_ref[2], ((1,), (0,)))
        d_ref[:, at : at + 256] = v.T
    x = x_ref[...].astype(F32)
    inv = lax.rsqrt(jnp.mean(x * x, axis=-1, keepdims=True) + EPS)
    out_ref[...] = (dres_ref[...] + norm_back(d_ref[...], x * inv, inv, gain_ref[...])).astype(BF16)


def latent_back(back, dres, x, gain, wq, wk, wv, after):
    rows, width = x.shape
    return call(
        latent_back_kernel,
        "latent_back",
        (back, dres, x, gain.reshape(1, width), wq, wk, wv),
        after,
        outs=[((rows, width), BF16)],
        scratch=[
            pltpu.VMEM((3, width, rows), BF16),
            pltpu.VMEM((rows, width), F32),
            pltpu.VMEM((3, width, width), BF16),
            pltpu.SemaphoreType.DMA((3,)),
        ],
        far=3,
    )[0]


def by_gain(sums, gain_ref, place):
    return jnp.broadcast_to(sums, (sums.shape[0], 128)).T[:1] / gain_ref[pl.ds(place, 1), :]


def head_rows_kernel(at_ref, in_ref, gain_ref, wq_ref, wk_ref, wv_ref, q_ref, k_ref, v_ref, dots_ref):
    total = None
    for t, (w_ref, o_ref) in enumerate(((wq_ref, q_ref), (wk_ref, k_ref), (wv_ref, v_ref))):
        for h in range(0, HEADS, 2):
            at = (h // 4 * 3 + t) * HEAD_DIM
            pair = [in_ref[h % 4 + n][:, at : at + HEAD_DIM] for n in range(2)]
            o_ref[:, h * HEAD_DIM : (h + 2) * HEAD_DIM] = jnp.concatenate(pair, axis=1).astype(F32)
        v = jnp.sum(o_ref[...] * w_ref[...].astype(F32), axis=1, keepdims=True)
        total = v if total is None else total + v
    dots_ref[...] = by_gain(total, gain_ref, at_ref[0])


def head_rows(where, v, gain, wq, wk, wv):
    own, width = v.shape[1], wq.shape[1]
    weight = pl.BlockSpec((own, width), lambda g, at: (at[0], 0))

    def whole(*shape):
        return pl.BlockSpec(shape, lambda g, at: (0,) * len(shape))

    out = pl.pallas_call(
        head_rows_kernel,
        grid_spec=pltpu.PrefetchScalarGridSpec(
            num_scalar_prefetch=1,
            grid=(1,),
            in_specs=[whole(*v.shape), whole(width // own, own), weight, weight, weight],
            out_specs=[whole(own, width)] * 3 + [whole(1, own)],
        ),
        out_shape=[jax.ShapeDtypeStruct((own, width), F32)] * 3 + [jax.ShapeDtypeStruct((1, own), F32)],
        cost_estimate=COST,
        name="head_rows",
    )(where, v, gain.reshape(width // own, own), in_hbm(wq), in_hbm(wk), in_hbm(wv))
    return *out[:3], out[3].reshape(own)


X_PAIRS = [(i, i ^ 1) for i in range(16)]
Y_PAIRS = [(i, i ^ 2) for i in range(16)]


def swap(v):
    return lax.ppermute(v, "dp", [(0, 1), (1, 0)])


def over_x(v):
    return lax.ppermute(v, "ctx", X_PAIRS)


def over_y(v):
    return lax.ppermute(v, "ctx", Y_PAIRS)


def over_z(v, k):
    return lax.ppermute(v, "ctx", [(i, i ^ (4 * k)) for i in range(16)])


Z_LINES = [[i + 4 * z for z in range(4)] for i in range(4)]
PLANES = [[i + 4 * z for i in range(4)] for z in range(4)]


def in_group(v, groups):
    return lax.all_to_all(v, "ctx", 0, 0, tiled=True, axis_index_groups=groups)


def to_ctx(v):
    return lax.all_to_all(v, "ctx", 0, 0, tiled=True)


def per_device_grid(
    latent_in,
    gain_attn,
    w_query,
    w_key,
    w_value,
    w_out,
    gain_ffn,
    w_gate,
    w_up,
    w_down,
    cotangent,
    seq_lengths,
    span_order,
):
    rows, width = latent_in.shape
    ff = w_gate.shape[1]
    half, own = width // 2, width // 32
    dp, ctx = lax.axis_index("dp"), lax.axis_index("ctx")
    at = jnp.stack([dp, ctx % 2, (ctx // 2) % 2, ctx // 4]).astype(jnp.int32)
    scalars = positions(seq_lengths, span_order, rows, ctx * 0)

    dy_mate = swap(cotangent)
    dy_x = over_x(jnp.concatenate([cotangent[:, :half], dy_mate[:, :half]], axis=0))
    dy_y = over_y(jnp.concatenate([cotangent[:, half:], dy_mate[:, half:]], axis=0))

    normed, qkv = norm_qkv(latent_in, gain_attn, w_query, w_key, w_value)
    qkv = to_ctx(qkv)

    line = jnp.concatenate([normed, over_x(normed)], axis=0)
    line = (line, over_y(line))
    out, full, top, inv = attn_fwd(1, scalars, qkv, (dy_x, dy_y))
    attn_t = to_ctx(out).reshape(width, rows)
    resid, normed_two, attn_send = out_norm(at, attn_t, latent_in, gain_ffn, w_out, (line[1],))
    normed_mate = swap(normed_two)
    attn_mate = swap(attn_send)

    hid, d_own, d_mate, send_x, send_y, tiles_x, tiles_y, kept_x, kept_y = ffn(
        at, normed_two, normed_mate, cotangent, dy_mate, w_gate, w_up, w_down, ()
    )
    d_got = swap(d_mate)
    got_x, got_y = over_x(send_x), over_y(send_y)
    tiles_x, tiles_y = (tiles_x, over_x(tiles_x)), (tiles_y, over_y(tiles_y))
    dres, dres_low, grad_attn = ffn_back(d_own, d_got, resid, gain_ffn, cotangent, w_out, ())
    grad_attn = to_ctx(grad_attn.reshape(HEADS, HEAD_DIM, rows))
    out_x, out_sx, out_y, out_sy = out_product(at, attn_t, attn_mate, dres_low, swap(dres_low), ())
    out_x, out_y = (out_x, over_x(out_sx)), (out_y, over_y(out_sy))

    dy_a, dy_b = (cotangent, dy_mate, dy_x), (cotangent, dy_mate, dy_y)
    one_a, other_a = first_product(0, kept_x, send_x, got_x, dy_a, (out_x[0],))
    one_b, other_b = first_product(1, kept_y, send_y, got_y, dy_b, (one_a,))
    one = (one_a, over_y(other_a), one_b, over_x(other_b))
    grad_qkv = attn_bwd(
        1, lambda slot: slot, scalars, qkv, grad_attn, full, top, inv, (one_b, tiles_x[1], tiles_y[1], out_x[1], out_y[1])
    )
    four = in_group(grad_qkv, Z_LINES).reshape(4, 4, 3 * HEAD_DIM, rows)
    two_a, other_a = second_product(width, kept_x, got_x, tiles_x, out_x, (grad_qkv,))
    two_b, other_b = second_product(width, kept_y, got_y, tiles_y, out_y, (two_a,))
    two = (two_a, over_y(other_a), two_b, over_x(other_b))
    one_own, one_far, one_send = combine(at, one, (two_b,))
    one_got = over_z(one_send, 1)
    y_own, y_mate = ffn_out(at, hid, w_down, (one_own,))
    latents = (resid + y_own + swap(y_mate).astype(F32)).astype(BF16)
    two_own, two_far, two_send = combine(at, two, (y_own,))
    two_got = over_z(two_send, 1)

    turned = turn(four, (two_own,))
    back = in_group(turned, PLANES).reshape(16, 3 * HEAD_DIM, rows)
    one_own, one_send = cross(one_own, one_far, one_got, (turned,))
    head_mine, head_theirs = head_product(at, line, four, (one_own,))
    head_own, head_far, head_send = head_split(at, head_mine, swap(head_theirs), ())
    head_got = over_z(head_send, 1)
    down_sum, mine0, theirs0 = unpack_one(
        at, (one_own, over_z(one_send, 3)), own, ff // 32, width, (head_own,)
    )
    two_own, two_send = cross(two_own, two_far, two_got, (down_sum,))
    latent_grad = latent_back(back, dres, latent_in, gain_attn, w_query, w_key, w_value, (two_own,))
    head_own, head_send = cross(head_own, head_far, head_got, (latent_grad,))
    heads = head_end(head_own, over_z(head_send, 3), ())
    heads = in_group(heads, PLANES)
    place = dp * 16 + ctx
    where = jnp.stack([place, dp]).astype(jnp.int32)
    mine1, theirs1, out_sum = unpack_two(at, (two_own, over_z(two_send, 3)), own, ff // 2, width, (head_own,))
    theirs = (swap(theirs0), swap(theirs1))
    query_sum, key_sum, value_sum, gain_attn_sum = head_rows(
        where, order(heads, (out_sum,)), gain_attn, w_query, w_key, w_value
    )
    gate_sum, up_sum, gain_ffn_sum = finish(where, (mine0, mine1), theirs, gain_ffn, w_gate, w_up)
    return (
        latents,
        latent_grad,
        gain_attn_sum,
        query_sum,
        key_sum,
        value_sum,
        out_sum,
        gain_ffn_sum,
        gate_sum,
        up_sum,
        down_sum,
    )


def solution(mesh):
    n_dp, n_ctx = mesh.shape["dp"], mesh.shape["ctx"]
    if n_dp == 2 and n_ctx == 16:
        body = per_device_grid
    else:
        body = functools.partial(per_device_any, Moves(n_dp, n_ctx))
    rows, whole, share = P(("dp", "ctx"), None), P(), P("dp", None)
    flat = P(("dp", "ctx"))
    return jax.shard_map(
        body,
        mesh=mesh,
        in_specs=(rows,) + (whole,) * 9 + (rows, share, share),
        out_specs=(rows, rows, flat, rows, rows, rows, rows, flat, rows, rows, rows),
        check_vma=False,
    )
```

```python
import functools

import jax
import jax.numpy as jnp
from jax import lax
from jax.experimental import pallas as pl
from jax.experimental.pallas import tpu as pltpu
from jax.sharding import PartitionSpec as P

HEADS = 16
HEAD_DIM = 64
EPS = 1e-06
NEG_FILL = -1e30
LOG2E = 1.4426950408889634
SCALE = HEAD_DIM**-0.5

BF16 = jnp.bfloat16
F32 = jnp.float32


def dot(a, b, dims):
    return lax.dot_general(a, b, (dims, ((), ())), preferred_element_type=F32)


def query_starts(ends_ref, pos):
    start = jnp.zeros_like(pos)
    for n in range(ends_ref.shape[0]):
        start = jnp.where(pos >= ends_ref[n], ends_ref[n], start)
    return start


def block_mask(ends_ref, i, j, blk):
    pos = lax.broadcasted_iota(jnp.int32, (1, blk), 1) + i * blk
    start = query_starts(ends_ref, pos) - j * blk
    key = lax.broadcasted_iota(jnp.int32, (2 * blk, blk), 0)
    return (key <= pos - j * blk) & (key >= start)


def four_slots(slot_ref, j, count):
    n = jnp.minimum(j + 1, count - 1)
    return slot_ref[2 * j], slot_ref[2 * j + 1], slot_ref[2 * n], slot_ref[2 * n + 1]


def attn_fwd_kernel(rep, slot_ref, low_ref, ends_ref, part_ref, qkv_ref, out_ref, full_ref, top_ref, inv_ref, key_ref):
    slots, _, rows = qkv_ref.shape
    blk = 2 * rows
    count = slots // 2
    hd = HEAD_DIM

    def flip(s, c):
        key_ref[s] = qkv_ref[s, hd : 2 * hd, :].T
        return c

    lax.fori_loop(0, slots, flip, 0)
    if rep > 1:
        out_ref[...] = jnp.zeros_like(out_ref)
        full_ref[...] = jnp.zeros_like(full_ref)

    def query_block(i, c):
        s0, s1 = slot_ref[2 * i], slot_ref[2 * i + 1]
        q = jnp.concatenate([qkv_ref[s0, :hd, :], qkv_ref[s1, :hd, :]], axis=1)

        low = low_ref[i]

        def key_block(n, state):
            top, mass, acc = state
            j = low + 2 * n
            keys = four_slots(slot_ref, j, count)
            k = jnp.concatenate([key_ref[t] for t in keys], axis=0)
            v = jnp.concatenate([qkv_ref[t, 2 * hd :, :] for t in keys], axis=1)
            s = dot(k, q, ((1,), (0,))) * (SCALE * LOG2E)
            s = jnp.where(block_mask(ends_ref, i, j, blk), s, NEG_FILL)
            new_top = jnp.maximum(top, jnp.max(s, axis=0, keepdims=True))
            shrink = jnp.exp2(top - new_top)
            w = jnp.exp2(s - new_top)
            mass = mass * shrink + jnp.sum(w, axis=0, keepdims=True)
            acc = acc * shrink + dot(v, w.astype(BF16), ((1,), (0,)))
            return new_top, mass, acc

        init = (
            jnp.full((1, blk), NEG_FILL, F32),
            jnp.zeros((1, blk), F32),
            jnp.zeros((hd, blk), F32),
        )
        top, mass, acc = lax.fori_loop(0, (i + 2 - low) // 2, key_block, init)
        inv = 1.0 / mass
        acc = acc * inv
        full_ref[s0] = acc[:, :rows]
        full_ref[s1] = acc[:, rows:]
        rounded = acc.astype(BF16)
        out_ref[s0] = rounded[:, :rows]
        out_ref[s1] = rounded[:, rows:]
        top_ref[i] = top
        inv_ref[i] = inv
        return c

    lax.fori_loop(0, count // rep, lambda n, c: query_block(n * rep + part_ref[0], c), 0)


def attn_bwd_kernel(
    rep, place, slot_ref, low_ref, ends_ref, part_ref, qkv_ref, da_ref, full_ref, top_ref, inv_ref,
    out_ref, key_ref, value_ref, dk_ref, dv_ref,
):
    slots, _, rows = qkv_ref.shape
    blk = 2 * rows
    count = slots // 2
    hd = HEAD_DIM

    def flip(s, c):
        key_ref[s] = qkv_ref[s, hd : 2 * hd, :].T
        value_ref[s] = qkv_ref[s, 2 * hd :, :].T
        return c

    lax.fori_loop(0, slots, flip, 0)
    dk_ref[...] = jnp.zeros_like(dk_ref)
    dv_ref[...] = jnp.zeros_like(dv_ref)
    if rep > 1:
        out_ref[...] = jnp.zeros_like(out_ref)

    def pair(ref, a, b, lo, hi):
        return jnp.concatenate([ref[a, lo:hi, :], ref[b, lo:hi, :]], axis=1)

    def query_block(i, c):
        s0, s1 = slot_ref[2 * i], slot_ref[2 * i + 1]
        q = pair(qkv_ref, s0, s1, 0, hd)
        da = pair(da_ref, s0, s1, 0, hd)
        full = pair(full_ref, s0, s1, 0, hd)
        delta = jnp.sum(da.astype(F32) * full, axis=0, keepdims=True)
        top, inv = top_ref[i], inv_ref[i]

        low = low_ref[i]

        def key_block(n, dq):
            j = low + 2 * n
            after = jnp.minimum(j + 1, count - 1)
            keys = four_slots(slot_ref, j, count)
            k = jnp.concatenate([key_ref[t] for t in keys], axis=0)
            v = jnp.concatenate([value_ref[t] for t in keys], axis=0)
            s = dot(k, q, ((1,), (0,))) * (SCALE * LOG2E)
            s = jnp.where(block_mask(ends_ref, i, j, blk), s, NEG_FILL)
            p = jnp.exp2(s - top) * inv
            dp = dot(v, da, ((1,), (0,)))
            ds = (p * (dp - delta)).astype(BF16)
            dk = dot(q, ds, ((1,), (1,)))
            dv = dot(da, p.astype(BF16), ((1,), (1,)))
            dk_ref[j] += dk[:, :blk]
            dk_ref[after] += dk[:, blk:]
            dv_ref[j] += dv[:, :blk]
            dv_ref[after] += dv[:, blk:]
            k_t = jnp.concatenate([qkv_ref[t, hd : 2 * hd, :] for t in keys], axis=1)
            return dq + dot(k_t, ds, ((1,), (0,)))

        dq = lax.fori_loop(0, (i + 2 - low) // 2, key_block, jnp.zeros((hd, blk), F32))
        dq = (dq * SCALE).astype(BF16)
        out_ref[place(s0), :hd, :] = dq[:, :rows]
        out_ref[place(s1), :hd, :] = dq[:, rows:]
        return c

    lax.fori_loop(0, count // rep, lambda n, c: query_block(n * rep + part_ref[0], c), 0)

    def finish(j, c):
        k0, k1 = place(slot_ref[2 * j]), place(slot_ref[2 * j + 1])
        dk = (dk_ref[j] * SCALE).astype(BF16)
        dv = dv_ref[j].astype(BF16)
        out_ref[k0, hd : 2 * hd, :] = dk[:, :rows]
        out_ref[k1, hd : 2 * hd, :] = dk[:, rows:]
        out_ref[k0, 2 * hd :, :] = dv[:, :rows]
        out_ref[k1, 2 * hd :, :] = dv[:, rows:]
        return c

    lax.fori_loop(0, count, finish, 0)


def in_hbm(v):
    return pltpu.with_memory_space_constraint(v, pltpu.HBM)


class Chain:
    last = ()


def call(kernel, name, args, after=(), smem=0, outs=(), scratch=(), vmem=24, far=0):
    held = len(args)
    after = (*after, *Chain.last)
    skip = held + len(after)
    if far:
        args = (*args[: held - far], *(in_hbm(v) for v in args[held - far :]))

    def body(*refs):
        refs[skip][...] = jnp.zeros((8, 128), F32)
        kernel(*refs[:held], *refs[skip + 1 :])

    token, *result = pl.pallas_call(
        body,
        in_specs=[SMEM] * smem + [VMEM] * (held - smem - far) + [HBM] * far + [ANY] * len(after),
        out_specs=[VMEM] * (1 + len(outs)),
        out_shape=[jax.ShapeDtypeStruct((8, 128), F32)]
        + [pltpu.HBM(*o[:2]) if len(o) > 2 else jax.ShapeDtypeStruct(*o) for o in outs],
        scratch_shapes=list(scratch),
        cost_estimate=COST,
        compiler_params=pltpu.CompilerParams(vmem_limit_bytes=vmem * 2**20),
        name=name,
    )(*args, *after)
    Chain.last = (token,)
    return result


def order(v, after):
    return pl.pallas_call(
        lambda *refs: None,
        in_specs=[ANY] * (1 + len(after)),
        out_specs=ANY,
        out_shape=jax.ShapeDtypeStruct(v.shape, v.dtype),
        input_output_aliases={0: 0},
        cost_estimate=COST,
        name="order",
    )(v, *after)


COST = pl.CostEstimate(flops=10**6, bytes_accessed=10**5, transcendentals=0)
SMEM = pl.BlockSpec(memory_space=pltpu.SMEM)
ANY = pl.BlockSpec(memory_space=pl.ANY)
HBM = pl.BlockSpec(memory_space=pltpu.HBM)
VMEM = pl.BlockSpec(memory_space=pltpu.VMEM)


def attn_fwd(rep, scalars, qkv, after=()):
    slots, _, rows = qkv.shape
    stat = ((slots // 2, 1, 2 * rows), F32)
    return call(
        functools.partial(attn_fwd_kernel, rep),
        "attn_fwd",
        (*scalars, qkv),
        after,
        smem=4,
        outs=[((slots, HEAD_DIM, rows), BF16), ((slots, HEAD_DIM, rows), F32), stat, stat],
        scratch=[pltpu.VMEM((slots, rows, HEAD_DIM), BF16)],
        vmem=24,
    )


def attn_bwd(rep, place, scalars, qkv, da, full, top, inv, after=()):
    slots, _, rows = qkv.shape
    return call(
        functools.partial(attn_bwd_kernel, rep, place),
        "attn_bwd",
        (*scalars, qkv, da, full, top, inv),
        after,
        smem=4,
        outs=[((slots, 3 * HEAD_DIM, rows), BF16)],
        scratch=[
            pltpu.VMEM((slots, rows, HEAD_DIM), BF16),
            pltpu.VMEM((slots, rows, HEAD_DIM), BF16),
            pltpu.VMEM((slots // 2, HEAD_DIM, 2 * rows), F32),
            pltpu.VMEM((slots // 2, HEAD_DIM, 2 * rows), F32),
        ],
        vmem=24,
    )[0]


def positions(seq_lengths, span_order, rows, part):
    ends = jnp.cumsum(seq_lengths[0]).astype(jnp.int32)
    count = span_order.shape[1]
    blocks = jnp.arange(count, dtype=jnp.int32)
    slot_of = jnp.sum(jnp.where(span_order[0][None, :] == blocks[:, None], blocks[None, :], 0), axis=1)
    starts = jnp.arange(count // 2, dtype=jnp.int32) * (2 * rows)
    low = jnp.max(jnp.where(starts[:, None] >= ends[None, :], ends[None, :], 0), axis=1) // (2 * rows)
    return slot_of.astype(jnp.int32), low.astype(jnp.int32), ends, part.reshape(1).astype(jnp.int32)


def norm_back(grad_normed, unit_rows, inv_rows, gain_vec):
    scaled = grad_normed * gain_vec
    return inv_rows * (scaled - unit_rows * jnp.mean(scaled * unit_rows, axis=-1, keepdims=True))


class Moves:
    def __init__(self, n_dp, n_ctx):
        self.n_dp, self.n_ctx = n_dp, n_ctx

    def rows_gather(self, v):
        return lax.all_gather(v, "dp", axis=0, tiled=True)

    def rows_sum(self, v):
        return lax.psum_scatter(v, "dp", scatter_dimension=0, tiled=True)

    def columns_gather(self, v):
        return lax.all_gather(v, "dp", axis=1, tiled=True)

    def to_ctx(self, v):
        return lax.all_to_all(v, "ctx", 0, 0, tiled=True)

    def sum_product(self, left, right):
        part = dot(left, right, ((1,), (0,))).astype(BF16)
        return lax.psum_scatter(part, "ctx", scatter_dimension=0, tiled=True).astype(F32)


def per_device_any(
    moves,
    latent_in,
    gain_attn,
    w_query,
    w_key,
    w_value,
    w_out,
    gain_ffn,
    w_gate,
    w_up,
    w_down,
    cotangent,
    seq_lengths,
    span_order,
):
    Chain.last = ()
    n_dp, n_ctx = moves.n_dp, moves.n_ctx
    rows, width = latent_in.shape
    ff = w_gate.shape[1]
    dp, ctx = lax.axis_index("dp"), lax.axis_index("ctx")
    rep = n_ctx // HEADS

    scalars = positions(seq_lengths, span_order, rows, ctx % rep)

    share = ff // n_dp
    gate_w = lax.dynamic_slice_in_dim(w_gate, dp * share, share, 1)
    up_w = lax.dynamic_slice_in_dim(w_up, dp * share, share, 1)
    down_w = lax.dynamic_slice_in_dim(w_down, dp * share, share, 0)

    latent_f = latent_in.astype(F32)
    inv_one = lax.rsqrt(jnp.mean(latent_f * latent_f, axis=-1, keepdims=True) + EPS)
    unit_one = latent_f * inv_one
    normed_one = (unit_one * gain_attn).astype(BF16)

    def project(w):
        return dot(w, normed_one, ((0,), (1,))).astype(BF16).reshape(HEADS, HEAD_DIM, rows)

    qkv = jnp.concatenate([project(w_query), project(w_key), project(w_value)], axis=1)
    qkv = moves.to_ctx(jnp.repeat(qkv, rep, axis=0) if rep > 1 else qkv)
    normed_all = lax.all_gather(normed_one, "ctx", axis=0, tiled=True)

    out, full, top, inv = attn_fwd(rep, scalars, qkv)

    def from_heads(v):
        v = moves.to_ctx(v)
        if rep > 1:
            v = jnp.sum(v.astype(F32).reshape((HEADS, rep) + v.shape[1:]), axis=1).astype(BF16)
        return v

    attn_t = from_heads(out).reshape(width, rows)
    resid = latent_f + dot(attn_t, w_out, ((0,), (0,)))
    inv_two = lax.rsqrt(jnp.mean(resid * resid, axis=-1, keepdims=True) + EPS)
    unit_two = resid * inv_two
    normed_two = (unit_two * gain_ffn).astype(BF16)

    top_all = moves.rows_gather(cotangent)
    grad_hidden = dot(top_all, down_w, ((1,), (1,)))
    normed_two_all = moves.rows_gather(normed_two)
    gate_pre = dot(normed_two_all, gate_w, ((1,), (0,)))
    up_pre = dot(normed_two_all, up_w, ((1,), (0,)))
    gate_sig = jax.nn.sigmoid(gate_pre)
    swish = gate_pre * gate_sig
    hidden = (swish * up_pre).astype(BF16)
    latents = (resid + moves.rows_sum(dot(hidden, down_w, ((1,), (0,))))).astype(BF16)
    grad_gate = (grad_hidden * up_pre * gate_sig * (1.0 + gate_pre * (1.0 - gate_sig))).astype(BF16)
    grad_up = (grad_hidden * swish).astype(BF16)
    grad_norm_two = moves.rows_sum(
        dot(grad_gate, gate_w, ((1,), (1,))) + dot(grad_up, up_w, ((1,), (1,)))
    )
    grad_resid = cotangent.astype(F32) + norm_back(grad_norm_two, unit_two, inv_two, gain_ffn)
    grad_mixed = grad_resid.astype(BF16)

    grad_attn = dot(w_out, grad_mixed, ((1,), (1,))).astype(BF16).reshape(HEADS, HEAD_DIM, rows)
    grad_attn = moves.to_ctx(jnp.repeat(grad_attn, rep, axis=0) if rep > 1 else grad_attn)
    grad_qkv = attn_bwd(rep, lambda slot: slot, scalars, qkv, grad_attn, full, top, inv)

    strip = width // n_dp
    down_sum = moves.sum_product(hidden.T, top_all)
    normed_rows = lax.dynamic_slice_in_dim(normed_two_all, dp * strip, strip, 1).T
    gate_sum = moves.sum_product(normed_rows, moves.columns_gather(grad_gate))
    up_sum = moves.sum_product(normed_rows, moves.columns_gather(grad_up))
    attn_rows = moves.rows_gather(attn_t.T)
    attn_rows = lax.dynamic_slice_in_dim(attn_rows, dp * strip, strip, 1).T
    out_sum = moves.sum_product(attn_rows, moves.rows_gather(grad_mixed))

    lanes = jnp.transpose(grad_qkv, (0, 2, 1)).reshape(n_ctx * rows, 3 * HEAD_DIM)
    head_grad = dot(normed_all, lanes, ((0,), (0,)))
    head_grad = head_grad.reshape(n_dp, strip, 3 * HEAD_DIM)
    head_grad = lax.psum_scatter(head_grad, "dp", scatter_dimension=0, tiled=False)
    own = strip // n_ctx
    head_grad = moves.to_ctx(head_grad.astype(BF16).reshape(n_ctx, own, 3 * HEAD_DIM)).astype(F32)
    head_grad = jnp.sum(head_grad.reshape(HEADS, rep, own, 3, HEAD_DIM), axis=1)
    head_grad = jnp.transpose(head_grad, (2, 1, 0, 3)).reshape(3, own, width)
    query_sum, key_sum, value_sum = head_grad[0], head_grad[1], head_grad[2]

    first_row = (dp * n_ctx + ctx) * own

    def own_rows(w):
        return lax.dynamic_slice_in_dim(w, first_row, own, 0).astype(F32)

    def own_gain(v):
        return lax.dynamic_slice_in_dim(v, first_row, own, 0)

    gain_ffn_sum = jnp.sum(own_rows(w_gate) * gate_sum + own_rows(w_up) * up_sum, axis=1) / own_gain(gain_ffn)
    gain_attn_sum = jnp.sum(
        own_rows(w_query) * query_sum + own_rows(w_key) * key_sum + own_rows(w_value) * value_sum, axis=1
    ) / own_gain(gain_attn)

    back = from_heads(grad_qkv).reshape(HEADS, 3, HEAD_DIM, rows)
    grad_norm_one = sum(
        dot(back[:, n].reshape(width, rows), w, ((0,), (1,)))
        for n, w in enumerate((w_query, w_key, w_value))
    )
    latent_grad = (grad_resid + norm_back(grad_norm_one, unit_one, inv_one, gain_attn)).astype(BF16)
    return (
        latents,
        latent_grad,
        gain_attn_sum,
        query_sum,
        key_sum,
        value_sum,
        out_sum,
        gain_ffn_sum,
        gate_sum,
        up_sum,
        down_sum,
    )


def low_t(v):
    return v.astype(F32).T.astype(BF16)


def sel(at, other):
    return 1 - at if other else at


def norm_qkv_kernel(x_ref, gain_ref, wq_ref, wk_ref, wv_ref, n_ref, qkv_ref, held_ref, sems):
    loads = [pltpu.make_async_copy(w, held_ref.at[t], sems.at[t]) for t, w in enumerate((wq_ref, wk_ref, wv_ref))]
    for load in loads:
        load.start()
    x = x_ref[...].astype(F32)
    inv = lax.rsqrt(jnp.mean(x * x, axis=-1, keepdims=True) + EPS)
    n = (x * inv * gain_ref[...]).astype(BF16)
    n_ref[...] = n
    cols = 256
    for t, load in enumerate(loads):
        load.wait()
        for c in range(0, held_ref.shape[2], cols):
            p = dot(n, held_ref[t, :, c : c + cols], ((1,), (0,))).T.astype(BF16)
            for h in range(cols // HEAD_DIM):
                qkv_ref[c // HEAD_DIM + h, t * HEAD_DIM : (t + 1) * HEAD_DIM, :] = p[h * HEAD_DIM : (h + 1) * HEAD_DIM]


def norm_qkv(x, gain, wq, wk, wv):
    rows, width = x.shape
    return call(
        norm_qkv_kernel,
        "norm_qkv",
        (in_hbm(x), gain.reshape(1, width), wq, wk, wv),
        outs=[
            ((rows, width), BF16),
            ((HEADS, 3 * HEAD_DIM, rows), BF16),
        ],
        scratch=[pltpu.VMEM((3, width, width), BF16), pltpu.SemaphoreType.DMA((3,))],
        far=3,
    )


def out_norm_kernel(at_ref, ab_ref, x_ref, gain_ref, w_ref, resid_ref, n_ref, send_ref, held_ref, sem):
    load = pltpu.make_async_copy(w_ref, held_ref, sem)
    load.start()
    left = low_t(ab_ref[...])
    half = send_ref.shape[0]
    send_ref[...] = ab_ref[pl.ds(pl.multiple_of((1 - at_ref[0]) * half, half), half), :]
    load.wait()
    cols = 256
    mixed = [dot(left, held_ref[:, c : c + cols], ((1,), (0,))) for c in range(0, held_ref.shape[1], cols)]
    resid = x_ref[...].astype(F32) + jnp.concatenate(mixed, axis=1)
    resid_ref[...] = resid
    inv = lax.rsqrt(jnp.mean(resid * resid, axis=-1, keepdims=True) + EPS)
    n_ref[...] = (resid * inv * gain_ref[...]).astype(BF16)


def out_norm(at, ab, x, gain, w, after):
    rows, width = x.shape
    return call(
        out_norm_kernel,
        "out_norm",
        (at, ab, x, gain.reshape(1, width), w),
        after,
        smem=1,
        outs=[((rows, width), F32), ((rows, width), BF16), ((width // 2, rows), BF16)],
        scratch=[pltpu.VMEM(w.shape, BF16), pltpu.SemaphoreType.DMA],
        far=1,
    )


def ffn_kernel(
    at_ref, n0_ref, n1_ref, dy0_ref, dy1_ref, wg_ref, wu_ref, wd_ref,
    hid_ref, d0_ref, d1_ref, px_ref, py_ref, tx_ref, ty_ref, kx_ref, ky_ref,
    n_ref, dy_ref, dg_ref, du_ref, hid_t_ref, n_t_ref, g_w, u_w, d_w, sems,
):
    rows, width = n0_ref.shape
    share = g_w.shape[1]
    high = kx_ref.shape[0]
    first = pl.multiple_of(at_ref[0] * share, 128)
    parts = ((0, 256), (256, 768), (768, share))
    loads = []
    for n, (lo, hi) in enumerate(parts):
        cols = pl.ds(pl.multiple_of(first + lo, 128), hi - lo)
        loads.append(
            (
                pltpu.make_async_copy(wg_ref.at[:, cols], g_w.at[:, pl.ds(lo, hi - lo)], sems.at[n, 0]),
                pltpu.make_async_copy(wu_ref.at[:, cols], u_w.at[:, pl.ds(lo, hi - lo)], sems.at[n, 1]),
                pltpu.make_async_copy(wd_ref.at[cols, :], d_w.at[pl.ds(lo, hi - lo), :], sems.at[n, 2]),
            )
        )
        for load in loads[n]:
            load.start()
    n_ref[:rows] = n0_ref[...]
    n_ref[rows:] = n1_ref[...]
    dy_ref[:rows] = dy0_ref[...]
    dy_ref[rows:] = dy1_ref[...]
    n_t_ref[...] = low_t(n_ref[...])

    for lo, hi in parts:
        for load in loads[parts.index((lo, hi))]:
            load.wait()
        for at in range(lo, hi, 256):
            lanes = slice(at, min(at + 256, share))
            g = dot(n_ref[...], g_w[:, lanes], ((1,), (0,)))
            u = dot(n_ref[...], u_w[:, lanes], ((1,), (0,)))
            dh = dot(dy_ref[...], d_w[lanes, :], ((1,), (1,)))
            sig = jax.nn.sigmoid(g)
            swish = g * sig
            hid = (swish * u).astype(BF16)
            dg = (dh * u * sig * (1.0 + g * (1.0 - sig))).astype(BF16)
            du = (dh * swish).astype(BF16)
            hid_ref[:, lanes] = hid
            hid_t_ref[lanes, :] = hid.astype(F32).T
            dg_ref[:, lanes] = dg
            du_ref[:, lanes] = du
            for k in range(dg.shape[1] // rows):
                to = high + (at // rows + k) * 2 * rows
                x_ref, y_ref = px_ref, py_ref
                if to >= px_ref.shape[0]:
                    to, x_ref, y_ref = to - px_ref.shape[0], tx_ref, ty_ref
                x_ref[to : to + 2 * rows, :] = dg[:, k * rows : (k + 1) * rows]
                y_ref[to : to + 2 * rows, :] = du[:, k * rows : (k + 1) * rows]

    for at in range(0, width, 256):
        cols = slice(at, at + 256)
        d = dot(dg_ref[...], g_w[cols, :], ((1,), (1,))) + dot(du_ref[...], u_w[cols, :], ((1,), (1,)))
        d0_ref[:, cols] = d[:rows]
        d1_ref[:, cols] = d[rows:].astype(BF16)

    own = width // 32
    chunk = share // 16
    base = high - width
    padded = base // 16
    x, y = at_ref[1], at_ref[2]
    fill = jnp.zeros((padded - chunk, rows), F32)

    def put(ref, inner, z, xs, ys):
        c = z * 4 + ys * 2 + xs
        for half in range(2):
            lanes = slice(half * rows, (half + 1) * rows)
            v = hid_t_ref[pl.ds(pl.multiple_of(c * chunk, 8), chunk), lanes]
            to = ((inner * 4 + z) * 2 + half) * padded
            ref[to : to + padded, :] = jnp.concatenate([v, fill], axis=0).astype(BF16)
            for d in range(2):
                to = base + half * (width // 2) + ((inner * 4 + z) * 2 + d) * own
                at = pl.multiple_of(d * (width // 2) + c * own, own)
                ref[to : to + own, :] = n_t_ref[pl.ds(at, own), lanes]

    for inner in range(2):
        for z in range(4):
            put(kx_ref, inner, z, x, sel(y, inner))
            put(px_ref, inner, z, 1 - x, sel(y, inner))
            put(ky_ref, inner, z, sel(x, inner), y)
            put(py_ref, inner, z, sel(x, inner), 1 - y)


def ffn(at, n0, n1, dy0, dy1, wg, wu, wd, after):
    rows, width = n0.shape
    share = wg.shape[1] // 2
    padded = -(-(share // 16) // 16) * 16
    high = 16 * padded + width
    early = EARLY * 2 * rows
    sizes = [high + early] * 2 + [2 * share - early] * 2 + [high] * 2
    return call(
        ffn_kernel,
        "ffn",
        (at, n0, n1, dy0, dy1, wg, wu, wd),
        after,
        smem=1,
        outs=[((2 * rows, share), BF16), ((rows, width), F32), ((rows, width), BF16)]
        + [((n, rows), BF16) for n in sizes[:4]]
        + [((n, rows), BF16, HBM) for n in sizes[4:]],
        scratch=[
            pltpu.VMEM((2 * rows, width), BF16),
            pltpu.VMEM((2 * rows, width), BF16),
            pltpu.VMEM((2 * rows, share), BF16),
            pltpu.VMEM((2 * rows, share), BF16),
            pltpu.VMEM((share, 2 * rows), F32),
            pltpu.VMEM((width, 2 * rows), BF16),
            pltpu.VMEM((width, share), BF16),
            pltpu.VMEM((width, share), BF16),
            pltpu.VMEM((share, width), BF16),
            pltpu.SemaphoreType.DMA((3, 3)),
        ],
        vmem=40,
        far=3,
    )


def ffn_out_kernel(at_ref, hid_ref, w_ref, y0_ref, y1_ref, held_ref, sem):
    rows, width = y0_ref.shape
    share = held_ref.shape[0]
    first = pl.multiple_of(at_ref[0] * share, 128)
    load = pltpu.make_async_copy(w_ref.at[pl.ds(first, share), :], held_ref, sem)
    load.start()
    load.wait()
    for at in range(0, width, 256):
        cols = slice(at, at + 256)
        y = dot(hid_ref[...], held_ref[:, cols], ((1,), (0,)))
        y0_ref[:, cols] = y[:rows]
        y1_ref[:, cols] = y[rows:].astype(BF16)


def ffn_out(at, hid, w, after):
    shape = (hid.shape[0] // 2, w.shape[1])
    return call(
        ffn_out_kernel,
        "ffn_out",
        (at, hid, w),
        after,
        smem=1,
        outs=[(shape, F32), (shape, BF16)],
        scratch=[pltpu.VMEM((hid.shape[1], w.shape[1]), BF16), pltpu.SemaphoreType.DMA],
        far=1,
    )


def ffn_back_kernel(d_ref, got_ref, resid_ref, gain_ref, dy_ref, w_ref, dres_ref, low_ref, da_ref, held_ref, sem):
    load = pltpu.make_async_copy(w_ref, held_ref, sem)
    load.start()
    d = d_ref[...] + got_ref[...].astype(F32)
    resid = resid_ref[...]
    inv = lax.rsqrt(jnp.mean(resid * resid, axis=-1, keepdims=True) + EPS)
    dres = dy_ref[...].astype(F32) + norm_back(d, resid * inv, inv, gain_ref[...])
    dres_ref[...] = dres
    low = dres.astype(BF16)
    low_ref[...] = low
    load.wait()
    for at in range(0, held_ref.shape[0], 256):
        da_ref[at : at + 256, :] = dot(held_ref[at : at + 256, :], low, ((1,), (1,))).astype(BF16)


def ffn_back(d, got, resid, gain, dy, w, after):
    rows, width = d.shape
    return call(
        ffn_back_kernel,
        "ffn_back",
        (d, got, resid, gain.reshape(1, width), dy, w),
        after,
        outs=[((rows, width), F32), ((rows, width), BF16), ((width, rows), BF16)],
        scratch=[pltpu.VMEM(w.shape, BF16), pltpu.SemaphoreType.DMA],
        far=1,
    )


EARLY = 4


def out_product_kernel(at_ref, ab_ref, got_ref, low0_ref, low1_ref, kx_ref, px_ref, ky_ref, py_ref, acc_ref):
    half, rows = got_ref.shape
    own = half // 16
    x, y = at_ref[1], at_ref[2]
    mine = ab_ref[pl.ds(pl.multiple_of(at_ref[0] * half, half), half), :]
    left = jnp.concatenate([mine, got_ref[...]], axis=1)
    right = jnp.concatenate([low0_ref[...], low1_ref[...]], axis=0)
    for at in range(0, acc_ref.shape[1], 256):
        acc_ref[:, at : at + 256] = dot(left, right[:, at : at + 256], ((1,), (0,)))
    tiles = acc_ref.shape[1] // 2 // rows

    def put(ref, inner, z, xs, ys, side):
        at = pl.multiple_of((z * 4 + ys * 2 + xs) * own, own)
        for j in range(tiles):
            lanes = slice((side * tiles + j) * rows, (side * tiles + j + 1) * rows)
            to = ((inner * 4 + z) * tiles + j) * own
            ref[to : to + own, :] = acc_ref[pl.ds(at, own), lanes].astype(BF16)

    for inner in range(2):
        for z in range(4):
            put(kx_ref, inner, z, x, sel(y, inner), 0)
            put(px_ref, inner, z, 1 - x, sel(y, inner), 0)
            put(ky_ref, inner, z, sel(x, inner), y, 1)
            put(py_ref, inner, z, sel(x, inner), 1 - y, 1)


def out_product(at, ab, got, low, low_mate, after):
    half, rows = got.shape
    high = half // 2 * (low.shape[1] // 2) // rows
    return call(
        out_product_kernel,
        "out_product",
        (at, ab, got, low, low_mate),
        after,
        smem=1,
        outs=[((high, rows), BF16)] * 4,
        scratch=[pltpu.VMEM((half, low.shape[1]), F32)],
    )


def store(refs, v, lanes, high, to):
    for inner in range(2):
        for z in range(4):
            at = (inner * 4 + z) * high
            refs[inner][z, to : to + high, :] = v[at : at + high, lanes]


def pair_tiles(out, left, f0, f1, start, count, base, own):
    rows = f0.shape[1]
    for t in range(0, count, 2):
        n = min(2, count - t)
        at = [start + (t + k) * 2 * rows for k in range(n)]
        right = [jnp.concatenate([f[a : a + 2 * rows, :] for f in (f0, f1)], axis=0) for a in at]
        v = dot(left, jnp.concatenate(right, axis=1), ((1,), (0,))).astype(BF16)
        for k in range(n):
            store(out, v, slice(k * rows, (k + 1) * rows), 2 * own, base + (t + k) * 2 * own)


def left_rows(k0, p1, width):
    high, half = k0.shape[0], width // 2
    at = high - width
    return jnp.concatenate([r[at + k * half : at + (k + 1) * half, :] for r in (k0, p1) for k in range(2)], axis=1)


def first_product_kernel(side, k0, p0, p1, dy0, dy1, dy2, same_ref, other_ref):
    out = (same_ref, other_ref)
    high, rows = k0.shape
    width = dy0.shape[1]
    half, own = width // 2, width // 32
    padded = (high - width) // 16

    def lanes(ref, k):
        at = k * 2 * padded
        return jnp.concatenate([ref[at : at + padded, :], ref[at + padded : at + 2 * padded, :]], axis=1)

    hid = jnp.concatenate([jnp.concatenate([lanes(k0, k), lanes(p1, k)], axis=1) for k in range(8)], axis=0)
    cols = slice(side * half, (side + 1) * half)
    dy = jnp.concatenate([dy0[:, cols], dy1[:, cols], dy2[...]], axis=0)
    v = dot(hid, dy, ((1,), (0,))).astype(BF16)
    for j in range(half // rows):
        store(out, v, slice(j * rows, (j + 1) * rows), padded, j * padded)
    count = (p0.shape[0] - high) // (2 * rows)
    pair_tiles(out, left_rows(k0, p1, width), p0, p1, high, count, half // rows * padded, own)


def first_product(side, kept, sent, got, dy, after):
    (high, rows), width = kept.shape, dy[0].shape[1]
    tall = width // 2 // rows * (high - width) // 16 + (sent.shape[0] - high) // (2 * rows) * (width // 16)
    kernel = functools.partial(first_product_kernel, side)
    outs = [((4, tall, rows), BF16)] * 2
    return call(kernel, "first_product", (kept, sent, got, *dy), after, outs=outs)


def second_product_kernel(width, k0, p1, f0, f1, q0, q1, same_ref, other_ref):
    out = (same_ref, other_ref)
    count, own = f0.shape[0] // (2 * f0.shape[1]), width // 32
    pair_tiles(out, left_rows(k0, p1, width), f0, f1, 0, count, 0, own)
    base, tall = count * 2 * own, q0.shape[0] // 8
    for k in range(8):
        v = q0[k * tall : (k + 1) * tall, :].astype(F32) + q1[k * tall : (k + 1) * tall, :].astype(F32)
        out[k // 4][k % 4, base : base + tall, :] = v.astype(BF16)


def second_product(width, kept, got, tiles, q, after):
    rows = kept.shape[1]
    tall = tiles[0].shape[0] // (2 * rows) * (width // 16) + q[0].shape[0] // 8
    kernel = functools.partial(second_product_kernel, width)
    outs = [((4, tall, rows), BF16)] * 2
    return call(kernel, "second_product", (kept, got, *tiles, *q), after, outs=outs)


def combine_kernel(at_ref, *refs):
    parts, (own_ref, far_ref, send_ref) = refs[:-3], refs[-3:]
    high = own_ref.shape[0]
    for k, out_ref, start in ((0, own_ref, 0), (3, far_ref, 0), (1, send_ref, 0), (2, send_ref, high)):
        z = jnp.bitwise_xor(at_ref[3], k)
        to = start
        for n in range(0, len(parts), 2):
            rows = parts[n].shape[1]
            out_ref[to : to + rows, :] = (parts[n][z].astype(F32) + parts[n + 1][z].astype(F32)).astype(BF16)
            to += rows


def combine(at, parts, after):
    high, rows = sum(v.shape[1] for v in parts[::2]), parts[0].shape[2]
    outs = [((high, rows), BF16), ((high, rows), BF16), ((2 * high, rows), BF16)]
    return call(combine_kernel, "combine", (at, *parts), after, smem=1, outs=outs)


def cross_kernel(own_ref, far_ref, got_ref, sum_ref, send_ref):
    high = own_ref.shape[0]
    sum_ref[...] = (own_ref[...].astype(F32) + got_ref[:high, :].astype(F32)).astype(BF16)
    send_ref[...] = (far_ref[...].astype(F32) + got_ref[high:, :].astype(F32)).astype(BF16)


def cross(own, far, got, after):
    return call(cross_kernel, "cross", (own, far, got), after, outs=[(own.shape, BF16)] * 2)


def add_lines(refs, sum_ref):
    total = refs[0][...].astype(F32)
    for ref in refs[1:]:
        total += ref[...].astype(F32)
    sum_ref[...] = total


def shares(ref, at, own, dp, mine_ref, theirs_ref, part, t):
    rows = ref.shape[1]
    lanes = slice(t * rows, (t + 1) * rows)
    mine_ref[part, :, lanes] = ref[pl.ds(pl.multiple_of(at + dp * own, own), own), :]
    theirs_ref[part, :, lanes] = ref[pl.ds(pl.multiple_of(at + (1 - dp) * own, own), own), :].astype(BF16)


def unpack_one_kernel(at_ref, i0, i1, down_ref, mine_ref, theirs_ref, sum_ref):
    add_lines((i0, i1), sum_ref)
    rows = i0.shape[1]
    own = mine_ref.shape[1]
    chunk, width = down_ref.shape
    padded = -(-chunk // 16) * 16
    count = width // 2 // rows
    for part in range(2):
        base = part * (i0.shape[0] // 2)
        for j in range(count):
            lanes = slice((part * count + j) * rows, (part * count + j + 1) * rows)
            down_ref[:, lanes] = sum_ref[base + j * padded : base + j * padded + chunk, :]
        for t in range(EARLY):
            shares(sum_ref, base + count * padded + t * 2 * own, own, at_ref[0], mine_ref, theirs_ref, part, t)


def unpack_one(at, v, own, chunk, width, after):
    wide = EARLY * v[0].shape[1]
    outs = [((chunk, width), F32), ((2, own, wide), F32), ((2, own, wide), BF16)]
    scratch = [pltpu.VMEM(v[0].shape, F32)]
    return call(unpack_one_kernel, "unpack_one", (at, *v), after, smem=1, outs=outs, scratch=scratch)


def unpack_two_kernel(at_ref, i0, i1, mine_ref, theirs_ref, out_ref, sum_ref):
    add_lines((i0, i1), sum_ref)
    rows = i0.shape[1]
    own, width = out_ref.shape
    tiles = mine_ref.shape[2] // rows
    count = width // 2 // rows
    for part in range(2):
        base = part * (i0.shape[0] // 2)
        for t in range(tiles):
            shares(sum_ref, base + t * 2 * own, own, at_ref[0], mine_ref, theirs_ref, part, t)
        base += tiles * 2 * own
        for j in range(count):
            lanes = slice((part * count + j) * rows, (part * count + j + 1) * rows)
            out_ref[:, lanes] = sum_ref[base + j * own : base + (j + 1) * own, :]


def unpack_two(at, v, own, wide, width, after):
    wide -= EARLY * v[0].shape[1]
    outs = [((2, own, wide), F32), ((2, own, wide), BF16), ((own, width), F32)]
    scratch = [pltpu.VMEM(v[0].shape, F32)]
    return call(unpack_two_kernel, "unpack_two", (at, *v), after, smem=1, outs=outs, scratch=scratch)


def finish_kernel(at_ref, m0, m1, o0, o1, gain_ref, wg_ref, wu_ref, gate_ref, up_ref, dots_ref):
    dp = at_ref[1]
    share = gate_ref.shape[1] // 2
    early = m0.shape[2]
    for part, ref in enumerate((gate_ref, up_ref)):

        def put(at, a, b):
            ref[:, at : at + early] = a[part].astype(F32)
            ref[:, at + early : at + share] = b[part].astype(F32)

        @pl.when(dp == 0)
        def _():
            put(0, m0, m1)
            put(share, o0, o1)

        @pl.when(dp == 1)
        def _():
            put(0, o0, o1)
            put(share, m0, m1)

    total = gate_ref[...] * wg_ref[...].astype(F32) + up_ref[...] * wu_ref[...].astype(F32)
    dots_ref[...] = by_gain(jnp.sum(total, axis=1, keepdims=True), gain_ref, at_ref[0])


def finish(where, mine, theirs, gain, wg, wu):
    own, ff = mine[0].shape[1], wg.shape[1]
    count = wg.shape[0] // own

    def whole(*shape):
        return pl.BlockSpec(shape, lambda g, at: (0,) * len(shape))

    weight = pl.BlockSpec((own, ff), lambda g, at: (at[0], 0))
    gate, up, dots = pl.pallas_call(
        finish_kernel,
        grid_spec=pltpu.PrefetchScalarGridSpec(
            num_scalar_prefetch=1,
            grid=(1,),
            in_specs=[whole(*v.shape) for v in (*mine, *theirs)] + [whole(count, own), weight, weight],
            out_specs=[whole(own, ff), whole(own, ff), whole(1, own)],
        ),
        out_shape=[jax.ShapeDtypeStruct((own, ff), F32)] * 2 + [jax.ShapeDtypeStruct((1, own), F32)],
        cost_estimate=COST,
        name="finish",
    )(where, *mine, *theirs, gain.reshape(count, own), in_hbm(wg), in_hbm(wu))
    return gate, up, dots.reshape(own)


def turn_kernel(in_ref, out_ref):
    for h in range(4):
        for z in range(4):
            out_ref[z, h] = in_ref[h, z]


def turn(v, after):
    return call(turn_kernel, "turn", (v,), after, outs=[(v.shape, BF16)])[0]


def head_product_kernel(at_ref, n0, n1, in_ref, mine_ref, theirs_ref, acc_ref):
    half = mine_ref.shape[0]
    x, y = at_ref[1], at_ref[2]
    left = jnp.concatenate(
        [
            jnp.concatenate([in_ref[h, sel(y, oy) * 2 + sel(x, ox)] for oy in range(2) for ox in range(2)], axis=1)
            for h in range(4)
        ],
        axis=0,
    )
    right = jnp.concatenate([n0[...], n1[...]], axis=0)
    for at in range(0, acc_ref.shape[0], 256):
        acc_ref[at : at + 256, :] = dot(left, right[:, at : at + 256], ((1,), (0,))).T
    dp = at_ref[0]
    mine_ref[...] = acc_ref[pl.ds(pl.multiple_of(dp * half, half), half), :]
    theirs_ref[...] = acc_ref[pl.ds(pl.multiple_of((1 - dp) * half, half), half), :].astype(BF16)


def head_product(at, n, v, after):
    width, wide = n[0].shape[1], 4 * v.shape[2]
    return call(
        head_product_kernel,
        "head_product",
        (at, *n, v),
        after,
        smem=1,
        outs=[((width // 2, wide), F32), ((width // 2, wide), BF16)],
        scratch=[pltpu.VMEM((width, wide), F32)],
    )


def head_split_kernel(at_ref, mine_ref, got_ref, own_ref, far_ref, send_ref):
    high = own_ref.shape[0]
    for k, ref, to in ((0, own_ref, 0), (3, far_ref, 0), (1, send_ref, 0), (2, send_ref, high)):
        rows = pl.ds(pl.multiple_of(jnp.bitwise_xor(at_ref[3], k) * high, high), high)
        ref[to : to + high, :] = (mine_ref[rows, :] + got_ref[rows, :].astype(F32)).astype(BF16)


def head_split(at, mine, got, after):
    half, wide = mine.shape
    outs = [((half // 4, wide), BF16), ((half // 4, wide), BF16), ((half // 2, wide), BF16)]
    return call(head_split_kernel, "head_split", (at, mine, got), after, smem=1, outs=outs)


def head_end_kernel(a, ga, out_ref):
    own = a.shape[0] // 4
    v = (a[...].astype(F32) + ga[...].astype(F32)).astype(BF16)
    for p in range(4):
        out_ref[p] = v[p * own : (p + 1) * own]


def head_end(a, ga, after):
    outs = [((4, a.shape[0] // 4, a.shape[1]), BF16)]
    return call(head_end_kernel, "head_end", (a, ga), after, outs=outs)[0]


def latent_back_kernel(
    back_ref, dres_ref, x_ref, gain_ref, wq_ref, wk_ref, wv_ref, out_ref, left_ref, d_ref, held_ref, sems
):
    loads = [pltpu.make_async_copy(w, held_ref.at[t], sems.at[t]) for t, w in enumerate((wq_ref, wk_ref, wv_ref))]
    for load in loads:
        load.start()
    for h in range(HEADS):
        for t in range(3):
            left_ref[t, h * HEAD_DIM : (h + 1) * HEAD_DIM, :] = back_ref[h % 4 * 4 + h // 4, t * HEAD_DIM : (t + 1) * HEAD_DIM, :]
    for load in loads:
        load.wait()
    for at in range(0, d_ref.shape[1], 256):
        v = dot(held_ref[0, at : at + 256, :], left_ref[0], ((1,), (0,)))
        v += dot(held_ref[1, at : at + 256, :], left_ref[1], ((1,), (0,)))
        v += dot(held_ref[2, at : at + 256, :], left_ref[2], ((1,), (0,)))
        d_ref[:, at : at + 256] = v.T
    x = x_ref[...].astype(F32)
    inv = lax.rsqrt(jnp.mean(x * x, axis=-1, keepdims=True) + EPS)
    out_ref[...] = (dres_ref[...] + norm_back(d_ref[...], x * inv, inv, gain_ref[...])).astype(BF16)


def latent_back(back, dres, x, gain, wq, wk, wv, after):
    rows, width = x.shape
    return call(
        latent_back_kernel,
        "latent_back",
        (back, dres, x, gain.reshape(1, width), wq, wk, wv),
        after,
        outs=[((rows, width), BF16)],
        scratch=[
            pltpu.VMEM((3, width, rows), BF16),
            pltpu.VMEM((rows, width), F32),
            pltpu.VMEM((3, width, width), BF16),
            pltpu.SemaphoreType.DMA((3,)),
        ],
        far=3,
    )[0]


def by_gain(sums, gain_ref, place):
    return jnp.broadcast_to(sums, (sums.shape[0], 128)).T[:1] / gain_ref[pl.ds(place, 1), :]


def head_rows_kernel(at_ref, in_ref, gain_ref, wq_ref, wk_ref, wv_ref, q_ref, k_ref, v_ref, dots_ref):
    total = None
    for t, (w_ref, o_ref) in enumerate(((wq_ref, q_ref), (wk_ref, k_ref), (wv_ref, v_ref))):
        for h in range(0, HEADS, 2):
            at = (h // 4 * 3 + t) * HEAD_DIM
            pair = [in_ref[h % 4 + n][:, at : at + HEAD_DIM] for n in range(2)]
            o_ref[:, h * HEAD_DIM : (h + 2) * HEAD_DIM] = jnp.concatenate(pair, axis=1).astype(F32)
        v = jnp.sum(o_ref[...] * w_ref[...].astype(F32), axis=1, keepdims=True)
        total = v if total is None else total + v
    dots_ref[...] = by_gain(total, gain_ref, at_ref[0])


def head_rows(where, v, gain, wq, wk, wv):
    own, width = v.shape[1], wq.shape[1]
    weight = pl.BlockSpec((own, width), lambda g, at: (at[0], 0))

    def whole(*shape):
        return pl.BlockSpec(shape, lambda g, at: (0,) * len(shape))

    out = pl.pallas_call(
        head_rows_kernel,
        grid_spec=pltpu.PrefetchScalarGridSpec(
            num_scalar_prefetch=1,
            grid=(1,),
            in_specs=[whole(*v.shape), whole(width // own, own), weight, weight, weight],
            out_specs=[whole(own, width)] * 3 + [whole(1, own)],
        ),
        out_shape=[jax.ShapeDtypeStruct((own, width), F32)] * 3 + [jax.ShapeDtypeStruct((1, own), F32)],
        cost_estimate=COST,
        name="head_rows",
    )(where, v, gain.reshape(width // own, own), in_hbm(wq), in_hbm(wk), in_hbm(wv))
    return *out[:3], out[3].reshape(own)


X_PAIRS = [(i, i ^ 1) for i in range(16)]
Y_PAIRS = [(i, i ^ 2) for i in range(16)]


def swap(v):
    return lax.ppermute(v, "dp", [(0, 1), (1, 0)])


def over_x(v):
    return lax.ppermute(v, "ctx", X_PAIRS)


def over_y(v):
    return lax.ppermute(v, "ctx", Y_PAIRS)


def over_z(v, k):
    return lax.ppermute(v, "ctx", [(i, i ^ (4 * k)) for i in range(16)])


Z_LINES = [[i + 4 * z for z in range(4)] for i in range(4)]
PLANES = [[i + 4 * z for i in range(4)] for z in range(4)]


def in_group(v, groups):
    return lax.all_to_all(v, "ctx", 0, 0, tiled=True, axis_index_groups=groups)


def to_ctx(v):
    return lax.all_to_all(v, "ctx", 0, 0, tiled=True)


def per_device_grid(
    latent_in,
    gain_attn,
    w_query,
    w_key,
    w_value,
    w_out,
    gain_ffn,
    w_gate,
    w_up,
    w_down,
    cotangent,
    seq_lengths,
    span_order,
):
    Chain.last = ()
    rows, width = latent_in.shape
    ff = w_gate.shape[1]
    half, own = width // 2, width // 32
    dp, ctx = lax.axis_index("dp"), lax.axis_index("ctx")
    at = jnp.stack([dp, ctx % 2, (ctx // 2) % 2, ctx // 4]).astype(jnp.int32)
    scalars = positions(seq_lengths, span_order, rows, ctx * 0)

    dy_mate = swap(cotangent)
    dy_x = over_x(jnp.concatenate([cotangent[:, :half], dy_mate[:, :half]], axis=0))
    dy_y = over_y(jnp.concatenate([cotangent[:, half:], dy_mate[:, half:]], axis=0))
    dy_a, dy_b = (cotangent, dy_mate, dy_x), (cotangent, dy_mate, dy_y)
    place = dp * 16 + ctx
    where = jnp.stack([place, dp]).astype(jnp.int32)

    normed, qkv = norm_qkv(latent_in, gain_attn, w_query, w_key, w_value)
    qkv = to_ctx(qkv)
    line = jnp.concatenate([normed, over_x(normed)], axis=0)
    line = (line, over_y(line))
    out, full, top, inv = attn_fwd(1, scalars, qkv, ())
    attn_t = to_ctx(out).reshape(width, rows)
    resid, normed_two, attn_send = out_norm(at, attn_t, latent_in, gain_ffn, w_out, (line[1], dy_x, dy_y))
    normed_mate = swap(normed_two)
    attn_mate = swap(attn_send)
    hid, d_own, d_mate, send_x, send_y, tiles_x, tiles_y, kept_x, kept_y = ffn(
        at, normed_two, normed_mate, cotangent, dy_mate, w_gate, w_up, w_down, ()
    )
    d_got = swap(d_mate)
    got_x, got_y = over_x(send_x), over_y(send_y)
    tiles_x, tiles_y = (tiles_x, over_x(tiles_x)), (tiles_y, over_y(tiles_y))
    dres, dres_low, grad_attn = ffn_back(d_own, d_got, resid, gain_ffn, cotangent, w_out, ())
    grad_attn = to_ctx(grad_attn.reshape(HEADS, HEAD_DIM, rows))
    out_x, out_sx, out_y, out_sy = out_product(at, attn_t, attn_mate, dres_low, swap(dres_low), ())
    out_x, out_y = (out_x, over_x(out_sx)), (out_y, over_y(out_sy))
    one_a, other_a = first_product(0, kept_x, send_x, got_x, dy_a, ())
    sent_a = over_y(other_a)
    one_b, other_b = first_product(1, kept_y, send_y, got_y, dy_b, ())
    sent_b = over_x(other_b)
    grad_qkv = attn_bwd(1, lambda slot: slot, scalars, qkv, grad_attn, full, top, inv, (tiles_x[1], tiles_y[1], out_x[1], out_y[1]))
    four = in_group(grad_qkv, Z_LINES).reshape(4, 4, 3 * HEAD_DIM, rows)
    two_a, other_a = second_product(width, kept_x, got_x, tiles_x, out_x, ())
    sent_two_a = over_y(other_a)
    two_b, other_b = second_product(width, kept_y, got_y, tiles_y, out_y, ())
    sent_two_b = over_x(other_b)
    one_own, one_far, one_send = combine(at, (one_a, sent_a, one_b, sent_b), ())
    one_got = over_z(one_send, 1)
    y_own, y_mate = ffn_out(at, hid, w_down, ())
    latents = (resid + y_own + swap(y_mate).astype(F32)).astype(BF16)
    two_own, two_far, two_send = combine(at, (two_a, sent_two_a, two_b, sent_two_b), ())
    two_got = over_z(two_send, 1)
    back = in_group(turn(four, ()), PLANES).reshape(16, 3 * HEAD_DIM, rows)
    one_own, one_send = cross(one_own, one_far, one_got, ())
    one_got = over_z(one_send, 3)
    head_mine, head_theirs = head_product(at, line, four, ())
    head_theirs = swap(head_theirs)
    head_own, head_far, head_send = head_split(at, head_mine, head_theirs, ())
    head_got = over_z(head_send, 1)
    down_sum, mine0, theirs0 = unpack_one(at, (one_own, one_got), own, ff // 32, width, ())
    theirs0 = swap(theirs0)
    two_own, two_send = cross(two_own, two_far, two_got, ())
    two_got = over_z(two_send, 3)
    latent_grad = latent_back(back, dres, latent_in, gain_attn, w_query, w_key, w_value, ())
    head_own, head_send = cross(head_own, head_far, head_got, ())
    head_got = over_z(head_send, 3)
    mine1, theirs1, out_sum = unpack_two(at, (two_own, two_got), own, ff // 2, width, ())
    theirs1 = swap(theirs1)
    heads = in_group(head_end(head_own, head_got, ()), PLANES)
    query_sum, key_sum, value_sum, gain_attn_sum = head_rows(where, heads, gain_attn, w_query, w_key, w_value)
    gate_sum, up_sum, gain_ffn_sum = finish(where, (mine0, mine1), (theirs0, theirs1), gain_ffn, w_gate, w_up)
    return (
        latents,
        latent_grad,
        gain_attn_sum,
        query_sum,
        key_sum,
        value_sum,
        out_sum,
        gain_ffn_sum,
        gate_sum,
        up_sum,
        down_sum,
    )


def solution(mesh):
    n_dp, n_ctx = mesh.shape["dp"], mesh.shape["ctx"]
    if n_dp == 2 and n_ctx == 16:
        body = per_device_grid
    else:
        body = functools.partial(per_device_any, Moves(n_dp, n_ctx))
    rows, whole, share = P(("dp", "ctx"), None), P(), P("dp", None)
    flat = P(("dp", "ctx"))
    return jax.shard_map(
        body,
        mesh=mesh,
        in_specs=(rows,) + (whole,) * 9 + (rows, share, share),
        out_specs=(rows, rows, flat, rows, rows, rows, rows, flat, rows, rows, rows),
        check_vma=False,
    )
```

```python
import functools

import jax
import jax.numpy as jnp
from jax import lax
from jax.experimental import pallas as pl
from jax.experimental.pallas import tpu as pltpu
from jax.sharding import PartitionSpec as P

HEADS = 16
HEAD_DIM = 64
EPS = 1e-06
NEG_FILL = -1e30
LOG2E = 1.4426950408889634
SCALE = HEAD_DIM**-0.5

BF16 = jnp.bfloat16
F32 = jnp.float32


def dot(a, b, dims):
    return lax.dot_general(a, b, (dims, ((), ())), preferred_element_type=F32)


def query_starts(ends_ref, pos):
    start = jnp.zeros_like(pos)
    for n in range(ends_ref.shape[0]):
        start = jnp.where(pos >= ends_ref[n], ends_ref[n], start)
    return start


def block_mask(ends_ref, i, j, blk):
    pos = lax.broadcasted_iota(jnp.int32, (1, blk), 1) + i * blk
    start = query_starts(ends_ref, pos) - j * blk
    key = lax.broadcasted_iota(jnp.int32, (2 * blk, blk), 0)
    return (key <= pos - j * blk) & (key >= start)


def four_slots(slot_ref, j, count):
    n = jnp.minimum(j + 1, count - 1)
    return slot_ref[2 * j], slot_ref[2 * j + 1], slot_ref[2 * n], slot_ref[2 * n + 1]


def attn_fwd_kernel(rep, slot_ref, low_ref, ends_ref, part_ref, qkv_ref, out_ref, full_ref, top_ref, inv_ref, key_ref):
    slots, _, rows = qkv_ref.shape
    blk = 2 * rows
    count = slots // 2
    hd = HEAD_DIM

    def flip(s, c):
        key_ref[s] = qkv_ref[s, hd : 2 * hd, :].T
        return c

    lax.fori_loop(0, slots, flip, 0)
    if rep > 1:
        out_ref[...] = jnp.zeros_like(out_ref)
        full_ref[...] = jnp.zeros_like(full_ref)

    def query_block(i, c):
        s0, s1 = slot_ref[2 * i], slot_ref[2 * i + 1]
        q = jnp.concatenate([qkv_ref[s0, :hd, :], qkv_ref[s1, :hd, :]], axis=1)

        low = low_ref[i]

        def key_block(n, state):
            top, mass, acc = state
            j = low + 2 * n
            keys = four_slots(slot_ref, j, count)
            k = jnp.concatenate([key_ref[t] for t in keys], axis=0)
            v = jnp.concatenate([qkv_ref[t, 2 * hd :, :] for t in keys], axis=1)
            s = dot(k, q, ((1,), (0,))) * (SCALE * LOG2E)
            s = jnp.where(block_mask(ends_ref, i, j, blk), s, NEG_FILL)
            new_top = jnp.maximum(top, jnp.max(s, axis=0, keepdims=True))
            shrink = jnp.exp2(top - new_top)
            w = jnp.exp2(s - new_top)
            mass = mass * shrink + jnp.sum(w, axis=0, keepdims=True)
            acc = acc * shrink + dot(v, w.astype(BF16), ((1,), (0,)))
            return new_top, mass, acc

        init = (
            jnp.full((1, blk), NEG_FILL, F32),
            jnp.zeros((1, blk), F32),
            jnp.zeros((hd, blk), F32),
        )
        top, mass, acc = lax.fori_loop(0, (i + 2 - low) // 2, key_block, init)
        inv = 1.0 / mass
        acc = acc * inv
        full_ref[s0] = acc[:, :rows]
        full_ref[s1] = acc[:, rows:]
        rounded = acc.astype(BF16)
        out_ref[s0] = rounded[:, :rows]
        out_ref[s1] = rounded[:, rows:]
        top_ref[i] = top
        inv_ref[i] = inv
        return c

    lax.fori_loop(0, count // rep, lambda n, c: query_block(n * rep + part_ref[0], c), 0)


def attn_bwd_kernel(
    rep, place, slot_ref, low_ref, ends_ref, part_ref, qkv_ref, da_ref, full_ref, top_ref, inv_ref,
    out_ref, key_ref, value_ref, dk_ref, dv_ref,
):
    slots, _, rows = qkv_ref.shape
    blk = 2 * rows
    count = slots // 2
    hd = HEAD_DIM

    def flip(s, c):
        key_ref[s] = qkv_ref[s, hd : 2 * hd, :].T
        value_ref[s] = qkv_ref[s, 2 * hd :, :].T
        return c

    lax.fori_loop(0, slots, flip, 0)
    dk_ref[...] = jnp.zeros_like(dk_ref)
    dv_ref[...] = jnp.zeros_like(dv_ref)
    if rep > 1:
        out_ref[...] = jnp.zeros_like(out_ref)

    def pair(ref, a, b, lo, hi):
        return jnp.concatenate([ref[a, lo:hi, :], ref[b, lo:hi, :]], axis=1)

    def query_block(i, c):
        s0, s1 = slot_ref[2 * i], slot_ref[2 * i + 1]
        q = pair(qkv_ref, s0, s1, 0, hd)
        da = pair(da_ref, s0, s1, 0, hd)
        full = pair(full_ref, s0, s1, 0, hd)
        delta = jnp.sum(da.astype(F32) * full, axis=0, keepdims=True)
        top, inv = top_ref[i], inv_ref[i]

        low = low_ref[i]

        def key_block(n, dq):
            j = low + 2 * n
            after = jnp.minimum(j + 1, count - 1)
            keys = four_slots(slot_ref, j, count)
            k = jnp.concatenate([key_ref[t] for t in keys], axis=0)
            v = jnp.concatenate([value_ref[t] for t in keys], axis=0)
            s = dot(k, q, ((1,), (0,))) * (SCALE * LOG2E)
            s = jnp.where(block_mask(ends_ref, i, j, blk), s, NEG_FILL)
            p = jnp.exp2(s - top) * inv
            dp = dot(v, da, ((1,), (0,)))
            ds = (p * (dp - delta)).astype(BF16)
            dk = dot(q, ds, ((1,), (1,)))
            dv = dot(da, p.astype(BF16), ((1,), (1,)))
            dk_ref[j] += dk[:, :blk]
            dk_ref[after] += dk[:, blk:]
            dv_ref[j] += dv[:, :blk]
            dv_ref[after] += dv[:, blk:]
            k_t = jnp.concatenate([qkv_ref[t, hd : 2 * hd, :] for t in keys], axis=1)
            return dq + dot(k_t, ds, ((1,), (0,)))

        dq = lax.fori_loop(0, (i + 2 - low) // 2, key_block, jnp.zeros((hd, blk), F32))
        dq = (dq * SCALE).astype(BF16)
        out_ref[place(s0), :hd, :] = dq[:, :rows]
        out_ref[place(s1), :hd, :] = dq[:, rows:]
        return c

    lax.fori_loop(0, count // rep, lambda n, c: query_block(n * rep + part_ref[0], c), 0)

    def finish(j, c):
        k0, k1 = place(slot_ref[2 * j]), place(slot_ref[2 * j + 1])
        dk = (dk_ref[j] * SCALE).astype(BF16)
        dv = dv_ref[j].astype(BF16)
        out_ref[k0, hd : 2 * hd, :] = dk[:, :rows]
        out_ref[k1, hd : 2 * hd, :] = dk[:, rows:]
        out_ref[k0, 2 * hd :, :] = dv[:, :rows]
        out_ref[k1, 2 * hd :, :] = dv[:, rows:]
        return c

    lax.fori_loop(0, count, finish, 0)


def in_hbm(v):
    return pltpu.with_memory_space_constraint(v, pltpu.HBM)


class Chain:
    last = ()


def call(kernel, name, args, after=(), smem=0, outs=(), scratch=(), vmem=24, far=0):
    held = len(args)
    after = (*after, *Chain.last)
    skip = held + len(after)
    if far:
        args = (*args[: held - far], *(in_hbm(v) for v in args[held - far :]))

    def body(*refs):
        refs[skip][...] = jnp.zeros((8, 128), F32)
        kernel(*refs[:held], *refs[skip + 1 :])

    token, *result = pl.pallas_call(
        body,
        in_specs=[SMEM] * smem + [VMEM] * (held - smem - far) + [HBM] * far + [ANY] * len(after),
        out_specs=[VMEM] * (1 + len(outs)),
        out_shape=[jax.ShapeDtypeStruct((8, 128), F32)]
        + [pltpu.HBM(*o[:2]) if len(o) > 2 else jax.ShapeDtypeStruct(*o) for o in outs],
        scratch_shapes=list(scratch),
        cost_estimate=COST,
        compiler_params=pltpu.CompilerParams(vmem_limit_bytes=vmem * 2**20),
        name=name,
    )(*args, *after)
    Chain.last = (token,)
    return result


def order(v, after):
    return pl.pallas_call(
        lambda *refs: None,
        in_specs=[ANY] * (1 + len(after)),
        out_specs=ANY,
        out_shape=jax.ShapeDtypeStruct(v.shape, v.dtype),
        input_output_aliases={0: 0},
        cost_estimate=COST,
        name="order",
    )(v, *after)


COST = pl.CostEstimate(flops=10**6, bytes_accessed=10**5, transcendentals=0)
SMEM = pl.BlockSpec(memory_space=pltpu.SMEM)
ANY = pl.BlockSpec(memory_space=pl.ANY)
HBM = pl.BlockSpec(memory_space=pltpu.HBM)
VMEM = pl.BlockSpec(memory_space=pltpu.VMEM)


def attn_fwd(rep, scalars, qkv, after=()):
    slots, _, rows = qkv.shape
    stat = ((slots // 2, 1, 2 * rows), F32)
    return call(
        functools.partial(attn_fwd_kernel, rep),
        "attn_fwd",
        (*scalars, qkv),
        after,
        smem=4,
        outs=[((slots, HEAD_DIM, rows), BF16), ((slots, HEAD_DIM, rows), F32), stat, stat],
        scratch=[pltpu.VMEM((slots, rows, HEAD_DIM), BF16)],
        vmem=24,
    )


def attn_bwd(rep, place, scalars, qkv, da, full, top, inv, after=()):
    slots, _, rows = qkv.shape
    return call(
        functools.partial(attn_bwd_kernel, rep, place),
        "attn_bwd",
        (*scalars, qkv, da, full, top, inv),
        after,
        smem=4,
        outs=[((slots, 3 * HEAD_DIM, rows), BF16)],
        scratch=[
            pltpu.VMEM((slots, rows, HEAD_DIM), BF16),
            pltpu.VMEM((slots, rows, HEAD_DIM), BF16),
            pltpu.VMEM((slots // 2, HEAD_DIM, 2 * rows), F32),
            pltpu.VMEM((slots // 2, HEAD_DIM, 2 * rows), F32),
        ],
        vmem=24,
    )[0]


def positions(seq_lengths, span_order, rows, part):
    ends = jnp.cumsum(seq_lengths[0]).astype(jnp.int32)
    count = span_order.shape[1]
    blocks = jnp.arange(count, dtype=jnp.int32)
    slot_of = jnp.sum(jnp.where(span_order[0][None, :] == blocks[:, None], blocks[None, :], 0), axis=1)
    starts = jnp.arange(count // 2, dtype=jnp.int32) * (2 * rows)
    low = jnp.max(jnp.where(starts[:, None] >= ends[None, :], ends[None, :], 0), axis=1) // (2 * rows)
    return slot_of.astype(jnp.int32), low.astype(jnp.int32), ends, part.reshape(1).astype(jnp.int32)


def norm_back(grad_normed, unit_rows, inv_rows, gain_vec):
    scaled = grad_normed * gain_vec
    return inv_rows * (scaled - unit_rows * jnp.mean(scaled * unit_rows, axis=-1, keepdims=True))


class Moves:
    def __init__(self, n_dp, n_ctx):
        self.n_dp, self.n_ctx = n_dp, n_ctx

    def rows_gather(self, v):
        return lax.all_gather(v, "dp", axis=0, tiled=True)

    def rows_sum(self, v):
        return lax.psum_scatter(v, "dp", scatter_dimension=0, tiled=True)

    def columns_gather(self, v):
        return lax.all_gather(v, "dp", axis=1, tiled=True)

    def to_ctx(self, v):
        return lax.all_to_all(v, "ctx", 0, 0, tiled=True)

    def sum_product(self, left, right):
        part = dot(left, right, ((1,), (0,))).astype(BF16)
        return lax.psum_scatter(part, "ctx", scatter_dimension=0, tiled=True).astype(F32)


def per_device_any(
    moves,
    latent_in,
    gain_attn,
    w_query,
    w_key,
    w_value,
    w_out,
    gain_ffn,
    w_gate,
    w_up,
    w_down,
    cotangent,
    seq_lengths,
    span_order,
):
    Chain.last = ()
    n_dp, n_ctx = moves.n_dp, moves.n_ctx
    rows, width = latent_in.shape
    ff = w_gate.shape[1]
    dp, ctx = lax.axis_index("dp"), lax.axis_index("ctx")
    rep = n_ctx // HEADS

    scalars = positions(seq_lengths, span_order, rows, ctx % rep)

    share = ff // n_dp
    gate_w = lax.dynamic_slice_in_dim(w_gate, dp * share, share, 1)
    up_w = lax.dynamic_slice_in_dim(w_up, dp * share, share, 1)
    down_w = lax.dynamic_slice_in_dim(w_down, dp * share, share, 0)

    latent_f = latent_in.astype(F32)
    inv_one = lax.rsqrt(jnp.mean(latent_f * latent_f, axis=-1, keepdims=True) + EPS)
    unit_one = latent_f * inv_one
    normed_one = (unit_one * gain_attn).astype(BF16)

    def project(w):
        return dot(w, normed_one, ((0,), (1,))).astype(BF16).reshape(HEADS, HEAD_DIM, rows)

    qkv = jnp.concatenate([project(w_query), project(w_key), project(w_value)], axis=1)
    qkv = moves.to_ctx(jnp.repeat(qkv, rep, axis=0) if rep > 1 else qkv)
    normed_all = lax.all_gather(normed_one, "ctx", axis=0, tiled=True)

    out, full, top, inv = attn_fwd(rep, scalars, qkv)

    def from_heads(v):
        v = moves.to_ctx(v)
        if rep > 1:
            v = jnp.sum(v.astype(F32).reshape((HEADS, rep) + v.shape[1:]), axis=1).astype(BF16)
        return v

    attn_t = from_heads(out).reshape(width, rows)
    resid = latent_f + dot(attn_t, w_out, ((0,), (0,)))
    inv_two = lax.rsqrt(jnp.mean(resid * resid, axis=-1, keepdims=True) + EPS)
    unit_two = resid * inv_two
    normed_two = (unit_two * gain_ffn).astype(BF16)

    top_all = moves.rows_gather(cotangent)
    grad_hidden = dot(top_all, down_w, ((1,), (1,)))
    normed_two_all = moves.rows_gather(normed_two)
    gate_pre = dot(normed_two_all, gate_w, ((1,), (0,)))
    up_pre = dot(normed_two_all, up_w, ((1,), (0,)))
    gate_sig = jax.nn.sigmoid(gate_pre)
    swish = gate_pre * gate_sig
    hidden = (swish * up_pre).astype(BF16)
    latents = (resid + moves.rows_sum(dot(hidden, down_w, ((1,), (0,))))).astype(BF16)
    grad_gate = (grad_hidden * up_pre * gate_sig * (1.0 + gate_pre * (1.0 - gate_sig))).astype(BF16)
    grad_up = (grad_hidden * swish).astype(BF16)
    grad_norm_two = moves.rows_sum(
        dot(grad_gate, gate_w, ((1,), (1,))) + dot(grad_up, up_w, ((1,), (1,)))
    )
    grad_resid = cotangent.astype(F32) + norm_back(grad_norm_two, unit_two, inv_two, gain_ffn)
    grad_mixed = grad_resid.astype(BF16)

    grad_attn = dot(w_out, grad_mixed, ((1,), (1,))).astype(BF16).reshape(HEADS, HEAD_DIM, rows)
    grad_attn = moves.to_ctx(jnp.repeat(grad_attn, rep, axis=0) if rep > 1 else grad_attn)
    grad_qkv = attn_bwd(rep, lambda slot: slot, scalars, qkv, grad_attn, full, top, inv)

    strip = width // n_dp
    down_sum = moves.sum_product(hidden.T, top_all)
    normed_rows = lax.dynamic_slice_in_dim(normed_two_all, dp * strip, strip, 1).T
    gate_sum = moves.sum_product(normed_rows, moves.columns_gather(grad_gate))
    up_sum = moves.sum_product(normed_rows, moves.columns_gather(grad_up))
    attn_rows = moves.rows_gather(attn_t.T)
    attn_rows = lax.dynamic_slice_in_dim(attn_rows, dp * strip, strip, 1).T
    out_sum = moves.sum_product(attn_rows, moves.rows_gather(grad_mixed))

    lanes = jnp.transpose(grad_qkv, (0, 2, 1)).reshape(n_ctx * rows, 3 * HEAD_DIM)
    head_grad = dot(normed_all, lanes, ((0,), (0,)))
    head_grad = head_grad.reshape(n_dp, strip, 3 * HEAD_DIM)
    head_grad = lax.psum_scatter(head_grad, "dp", scatter_dimension=0, tiled=False)
    own = strip // n_ctx
    head_grad = moves.to_ctx(head_grad.astype(BF16).reshape(n_ctx, own, 3 * HEAD_DIM)).astype(F32)
    head_grad = jnp.sum(head_grad.reshape(HEADS, rep, own, 3, HEAD_DIM), axis=1)
    head_grad = jnp.transpose(head_grad, (2, 1, 0, 3)).reshape(3, own, width)
    query_sum, key_sum, value_sum = head_grad[0], head_grad[1], head_grad[2]

    first_row = (dp * n_ctx + ctx) * own

    def own_rows(w):
        return lax.dynamic_slice_in_dim(w, first_row, own, 0).astype(F32)

    def own_gain(v):
        return lax.dynamic_slice_in_dim(v, first_row, own, 0)

    gain_ffn_sum = jnp.sum(own_rows(w_gate) * gate_sum + own_rows(w_up) * up_sum, axis=1) / own_gain(gain_ffn)
    gain_attn_sum = jnp.sum(
        own_rows(w_query) * query_sum + own_rows(w_key) * key_sum + own_rows(w_value) * value_sum, axis=1
    ) / own_gain(gain_attn)

    back = from_heads(grad_qkv).reshape(HEADS, 3, HEAD_DIM, rows)
    grad_norm_one = sum(
        dot(back[:, n].reshape(width, rows), w, ((0,), (1,)))
        for n, w in enumerate((w_query, w_key, w_value))
    )
    latent_grad = (grad_resid + norm_back(grad_norm_one, unit_one, inv_one, gain_attn)).astype(BF16)
    return (
        latents,
        latent_grad,
        gain_attn_sum,
        query_sum,
        key_sum,
        value_sum,
        out_sum,
        gain_ffn_sum,
        gate_sum,
        up_sum,
        down_sum,
    )


def low_t(v):
    return v.astype(F32).T.astype(BF16)


def sel(at, other):
    return 1 - at if other else at


def norm_qkv_kernel(x_ref, gain_ref, wq_ref, wk_ref, wv_ref, n_ref, qkv_ref, held_ref, sems):
    loads = [pltpu.make_async_copy(w, held_ref.at[t], sems.at[t]) for t, w in enumerate((wq_ref, wk_ref, wv_ref))]
    for load in loads:
        load.start()
    x = x_ref[...].astype(F32)
    inv = lax.rsqrt(jnp.mean(x * x, axis=-1, keepdims=True) + EPS)
    n = (x * inv * gain_ref[...]).astype(BF16)
    n_ref[...] = n
    cols = 256
    for t, load in enumerate(loads):
        load.wait()
        for c in range(0, held_ref.shape[2], cols):
            p = dot(n, held_ref[t, :, c : c + cols], ((1,), (0,))).T.astype(BF16)
            for h in range(cols // HEAD_DIM):
                qkv_ref[c // HEAD_DIM + h, t * HEAD_DIM : (t + 1) * HEAD_DIM, :] = p[h * HEAD_DIM : (h + 1) * HEAD_DIM]


def norm_qkv(x, gain, wq, wk, wv):
    rows, width = x.shape
    return call(
        norm_qkv_kernel,
        "norm_qkv",
        (in_hbm(x), gain.reshape(1, width), wq, wk, wv),
        outs=[
            ((rows, width), BF16),
            ((HEADS, 3 * HEAD_DIM, rows), BF16),
        ],
        scratch=[pltpu.VMEM((3, width, width), BF16), pltpu.SemaphoreType.DMA((3,))],
        far=3,
    )


def out_norm_kernel(at_ref, ab_ref, x_ref, gain_ref, w_ref, resid_ref, n_ref, send_ref, held_ref, sem):
    load = pltpu.make_async_copy(w_ref, held_ref, sem)
    load.start()
    left = low_t(ab_ref[...])
    half = send_ref.shape[0]
    send_ref[...] = ab_ref[pl.ds(pl.multiple_of((1 - at_ref[0]) * half, half), half), :]
    load.wait()
    cols = 256
    mixed = [dot(left, held_ref[:, c : c + cols], ((1,), (0,))) for c in range(0, held_ref.shape[1], cols)]
    resid = x_ref[...].astype(F32) + jnp.concatenate(mixed, axis=1)
    resid_ref[...] = resid
    inv = lax.rsqrt(jnp.mean(resid * resid, axis=-1, keepdims=True) + EPS)
    n_ref[...] = (resid * inv * gain_ref[...]).astype(BF16)


def out_norm(at, ab, x, gain, w, after):
    rows, width = x.shape
    return call(
        out_norm_kernel,
        "out_norm",
        (at, ab, x, gain.reshape(1, width), w),
        after,
        smem=1,
        outs=[((rows, width), F32), ((rows, width), BF16), ((width // 2, rows), BF16)],
        scratch=[pltpu.VMEM(w.shape, BF16), pltpu.SemaphoreType.DMA],
        far=1,
    )


def ffn_kernel(
    at_ref, n0_ref, n1_ref, dy0_ref, dy1_ref, wg_ref, wu_ref, wd_ref,
    hid_ref, d0_ref, d1_ref, px_ref, py_ref, tx_ref, ty_ref, kx_ref, ky_ref,
    n_ref, dy_ref, dg_ref, du_ref, hid_t_ref, n_t_ref, g_w, u_w, d_w, sems,
):
    rows, width = n0_ref.shape
    share = g_w.shape[1]
    high = kx_ref.shape[0]
    first = pl.multiple_of(at_ref[0] * share, 128)
    parts = ((0, 256), (256, 768), (768, share))
    loads = []
    for n, (lo, hi) in enumerate(parts):
        cols = pl.ds(pl.multiple_of(first + lo, 128), hi - lo)
        loads.append(
            (
                pltpu.make_async_copy(wg_ref.at[:, cols], g_w.at[:, pl.ds(lo, hi - lo)], sems.at[n, 0]),
                pltpu.make_async_copy(wu_ref.at[:, cols], u_w.at[:, pl.ds(lo, hi - lo)], sems.at[n, 1]),
                pltpu.make_async_copy(wd_ref.at[cols, :], d_w.at[pl.ds(lo, hi - lo), :], sems.at[n, 2]),
            )
        )
        for load in loads[n]:
            load.start()
    n_ref[:rows] = n0_ref[...]
    n_ref[rows:] = n1_ref[...]
    dy_ref[:rows] = dy0_ref[...]
    dy_ref[rows:] = dy1_ref[...]
    n_t_ref[...] = low_t(n_ref[...])

    for lo, hi in parts:
        for load in loads[parts.index((lo, hi))]:
            load.wait()
        for at in range(lo, hi, 256):
            lanes = slice(at, min(at + 256, share))
            g = dot(n_ref[...], g_w[:, lanes], ((1,), (0,)))
            u = dot(n_ref[...], u_w[:, lanes], ((1,), (0,)))
            dh = dot(dy_ref[...], d_w[lanes, :], ((1,), (1,)))
            sig = jax.nn.sigmoid(g)
            swish = g * sig
            hid = (swish * u).astype(BF16)
            dg = (dh * u * sig * (1.0 + g * (1.0 - sig))).astype(BF16)
            du = (dh * swish).astype(BF16)
            hid_ref[:, lanes] = hid
            hid_t_ref[lanes, :] = hid.astype(F32).T
            dg_ref[:, lanes] = dg
            du_ref[:, lanes] = du
            for k in range(dg.shape[1] // rows):
                to = high + (at // rows + k) * 2 * rows
                x_ref, y_ref = px_ref, py_ref
                if to >= px_ref.shape[0]:
                    to, x_ref, y_ref = to - px_ref.shape[0], tx_ref, ty_ref
                x_ref[to : to + 2 * rows, :] = dg[:, k * rows : (k + 1) * rows]
                y_ref[to : to + 2 * rows, :] = du[:, k * rows : (k + 1) * rows]

    for at in range(0, width, 256):
        cols = slice(at, at + 256)
        d = dot(dg_ref[...], g_w[cols, :], ((1,), (1,))) + dot(du_ref[...], u_w[cols, :], ((1,), (1,)))
        d0_ref[:, cols] = d[:rows]
        d1_ref[:, cols] = d[rows:].astype(BF16)

    own = width // 32
    chunk = share // 16
    base = high - width
    padded = base // 16
    x, y = at_ref[1], at_ref[2]
    fill = jnp.zeros((padded - chunk, rows), F32)

    def put(ref, inner, z, xs, ys):
        c = z * 4 + ys * 2 + xs
        for half in range(2):
            lanes = slice(half * rows, (half + 1) * rows)
            v = hid_t_ref[pl.ds(pl.multiple_of(c * chunk, 8), chunk), lanes]
            to = ((inner * 4 + z) * 2 + half) * padded
            ref[to : to + padded, :] = jnp.concatenate([v, fill], axis=0).astype(BF16)
            for d in range(2):
                to = base + half * (width // 2) + ((inner * 4 + z) * 2 + d) * own
                at = pl.multiple_of(d * (width // 2) + c * own, own)
                ref[to : to + own, :] = n_t_ref[pl.ds(at, own), lanes]

    for inner in range(2):
        for z in range(4):
            put(kx_ref, inner, z, x, sel(y, inner))
            put(px_ref, inner, z, 1 - x, sel(y, inner))
            put(ky_ref, inner, z, sel(x, inner), y)
            put(py_ref, inner, z, sel(x, inner), 1 - y)


def ffn(at, n0, n1, dy0, dy1, wg, wu, wd, after):
    rows, width = n0.shape
    share = wg.shape[1] // 2
    padded = -(-(share // 16) // 16) * 16
    high = 16 * padded + width
    early = EARLY * 2 * rows
    sizes = [high + early] * 2 + [2 * share - early] * 2 + [high] * 2
    return call(
        ffn_kernel,
        "ffn",
        (at, n0, n1, dy0, dy1, wg, wu, wd),
        after,
        smem=1,
        outs=[((2 * rows, share), BF16), ((rows, width), F32), ((rows, width), BF16)]
        + [((n, rows), BF16) for n in sizes[:4]]
        + [((n, rows), BF16, HBM) for n in sizes[4:]],
        scratch=[
            pltpu.VMEM((2 * rows, width), BF16),
            pltpu.VMEM((2 * rows, width), BF16),
            pltpu.VMEM((2 * rows, share), BF16),
            pltpu.VMEM((2 * rows, share), BF16),
            pltpu.VMEM((share, 2 * rows), F32),
            pltpu.VMEM((width, 2 * rows), BF16),
            pltpu.VMEM((width, share), BF16),
            pltpu.VMEM((width, share), BF16),
            pltpu.VMEM((share, width), BF16),
            pltpu.SemaphoreType.DMA((3, 3)),
        ],
        vmem=40,
        far=3,
    )


def ffn_out_kernel(at_ref, hid_ref, w_ref, y0_ref, y1_ref, held_ref, sem):
    rows, width = y0_ref.shape
    share = held_ref.shape[0]
    first = pl.multiple_of(at_ref[0] * share, 128)
    load = pltpu.make_async_copy(w_ref.at[pl.ds(first, share), :], held_ref, sem)
    load.start()
    load.wait()
    for at in range(0, width, 256):
        cols = slice(at, at + 256)
        y = dot(hid_ref[...], held_ref[:, cols], ((1,), (0,)))
        y0_ref[:, cols] = y[:rows]
        y1_ref[:, cols] = y[rows:].astype(BF16)


def ffn_out(at, hid, w, after):
    shape = (hid.shape[0] // 2, w.shape[1])
    return call(
        ffn_out_kernel,
        "ffn_out",
        (at, hid, w),
        after,
        smem=1,
        outs=[(shape, F32), (shape, BF16)],
        scratch=[pltpu.VMEM((hid.shape[1], w.shape[1]), BF16), pltpu.SemaphoreType.DMA],
        far=1,
    )


def ffn_back_kernel(d_ref, got_ref, resid_ref, gain_ref, dy_ref, w_ref, dres_ref, low_ref, da_ref, held_ref, sem):
    load = pltpu.make_async_copy(w_ref, held_ref, sem)
    load.start()
    d = d_ref[...] + got_ref[...].astype(F32)
    resid = resid_ref[...]
    inv = lax.rsqrt(jnp.mean(resid * resid, axis=-1, keepdims=True) + EPS)
    dres = dy_ref[...].astype(F32) + norm_back(d, resid * inv, inv, gain_ref[...])
    dres_ref[...] = dres
    low = dres.astype(BF16)
    low_ref[...] = low
    load.wait()
    for at in range(0, held_ref.shape[0], 256):
        da_ref[at : at + 256, :] = dot(held_ref[at : at + 256, :], low, ((1,), (1,))).astype(BF16)


def ffn_back(d, got, resid, gain, dy, w, after):
    rows, width = d.shape
    return call(
        ffn_back_kernel,
        "ffn_back",
        (d, got, resid, gain.reshape(1, width), dy, w),
        after,
        outs=[((rows, width), F32), ((rows, width), BF16), ((width, rows), BF16)],
        scratch=[pltpu.VMEM(w.shape, BF16), pltpu.SemaphoreType.DMA],
        far=1,
    )


EARLY = 4


def out_product_kernel(at_ref, ab_ref, got_ref, low0_ref, low1_ref, kx_ref, px_ref, ky_ref, py_ref, acc_ref):
    half, rows = got_ref.shape
    own = half // 16
    x, y = at_ref[1], at_ref[2]
    mine = ab_ref[pl.ds(pl.multiple_of(at_ref[0] * half, half), half), :]
    left = jnp.concatenate([mine, got_ref[...]], axis=1)
    right = jnp.concatenate([low0_ref[...], low1_ref[...]], axis=0)
    for at in range(0, acc_ref.shape[1], 256):
        acc_ref[:, at : at + 256] = dot(left, right[:, at : at + 256], ((1,), (0,)))
    tiles = acc_ref.shape[1] // 2 // rows

    def put(ref, inner, z, xs, ys, side):
        at = pl.multiple_of((z * 4 + ys * 2 + xs) * own, own)
        for j in range(tiles):
            lanes = slice((side * tiles + j) * rows, (side * tiles + j + 1) * rows)
            to = ((inner * 4 + z) * tiles + j) * own
            ref[to : to + own, :] = acc_ref[pl.ds(at, own), lanes].astype(BF16)

    for inner in range(2):
        for z in range(4):
            put(kx_ref, inner, z, x, sel(y, inner), 0)
            put(px_ref, inner, z, 1 - x, sel(y, inner), 0)
            put(ky_ref, inner, z, sel(x, inner), y, 1)
            put(py_ref, inner, z, sel(x, inner), 1 - y, 1)


def out_product(at, ab, got, low, low_mate, after):
    half, rows = got.shape
    high = half // 2 * (low.shape[1] // 2) // rows
    return call(
        out_product_kernel,
        "out_product",
        (at, ab, got, low, low_mate),
        after,
        smem=1,
        outs=[((high, rows), BF16)] * 4,
        scratch=[pltpu.VMEM((half, low.shape[1]), F32)],
    )


def store(refs, v, lanes, high, to):
    for inner in range(2):
        for z in range(4):
            at = (inner * 4 + z) * high
            refs[inner][z, to : to + high, :] = v[at : at + high, lanes]


def pair_tiles(out, left, f0, f1, start, count, base, own):
    rows = f0.shape[1]
    for t in range(0, count, 2):
        n = min(2, count - t)
        at = [start + (t + k) * 2 * rows for k in range(n)]
        right = [jnp.concatenate([f[a : a + 2 * rows, :] for f in (f0, f1)], axis=0) for a in at]
        v = dot(left, jnp.concatenate(right, axis=1), ((1,), (0,))).astype(BF16)
        for k in range(n):
            store(out, v, slice(k * rows, (k + 1) * rows), 2 * own, base + (t + k) * 2 * own)


def left_rows(k0, p1, width):
    high, half = k0.shape[0], width // 2
    at = high - width
    return jnp.concatenate([r[at + k * half : at + (k + 1) * half, :] for r in (k0, p1) for k in range(2)], axis=1)


def first_product_kernel(side, k0, p0, p1, dy0, dy1, dy2, same_ref, other_ref):
    out = (same_ref, other_ref)
    high, rows = k0.shape
    width = dy0.shape[1]
    half, own = width // 2, width // 32
    padded = (high - width) // 16

    def lanes(ref, k):
        at = k * 2 * padded
        return jnp.concatenate([ref[at : at + padded, :], ref[at + padded : at + 2 * padded, :]], axis=1)

    hid = jnp.concatenate([jnp.concatenate([lanes(k0, k), lanes(p1, k)], axis=1) for k in range(8)], axis=0)
    cols = slice(side * half, (side + 1) * half)
    dy = jnp.concatenate([dy0[:, cols], dy1[:, cols], dy2[...]], axis=0)
    v = dot(hid, dy, ((1,), (0,))).astype(BF16)
    for j in range(half // rows):
        store(out, v, slice(j * rows, (j + 1) * rows), padded, j * padded)
    count = (p0.shape[0] - high) // (2 * rows)
    pair_tiles(out, left_rows(k0, p1, width), p0, p1, high, count, half // rows * padded, own)


def first_product(side, kept, sent, got, dy, after):
    (high, rows), width = kept.shape, dy[0].shape[1]
    tall = width // 2 // rows * (high - width) // 16 + (sent.shape[0] - high) // (2 * rows) * (width // 16)
    kernel = functools.partial(first_product_kernel, side)
    outs = [((4, tall, rows), BF16)] * 2
    return call(kernel, "first_product", (kept, sent, got, *dy), after, outs=outs)


def second_product_kernel(width, k0, p1, f0, f1, q0, q1, same_ref, other_ref):
    out = (same_ref, other_ref)
    count, own = f0.shape[0] // (2 * f0.shape[1]), width // 32
    pair_tiles(out, left_rows(k0, p1, width), f0, f1, 0, count, 0, own)
    base, tall = count * 2 * own, q0.shape[0] // 8
    for k in range(8):
        v = q0[k * tall : (k + 1) * tall, :].astype(F32) + q1[k * tall : (k + 1) * tall, :].astype(F32)
        out[k // 4][k % 4, base : base + tall, :] = v.astype(BF16)


def second_product(width, kept, got, tiles, q, after):
    rows = kept.shape[1]
    tall = tiles[0].shape[0] // (2 * rows) * (width // 16) + q[0].shape[0] // 8
    kernel = functools.partial(second_product_kernel, width)
    outs = [((4, tall, rows), BF16)] * 2
    return call(kernel, "second_product", (kept, got, *tiles, *q), after, outs=outs)


def combine_kernel(at_ref, *refs):
    parts, (own_ref, far_ref, send_ref) = refs[:-3], refs[-3:]
    high = own_ref.shape[0]
    for k, out_ref, start in ((0, own_ref, 0), (3, far_ref, 0), (1, send_ref, 0), (2, send_ref, high)):
        z = jnp.bitwise_xor(at_ref[3], k)
        to = start
        for n in range(0, len(parts), 2):
            rows = parts[n].shape[1]
            out_ref[to : to + rows, :] = (parts[n][z].astype(F32) + parts[n + 1][z].astype(F32)).astype(BF16)
            to += rows


def combine(at, parts, after):
    high, rows = sum(v.shape[1] for v in parts[::2]), parts[0].shape[2]
    outs = [((high, rows), BF16), ((high, rows), BF16), ((2 * high, rows), BF16)]
    return call(combine_kernel, "combine", (at, *parts), after, smem=1, outs=outs)


def cross_kernel(own_ref, far_ref, got_ref, sum_ref, send_ref):
    high = own_ref.shape[0]
    sum_ref[...] = (own_ref[...].astype(F32) + got_ref[:high, :].astype(F32)).astype(BF16)
    send_ref[...] = (far_ref[...].astype(F32) + got_ref[high:, :].astype(F32)).astype(BF16)


def cross(own, far, got, after):
    return call(cross_kernel, "cross", (own, far, got), after, outs=[(own.shape, BF16)] * 2)


def add_lines(refs, sum_ref):
    total = refs[0][...].astype(F32)
    for ref in refs[1:]:
        total += ref[...].astype(F32)
    sum_ref[...] = total


def shares(ref, at, own, dp, mine_ref, theirs_ref, part, t):
    rows = ref.shape[1]
    lanes = slice(t * rows, (t + 1) * rows)
    mine_ref[part, :, lanes] = ref[pl.ds(pl.multiple_of(at + dp * own, own), own), :]
    theirs_ref[part, :, lanes] = ref[pl.ds(pl.multiple_of(at + (1 - dp) * own, own), own), :].astype(BF16)


def unpack_one_kernel(at_ref, i0, i1, down_ref, mine_ref, theirs_ref, sum_ref):
    add_lines((i0, i1), sum_ref)
    rows = i0.shape[1]
    own = mine_ref.shape[1]
    chunk, width = down_ref.shape
    padded = -(-chunk // 16) * 16
    count = width // 2 // rows
    for part in range(2):
        base = part * (i0.shape[0] // 2)
        for j in range(count):
            lanes = slice((part * count + j) * rows, (part * count + j + 1) * rows)
            down_ref[:, lanes] = sum_ref[base + j * padded : base + j * padded + chunk, :]
        for t in range(EARLY):
            shares(sum_ref, base + count * padded + t * 2 * own, own, at_ref[0], mine_ref, theirs_ref, part, t)


def unpack_one(at, v, own, chunk, width, after):
    wide = EARLY * v[0].shape[1]
    outs = [((chunk, width), F32), ((2, own, wide), F32), ((2, own, wide), BF16)]
    scratch = [pltpu.VMEM(v[0].shape, F32)]
    return call(unpack_one_kernel, "unpack_one", (at, *v), after, smem=1, outs=outs, scratch=scratch)


def unpack_two_kernel(at_ref, i0, i1, mine_ref, theirs_ref, out_ref, sum_ref):
    add_lines((i0, i1), sum_ref)
    rows = i0.shape[1]
    own, width = out_ref.shape
    tiles = mine_ref.shape[2] // rows
    count = width // 2 // rows
    for part in range(2):
        base = part * (i0.shape[0] // 2)
        for t in range(tiles):
            shares(sum_ref, base + t * 2 * own, own, at_ref[0], mine_ref, theirs_ref, part, t)
        base += tiles * 2 * own
        for j in range(count):
            lanes = slice((part * count + j) * rows, (part * count + j + 1) * rows)
            out_ref[:, lanes] = sum_ref[base + j * own : base + (j + 1) * own, :]


def unpack_two(at, v, own, wide, width, after):
    wide -= EARLY * v[0].shape[1]
    outs = [((2, own, wide), F32), ((2, own, wide), BF16), ((own, width), F32)]
    scratch = [pltpu.VMEM(v[0].shape, F32)]
    return call(unpack_two_kernel, "unpack_two", (at, *v), after, smem=1, outs=outs, scratch=scratch)


def finish_kernel(at_ref, m0, m1, o0, o1, gain_ref, wg_ref, wu_ref, gate_ref, up_ref, dots_ref):
    dp = at_ref[1]
    share = gate_ref.shape[1] // 2
    early = m0.shape[2]
    for part, ref in enumerate((gate_ref, up_ref)):

        def put(at, a, b):
            ref[:, at : at + early] = a[part].astype(F32)
            ref[:, at + early : at + share] = b[part].astype(F32)

        @pl.when(dp == 0)
        def _():
            put(0, m0, m1)
            put(share, o0, o1)

        @pl.when(dp == 1)
        def _():
            put(0, o0, o1)
            put(share, m0, m1)

    total = gate_ref[...] * wg_ref[...].astype(F32) + up_ref[...] * wu_ref[...].astype(F32)
    dots_ref[...] = by_gain(jnp.sum(total, axis=1, keepdims=True), gain_ref, at_ref[0])


def finish(where, mine, theirs, gain, wg, wu):
    own, ff = mine[0].shape[1], wg.shape[1]
    count = wg.shape[0] // own

    def whole(*shape):
        return pl.BlockSpec(shape, lambda g, at: (0,) * len(shape))

    weight = pl.BlockSpec((own, ff), lambda g, at: (at[0], 0))
    gate, up, dots = pl.pallas_call(
        finish_kernel,
        grid_spec=pltpu.PrefetchScalarGridSpec(
            num_scalar_prefetch=1,
            grid=(1,),
            in_specs=[whole(*v.shape) for v in (*mine, *theirs)] + [whole(count, own), weight, weight],
            out_specs=[whole(own, ff), whole(own, ff), whole(1, own)],
        ),
        out_shape=[jax.ShapeDtypeStruct((own, ff), F32)] * 2 + [jax.ShapeDtypeStruct((1, own), F32)],
        cost_estimate=COST,
        name="finish",
    )(where, *mine, *theirs, gain.reshape(count, own), in_hbm(wg), in_hbm(wu))
    return gate, up, dots.reshape(own)


def turn_kernel(in_ref, out_ref):
    for h in range(4):
        for z in range(4):
            out_ref[z, h] = in_ref[h, z]


def turn(v, after):
    return call(turn_kernel, "turn", (v,), after, outs=[(v.shape, BF16)])[0]


def head_product_kernel(at_ref, n0, n1, in_ref, mine_ref, theirs_ref, acc_ref):
    half = mine_ref.shape[0]
    x, y = at_ref[1], at_ref[2]
    left = jnp.concatenate(
        [
            jnp.concatenate([in_ref[h, sel(y, oy) * 2 + sel(x, ox)] for oy in range(2) for ox in range(2)], axis=1)
            for h in range(4)
        ],
        axis=0,
    )
    right = jnp.concatenate([n0[...], n1[...]], axis=0)
    for at in range(0, acc_ref.shape[0], 256):
        acc_ref[at : at + 256, :] = dot(left, right[:, at : at + 256], ((1,), (0,))).T
    dp = at_ref[0]
    mine_ref[...] = acc_ref[pl.ds(pl.multiple_of(dp * half, half), half), :]
    theirs_ref[...] = acc_ref[pl.ds(pl.multiple_of((1 - dp) * half, half), half), :].astype(BF16)


def head_product(at, n, v, after):
    width, wide = n[0].shape[1], 4 * v.shape[2]
    return call(
        head_product_kernel,
        "head_product",
        (at, *n, v),
        after,
        smem=1,
        outs=[((width // 2, wide), F32), ((width // 2, wide), BF16)],
        scratch=[pltpu.VMEM((width, wide), F32)],
    )


def head_split_kernel(at_ref, mine_ref, got_ref, own_ref, far_ref, send_ref):
    high = own_ref.shape[0]
    for k, ref, to in ((0, own_ref, 0), (3, far_ref, 0), (1, send_ref, 0), (2, send_ref, high)):
        rows = pl.ds(pl.multiple_of(jnp.bitwise_xor(at_ref[3], k) * high, high), high)
        ref[to : to + high, :] = (mine_ref[rows, :] + got_ref[rows, :].astype(F32)).astype(BF16)


def head_split(at, mine, got, after):
    half, wide = mine.shape
    outs = [((half // 4, wide), BF16), ((half // 4, wide), BF16), ((half // 2, wide), BF16)]
    return call(head_split_kernel, "head_split", (at, mine, got), after, smem=1, outs=outs)


def head_end_kernel(a, ga, out_ref):
    own = a.shape[0] // 4
    v = (a[...].astype(F32) + ga[...].astype(F32)).astype(BF16)
    for p in range(4):
        out_ref[p] = v[p * own : (p + 1) * own]


def head_end(a, ga, after):
    outs = [((4, a.shape[0] // 4, a.shape[1]), BF16)]
    return call(head_end_kernel, "head_end", (a, ga), after, outs=outs)[0]


def latent_back_kernel(
    back_ref, dres_ref, x_ref, gain_ref, wq_ref, wk_ref, wv_ref, out_ref, left_ref, d_ref, held_ref, sems
):
    loads = [pltpu.make_async_copy(w, held_ref.at[t], sems.at[t]) for t, w in enumerate((wq_ref, wk_ref, wv_ref))]
    for load in loads:
        load.start()
    for h in range(HEADS):
        for t in range(3):
            left_ref[t, h * HEAD_DIM : (h + 1) * HEAD_DIM, :] = back_ref[h % 4 * 4 + h // 4, t * HEAD_DIM : (t + 1) * HEAD_DIM, :]
    for load in loads:
        load.wait()
    for at in range(0, d_ref.shape[1], 256):
        v = dot(held_ref[0, at : at + 256, :], left_ref[0], ((1,), (0,)))
        v += dot(held_ref[1, at : at + 256, :], left_ref[1], ((1,), (0,)))
        v += dot(held_ref[2, at : at + 256, :], left_ref[2], ((1,), (0,)))
        d_ref[:, at : at + 256] = v.T
    x = x_ref[...].astype(F32)
    inv = lax.rsqrt(jnp.mean(x * x, axis=-1, keepdims=True) + EPS)
    out_ref[...] = (dres_ref[...] + norm_back(d_ref[...], x * inv, inv, gain_ref[...])).astype(BF16)


def latent_back(back, dres, x, gain, wq, wk, wv, after):
    rows, width = x.shape
    return call(
        latent_back_kernel,
        "latent_back",
        (back, dres, x, gain.reshape(1, width), wq, wk, wv),
        after,
        outs=[((rows, width), BF16)],
        scratch=[
            pltpu.VMEM((3, width, rows), BF16),
            pltpu.VMEM((rows, width), F32),
            pltpu.VMEM((3, width, width), BF16),
            pltpu.SemaphoreType.DMA((3,)),
        ],
        far=3,
    )[0]


def by_gain(sums, gain_ref, place):
    return jnp.broadcast_to(sums, (sums.shape[0], 128)).T[:1] / gain_ref[pl.ds(place, 1), :]


def head_rows_kernel(at_ref, in_ref, gain_ref, wq_ref, wk_ref, wv_ref, q_ref, k_ref, v_ref, dots_ref):
    total = None
    for t, (w_ref, o_ref) in enumerate(((wq_ref, q_ref), (wk_ref, k_ref), (wv_ref, v_ref))):
        for h in range(0, HEADS, 2):
            at = (h // 4 * 3 + t) * HEAD_DIM
            pair = [in_ref[h % 4 + n][:, at : at + HEAD_DIM] for n in range(2)]
            o_ref[:, h * HEAD_DIM : (h + 2) * HEAD_DIM] = jnp.concatenate(pair, axis=1).astype(F32)
        v = jnp.sum(o_ref[...] * w_ref[...].astype(F32), axis=1, keepdims=True)
        total = v if total is None else total + v
    dots_ref[...] = by_gain(total, gain_ref, at_ref[0])


def head_rows(where, v, gain, wq, wk, wv):
    own, width = v.shape[1], wq.shape[1]
    weight = pl.BlockSpec((own, width), lambda g, at: (at[0], 0))

    def whole(*shape):
        return pl.BlockSpec(shape, lambda g, at: (0,) * len(shape))

    out = pl.pallas_call(
        head_rows_kernel,
        grid_spec=pltpu.PrefetchScalarGridSpec(
            num_scalar_prefetch=1,
            grid=(1,),
            in_specs=[whole(*v.shape), whole(width // own, own), weight, weight, weight],
            out_specs=[whole(own, width)] * 3 + [whole(1, own)],
        ),
        out_shape=[jax.ShapeDtypeStruct((own, width), F32)] * 3 + [jax.ShapeDtypeStruct((1, own), F32)],
        cost_estimate=COST,
        name="head_rows",
    )(where, v, gain.reshape(width // own, own), in_hbm(wq), in_hbm(wk), in_hbm(wv))
    return *out[:3], out[3].reshape(own)


X_PAIRS = [(i, i ^ 1) for i in range(16)]
Y_PAIRS = [(i, i ^ 2) for i in range(16)]


def swap(v):
    return lax.ppermute(v, "dp", [(0, 1), (1, 0)])


def over_x(v):
    return lax.ppermute(v, "ctx", X_PAIRS)


def over_y(v):
    return lax.ppermute(v, "ctx", Y_PAIRS)


def over_z(v, k):
    return lax.ppermute(v, "ctx", [(i, i ^ (4 * k)) for i in range(16)])


Z_LINES = [[i + 4 * z for z in range(4)] for i in range(4)]
PLANES = [[i + 4 * z for i in range(4)] for z in range(4)]


def in_group(v, groups):
    return lax.all_to_all(v, "ctx", 0, 0, tiled=True, axis_index_groups=groups)


def to_ctx(v):
    return lax.all_to_all(v, "ctx", 0, 0, tiled=True)


def per_device_grid(
    latent_in,
    gain_attn,
    w_query,
    w_key,
    w_value,
    w_out,
    gain_ffn,
    w_gate,
    w_up,
    w_down,
    cotangent,
    seq_lengths,
    span_order,
):
    Chain.last = ()
    rows, width = latent_in.shape
    ff = w_gate.shape[1]
    half, own = width // 2, width // 32
    dp, ctx = lax.axis_index("dp"), lax.axis_index("ctx")
    at = jnp.stack([dp, ctx % 2, (ctx // 2) % 2, ctx // 4]).astype(jnp.int32)
    scalars = positions(seq_lengths, span_order, rows, ctx * 0)

    dy_mate = swap(cotangent)
    dy_x = over_x(jnp.concatenate([cotangent[:, :half], dy_mate[:, :half]], axis=0))
    dy_y = over_y(jnp.concatenate([cotangent[:, half:], dy_mate[:, half:]], axis=0))
    dy_a, dy_b = (cotangent, dy_mate, dy_x), (cotangent, dy_mate, dy_y)
    place = dp * 16 + ctx
    where = jnp.stack([place, dp]).astype(jnp.int32)

    normed, qkv = norm_qkv(latent_in, gain_attn, w_query, w_key, w_value)
    qkv = to_ctx(qkv)
    line = jnp.concatenate([normed, over_x(normed)], axis=0)
    line = (line, over_y(line))
    out, full, top, inv = attn_fwd(1, scalars, qkv, ())
    attn_t = to_ctx(out).reshape(width, rows)
    resid, normed_two, attn_send = out_norm(at, attn_t, latent_in, gain_ffn, w_out, (line[1], dy_x, dy_y))
    normed_mate = swap(normed_two)
    attn_mate = swap(attn_send)
    hid, d_own, d_mate, send_x, send_y, tiles_x, tiles_y, kept_x, kept_y = ffn(
        at, normed_two, normed_mate, cotangent, dy_mate, w_gate, w_up, w_down, ()
    )
    d_got = swap(d_mate)
    got_x, got_y = over_x(send_x), over_y(send_y)
    tiles_x, tiles_y = (tiles_x, over_x(tiles_x)), (tiles_y, over_y(tiles_y))
    dres, dres_low, grad_attn = ffn_back(d_own, d_got, resid, gain_ffn, cotangent, w_out, ())
    grad_attn = to_ctx(grad_attn.reshape(HEADS, HEAD_DIM, rows))
    out_x, out_sx, out_y, out_sy = out_product(at, attn_t, attn_mate, dres_low, swap(dres_low), ())
    out_x, out_y = (out_x, over_x(out_sx)), (out_y, over_y(out_sy))
    one_a, other_a = first_product(0, kept_x, send_x, got_x, dy_a, ())
    sent_a = over_y(other_a)
    one_b, other_b = first_product(1, kept_y, send_y, got_y, dy_b, ())
    sent_b = over_x(other_b)
    grad_qkv = attn_bwd(1, lambda slot: slot, scalars, qkv, grad_attn, full, top, inv, (tiles_x[1], tiles_y[1], out_x[1], out_y[1]))
    four = in_group(grad_qkv, Z_LINES).reshape(4, 4, 3 * HEAD_DIM, rows)
    two_a, other_a = second_product(width, kept_x, got_x, tiles_x, out_x, ())
    sent_two_a = over_y(other_a)
    two_b, other_b = second_product(width, kept_y, got_y, tiles_y, out_y, ())
    sent_two_b = over_x(other_b)
    one_own, one_far, one_send = combine(at, (one_a, sent_a, one_b, sent_b), ())
    one_got = over_z(one_send, 1)
    y_own, y_mate = ffn_out(at, hid, w_down, ())
    latents = (resid + y_own + swap(y_mate).astype(F32)).astype(BF16)
    two_own, two_far, two_send = combine(at, (two_a, sent_two_a, two_b, sent_two_b), ())
    two_got = over_z(two_send, 1)
    one_own, one_send = cross(one_own, one_far, one_got, ())
    one_got = over_z(one_send, 3)
    back = in_group(turn(four, ()), PLANES).reshape(16, 3 * HEAD_DIM, rows)
    head_mine, head_theirs = head_product(at, line, four, ())
    head_theirs = swap(head_theirs)
    head_own, head_far, head_send = head_split(at, head_mine, head_theirs, ())
    head_got = over_z(head_send, 1)
    down_sum, mine0, theirs0 = unpack_one(at, (one_own, one_got), own, ff // 32, width, ())
    theirs0 = swap(theirs0)
    two_own, two_send = cross(two_own, two_far, two_got, ())
    two_got = over_z(two_send, 3)
    latent_grad = latent_back(back, dres, latent_in, gain_attn, w_query, w_key, w_value, ())
    head_own, head_send = cross(head_own, head_far, head_got, ())
    head_got = over_z(head_send, 3)
    mine1, theirs1, out_sum = unpack_two(at, (two_own, two_got), own, ff // 2, width, ())
    theirs1 = swap(theirs1)
    heads = in_group(head_end(head_own, head_got, ()), PLANES)
    query_sum, key_sum, value_sum, gain_attn_sum = head_rows(where, heads, gain_attn, w_query, w_key, w_value)
    gate_sum, up_sum, gain_ffn_sum = finish(where, (mine0, mine1), (theirs0, theirs1), gain_ffn, w_gate, w_up)
    return (
        latents,
        latent_grad,
        gain_attn_sum,
        query_sum,
        key_sum,
        value_sum,
        out_sum,
        gain_ffn_sum,
        gate_sum,
        up_sum,
        down_sum,
    )


def solution(mesh):
    n_dp, n_ctx = mesh.shape["dp"], mesh.shape["ctx"]
    if n_dp == 2 and n_ctx == 16:
        body = per_device_grid
    else:
        body = functools.partial(per_device_any, Moves(n_dp, n_ctx))
    rows, whole, share = P(("dp", "ctx"), None), P(), P("dp", None)
    flat = P(("dp", "ctx"))
    return jax.shard_map(
        body,
        mesh=mesh,
        in_specs=(rows,) + (whole,) * 9 + (rows, share, share),
        out_specs=(rows, rows, flat, rows, rows, rows, rows, flat, rows, rows, rows),
        check_vma=False,
    )
```
